32 devices in a mesh: shard: 4 (over z), ctx: 2 (over y), tensor: 4 (over x, core).
Axes of the slice: x: 2, y: 2, z: 4, core: 2. Of those that a mesh axis runs over, the one named last changes fastest.
Arguments:
- tokens: bfloat16 [4, 2048, 2048], P('shard', 'ctx'), may hold values from -6 to 6
- cotangent: bfloat16 [4, 2048, 2048], P('shard', 'ctx'), may hold values from -6 to 6
- segment_ids: int32 [4, 2048], P('shard', 'ctx'), may hold values from 0 to 2, never falling along the last dimension, each value on 1 to 1280 neighbouring positions
- query_weight: float32 [2048, 2048], P(('shard', 'ctx'), 'tensor'), may hold values from -0.125 to 0.125
- key_weight: float32 [2048, 2048], P(('shard', 'ctx'), 'tensor'), may hold values from -0.125 to 0.125
- value_weight: float32 [2048, 2048], P(('shard', 'ctx'), 'tensor'), may hold values from -0.125 to 0.125
- output_weight: float32 [2048, 2048], P('tensor', ('shard', 'ctx')), may hold values from -0.125 to 0.125
- gate_weight: float32 [2048, 8192], P(('shard', 'ctx'), 'tensor'), may hold values from -0.125 to 0.125
- upward_weight: float32 [2048, 8192], P(('shard', 'ctx'), 'tensor'), may hold values from -0.125 to 0.125
- downward_weight: float32 [8192, 2048], P('tensor', ('shard', 'ctx')), may hold values from -0.0625 to 0.0625
- querynorm_weight: float32 [16, 128], P('tensor', ('shard', 'ctx')), may hold values from 0.5 to 1.5
- keynorm_weight: float32 [16, 128], P('tensor', ('shard', 'ctx')), may hold values from 0.5 to 1.5
- postattention_weight: float32 [2048], P(('shard', 'ctx')), may hold values from 0.5 to 1.5
- postfeedforward_weight: float32 [2048], P(('shard', 'ctx')), may hold values from 0.5 to 1.5
- query_mean: float32 [2048, 2048], P(('shard', 'ctx'), 'tensor'), may hold values from -112 to 112
- key_mean: float32 [2048, 2048], P(('shard', 'ctx'), 'tensor'), may hold values from -112 to 112
- value_mean: float32 [2048, 2048], P(('shard', 'ctx'), 'tensor'), may hold values from -112 to 112
- output_mean: float32 [2048, 2048], P('tensor', ('shard', 'ctx')), may hold values from -112 to 112
- gate_mean: float32 [2048, 8192], P(('shard', 'ctx'), 'tensor'), may hold values from -56 to 56
- upward_mean: float32 [2048, 8192], P(('shard', 'ctx'), 'tensor'), may hold values from -56 to 56
- downward_mean: float32 [8192, 2048], P('tensor', ('shard', 'ctx')), may hold values from -112 to 112
- querynorm_mean: float32 [16, 128], P('tensor', ('shard', 'ctx')), may hold values from -112 to 112
- keynorm_mean: float32 [16, 128], P('tensor', ('shard', 'ctx')), may hold values from -112 to 112
- postattention_mean: float32 [2048], P(('shard', 'ctx')), may hold values from -112 to 112
- postfeedforward_mean: float32 [2048], P(('shard', 'ctx')), may hold values from -112 to 112
- query_square: float32 [2048, 2048], P(('shard', 'ctx'), 'tensor'), may hold values from 409 to 1638
- key_square: float32 [2048, 2048], P(('shard', 'ctx'), 'tensor'), may hold values from 409 to 1638
- value_square: float32 [2048, 2048], P(('shard', 'ctx'), 'tensor'), may hold values from 409 to 1638
- output_square: float32 [2048, 2048], P('tensor', ('shard', 'ctx')), may hold values from 409 to 1638
- gate_square: float32 [2048, 8192], P(('shard', 'ctx'), 'tensor'), may hold values from 81 to 327
- upward_square: float32 [2048, 8192], P(('shard', 'ctx'), 'tensor'), may hold values from 81 to 327
- downward_square: float32 [8192, 2048], P('tensor', ('shard', 'ctx')), may hold values from 409 to 1638
- querynorm_square: float32 [16, 128], P('tensor', ('shard', 'ctx')), may hold values from 819 to 3276
- keynorm_square: float32 [16, 128], P('tensor', ('shard', 'ctx')), may hold values from 819 to 3276
- postattention_square: float32 [2048], P(('shard', 'ctx')), may hold values from 204 to 819
- postfeedforward_square: float32 [2048], P(('shard', 'ctx')), may hold values from 204 to 819
Outputs:
- block_out: float32 [4, 2048, 2048], P('shard', 'ctx')
- input_grad: float32 [4, 2048, 2048], P('shard', 'ctx')
- query_gradient: float32 [2048, 2048], P(('shard', 'ctx'), 'tensor')
- key_gradient: float32 [2048, 2048], P(('shard', 'ctx'), 'tensor')
- value_gradient: float32 [2048, 2048], P(('shard', 'ctx'), 'tensor')
- output_gradient: float32 [2048, 2048], P('tensor', ('shard', 'ctx'))
- gate_gradient: float32 [2048, 8192], P(('shard', 'ctx'), 'tensor')
- upward_gradient: float32 [2048, 8192], P(('shard', 'ctx'), 'tensor')
- downward_gradient: float32 [8192, 2048], P('tensor', ('shard', 'ctx'))
- querynorm_gradient: float32 [16, 128], P('tensor', ('shard', 'ctx'))
- keynorm_gradient: float32 [16, 128], P('tensor', ('shard', 'ctx'))
- postattention_gradient: float32 [2048], P(('shard', 'ctx'))
- postfeedforward_gradient: float32 [2048], P(('shard', 'ctx'))
- query_updated: float32 [2048, 2048], P(('shard', 'ctx'), 'tensor')
- key_updated: float32 [2048, 2048], P(('shard', 'ctx'), 'tensor')
- value_updated: float32 [2048, 2048], P(('shard', 'ctx'), 'tensor')
- output_updated: float32 [2048, 2048], P('tensor', ('shard', 'ctx'))
- gate_updated: float32 [2048, 8192], P(('shard', 'ctx'), 'tensor')
- upward_updated: float32 [2048, 8192], P(('shard', 'ctx'), 'tensor')
- downward_updated: float32 [8192, 2048], P('tensor', ('shard', 'ctx'))
- querynorm_updated: float32 [16, 128], P('tensor', ('shard', 'ctx'))
- keynorm_updated: float32 [16, 128], P('tensor', ('shard', 'ctx'))
- postattention_updated: float32 [2048], P(('shard', 'ctx'))
- postfeedforward_updated: float32 [2048], P(('shard', 'ctx'))
- query_newmean: float32 [2048, 2048], P(('shard', 'ctx'), 'tensor')
- key_newmean: float32 [2048, 2048], P(('shard', 'ctx'), 'tensor')
- value_newmean: float32 [2048, 2048], P(('shard', 'ctx'), 'tensor')
- output_newmean: float32 [2048, 2048], P('tensor', ('shard', 'ctx'))
- gate_newmean: float32 [2048, 8192], P(('shard', 'ctx'), 'tensor')
- upward_newmean: float32 [2048, 8192], P(('shard', 'ctx'), 'tensor')
- downward_newmean: float32 [8192, 2048], P('tensor', ('shard', 'ctx'))
- querynorm_newmean: float32 [16, 128], P('tensor', ('shard', 'ctx'))
- keynorm_newmean: float32 [16, 128], P('tensor', ('shard', 'ctx'))
- postattention_newmean: float32 [2048], P(('shard', 'ctx'))
- postfeedforward_newmean: float32 [2048], P(('shard', 'ctx'))
- query_newsquare: float32 [2048, 2048], P(('shard', 'ctx'), 'tensor')
- key_newsquare: float32 [2048, 2048], P(('shard', 'ctx'), 'tensor')
- value_newsquare: float32 [2048, 2048], P(('shard', 'ctx'), 'tensor')
- output_newsquare: float32 [2048, 2048], P('tensor', ('shard', 'ctx'))
- gate_newsquare: float32 [2048, 8192], P(('shard', 'ctx'), 'tensor')
- upward_newsquare: float32 [2048, 8192], P(('shard', 'ctx'), 'tensor')
- downward_newsquare: float32 [8192, 2048], P('tensor', ('shard', 'ctx'))
- querynorm_newsquare: float32 [16, 128], P('tensor', ('shard', 'ctx'))
- keynorm_newsquare: float32 [16, 128], P('tensor', ('shard', 'ctx'))
- postattention_newsquare: float32 [2048], P(('shard', 'ctx'))
- postfeedforward_newsquare: float32 [2048], P(('shard', 'ctx'))
The draws below stay inside these ranges and needn't reach their ends.
Inputs may be any that keep to these rules, and one draw needn't show every extreme that they name: `segment_ids`: document numbers never fall along a sequence; each of the 3 documents holds 1 to 1280 positions, one exactly 1280.
All inputs are finite; a program needn't handle non-finite values.
Results may differ from the reference program's by a relative error of at most 0.025.
Values may be sent and summed in bfloat16 or wider, within the bound.
No kernel may reach another device: no remote copies, remote signals or barrier semaphores. Data moves between devices by JAX's collectives and lax.ppermute only.
A program may use at most 320 MiB of HBM per device.

```python
import math
import jax
import jax.numpy as jnp
import numpy as np
from jax import lax

D = 2048
HEADS = 16
HEAD_DIM = 128
FF = 8192
LENGTH = 2048
DOCS = 3
SEQS = 4
MOST = 1280


def steps_of(stream_key, shape, split, low, largest):
    def one(position, shards_of):
        steps = jax.random.uniform(jax.random.fold_in(jax.random.fold_in(stream_key, 6), position), (shards_of,), jnp.float32, low / len(split), largest / len(split))
        return jnp.repeat(jnp.exp(steps), shape[position] // shards_of).reshape((-1,) + (1,) * (len(shape) - position - 1))

    level = one(*split[0])
    for cut in split[1:]:
        level = level * one(*cut)
    return level


def profile(number_of, total, bound, lean):
    portions = [(1 << 20) // math.isqrt(rank ** lean) + 1 for rank in range(2, number_of + 1)]
    surplus, given = total - bound - (number_of - 1), [1] * (number_of - 1)
    while surplus > 0:
        free = [i for i in range(number_of - 1) if given[i] < bound]
        whole, left = sum([portions[i] for i in free]), surplus
        for i in free:
            addition = min(bound - given[i], max(1, left * portions[i] // whole), surplus)
            given[i] = given[i] + addition
            surplus = surplus - addition
    return np.array([bound] + given)


def ragged(own_key, number_of, total, limit, skew):
    if number_of == 2:
        one = jax.random.randint(own_key, (), max(1, total - limit), min(limit, total - 1) + 1)
        return jnp.stack([one, total - one])
    lengths = jnp.asarray(profile(number_of, total, limit, skew), jnp.int32)
    twos = (number_of - 1) // 2
    donor, taker = lengths[1:1 + 2 * twos:2], lengths[2:2 + 2 * twos:2]
    slack = jnp.minimum(donor - 1, limit - taker)
    shifted = jax.random.randint(jax.random.fold_in(own_key, 1), (twos,), 0, 1 << 20) % (slack + 1)
    lengths = lengths.at[1:1 + 2 * twos:2].set(donor - shifted).at[2:2 + 2 * twos:2].set(taker + shifted)
    return lengths[jax.random.permutation(jax.random.fold_in(own_key, 2), number_of)]


def normal_values(stream_key, dims, spread, limit, split=(), held_as=jnp.bfloat16):
    entries = jax.random.normal(stream_key, dims, jnp.float32) * spread
    if len(split) > 0:
        entries = steps_of(stream_key, dims, split, -0.22, 0.18) * entries
    return jnp.clip(entries, min=-limit, max=limit).astype(held_as)


def setup_inputs(seed: int = 0) -> dict:
    seeds = jax.random.split(jax.random.key(seed), 37)
    tokens = normal_values(seeds[0], (SEQS, LENGTH, D), 1.0, 6.0, ((0, 4), (1, 2)))
    cotangent = normal_values(seeds[1], (SEQS, LENGTH, D), 1.0, 6.0, ((0, 4), (1, 2)))
    segment_ids = jax.vmap(lambda own: jnp.searchsorted(jnp.cumsum(ragged(own, DOCS, LENGTH, MOST, 0)), jnp.arange(LENGTH), side="right"))(jax.random.split(seeds[2], SEQS)).reshape((SEQS, LENGTH)).astype(jnp.int32)
    query_weight = normal_values(seeds[3], (D, D), D ** -0.5, 0.125, ((0, 8), (1, 4)), jnp.float32)
    key_weight = normal_values(seeds[4], (D, D), D ** -0.5, 0.125, ((0, 8), (1, 4)), jnp.float32)
    value_weight = normal_values(seeds[5], (D, D), D ** -0.5, 0.125, ((0, 8), (1, 4)), jnp.float32)
    output_weight = normal_values(seeds[6], (D, D), D ** -0.5, 0.125, ((0, 4), (1, 8)), jnp.float32)
    gate_weight = normal_values(seeds[7], (D, FF), D ** -0.5, 0.125, ((0, 8), (1, 4)), jnp.float32)
    upward_weight = normal_values(seeds[8], (D, FF), D ** -0.5, 0.125, ((0, 8), (1, 4)), jnp.float32)
    downward_weight = normal_values(seeds[9], (FF, D), FF ** -0.5, 0.0625, ((0, 4), (1, 8)), jnp.float32)
    querynorm_weight = jnp.clip(1.0 + 0.1 * jax.random.normal(seeds[10], (HEADS, HEAD_DIM), jnp.float32), 0.5, 1.5)
    keynorm_weight = jnp.clip(1.0 + 0.1 * jax.random.normal(seeds[11], (HEADS, HEAD_DIM), jnp.float32), 0.5, 1.5)
    postattention_weight = jnp.clip(1.0 + 0.1 * jax.random.normal(seeds[12], (D,), jnp.float32), 0.5, 1.5)
    postfeedforward_weight = jnp.clip(1.0 + 0.1 * jax.random.normal(seeds[13], (D,), jnp.float32), 0.5, 1.5)
    query_mean = normal_values(seeds[14], (D, D), (0.2 * (SEQS * LENGTH) ** 0.5), 112.0, ((0, 8), (1, 4)), jnp.float32)
    key_mean = normal_values(seeds[15], (D, D), (0.2 * (SEQS * LENGTH) ** 0.5), 112.0, ((0, 8), (1, 4)), jnp.float32)
    value_mean = normal_values(seeds[16], (D, D), (0.2 * (SEQS * LENGTH) ** 0.5), 112.0, ((0, 8), (1, 4)), jnp.float32)
    output_mean = normal_values(seeds[17], (D, D), (0.2 * (SEQS * LENGTH) ** 0.5), 112.0, ((0, 4), (1, 8)), jnp.float32)
    gate_mean = normal_values(seeds[18], (D, FF), (0.1 * (SEQS * LENGTH) ** 0.5), 56.0, ((0, 8), (1, 4)), jnp.float32)
    upward_mean = normal_values(seeds[19], (D, FF), (0.1 * (SEQS * LENGTH) ** 0.5), 56.0, ((0, 8), (1, 4)), jnp.float32)
    downward_mean = normal_values(seeds[20], (FF, D), (0.2 * (SEQS * LENGTH) ** 0.5), 112.0, ((0, 4), (1, 8)), jnp.float32)
    querynorm_mean = normal_values(seeds[21], (HEADS, HEAD_DIM), (0.2 * (SEQS * LENGTH) ** 0.5), 112.0, ((0, 4), (1, 8)), jnp.float32)
    keynorm_mean = normal_values(seeds[22], (HEADS, HEAD_DIM), (0.2 * (SEQS * LENGTH) ** 0.5), 112.0, ((0, 4), (1, 8)), jnp.float32)
    postattention_mean = normal_values(seeds[23], (D,), (0.2 * (SEQS * LENGTH) ** 0.5), 112.0, ((0, 8),), jnp.float32)
    postfeedforward_mean = normal_values(seeds[24], (D,), (0.2 * (SEQS * LENGTH) ** 0.5), 112.0, ((0, 8),), jnp.float32)
    query_square = jnp.clip(409.0 + 1229.0 * jax.random.uniform(seeds[25], (D, D), jnp.float32) ** steps_of(seeds[25], (D, D), ((0, 8), (1, 4)), -0.2, 0.2), 409.0, 1638.0)
    key_square = jnp.clip(409.0 + 1229.0 * jax.random.uniform(seeds[26], (D, D), jnp.float32) ** steps_of(seeds[26], (D, D), ((0, 8), (1, 4)), -0.2, 0.2), 409.0, 1638.0)
    value_square = jnp.clip(409.0 + 1229.0 * jax.random.uniform(seeds[27], (D, D), jnp.float32) ** steps_of(seeds[27], (D, D), ((0, 8), (1, 4)), -0.2, 0.2), 409.0, 1638.0)
    output_square = jnp.clip(409.0 + 1229.0 * jax.random.uniform(seeds[28], (D, D), jnp.float32) ** steps_of(seeds[28], (D, D), ((0, 4), (1, 8)), -0.2, 0.2), 409.0, 1638.0)
    gate_square = jnp.clip(81.0 + 246.0 * jax.random.uniform(seeds[29], (D, FF), jnp.float32) ** steps_of(seeds[29], (D, FF), ((0, 8), (1, 4)), -0.2, 0.2), 81.0, 327.0)
    upward_square = jnp.clip(81.0 + 246.0 * jax.random.uniform(seeds[30], (D, FF), jnp.float32) ** steps_of(seeds[30], (D, FF), ((0, 8), (1, 4)), -0.2, 0.2), 81.0, 327.0)
    downward_square = jnp.clip(409.0 + 1229.0 * jax.random.uniform(seeds[31], (FF, D), jnp.float32) ** steps_of(seeds[31], (FF, D), ((0, 4), (1, 8)), -0.2, 0.2), 409.0, 1638.0)
    querynorm_square = jnp.clip(819.0 + 2457.0 * jax.random.uniform(seeds[32], (HEADS, HEAD_DIM), jnp.float32) ** steps_of(seeds[32], (HEADS, HEAD_DIM), ((0, 4), (1, 8)), -0.2, 0.2), 819.0, 3276.0)
    keynorm_square = jnp.clip(819.0 + 2457.0 * jax.random.uniform(seeds[33], (HEADS, HEAD_DIM), jnp.float32) ** steps_of(seeds[33], (HEADS, HEAD_DIM), ((0, 4), (1, 8)), -0.2, 0.2), 819.0, 3276.0)
    postattention_square = jnp.clip(204.0 + 615.0 * jax.random.uniform(seeds[34], (D,), jnp.float32) ** steps_of(seeds[34], (D,), ((0, 8),), -0.2, 0.2), 204.0, 819.0)
    postfeedforward_square = jnp.clip(204.0 + 615.0 * jax.random.uniform(seeds[35], (D,), jnp.float32) ** steps_of(seeds[35], (D,), ((0, 8),), -0.2, 0.2), 204.0, 819.0)
    return dict(tokens=tokens, cotangent=cotangent, segment_ids=segment_ids, query_weight=query_weight, key_weight=key_weight, value_weight=value_weight, output_weight=output_weight, gate_weight=gate_weight, upward_weight=upward_weight, downward_weight=downward_weight, querynorm_weight=querynorm_weight, keynorm_weight=keynorm_weight, postattention_weight=postattention_weight, postfeedforward_weight=postfeedforward_weight, query_mean=query_mean, key_mean=key_mean, value_mean=value_mean, output_mean=output_mean, gate_mean=gate_mean, upward_mean=upward_mean, downward_mean=downward_mean, querynorm_mean=querynorm_mean, keynorm_mean=keynorm_mean, postattention_mean=postattention_mean, postfeedforward_mean=postfeedforward_mean, query_square=query_square, key_square=key_square, value_square=value_square, output_square=output_square, gate_square=gate_square, upward_square=upward_square, downward_square=downward_square, querynorm_square=querynorm_square, keynorm_square=keynorm_square, postattention_square=postattention_square, postfeedforward_square=postfeedforward_square)


rope_base = 500000.0
norm_eps = 1e-06
learn_rate = 0.3
beta_one = 0.9
beta_two = 0.95
adam_eps = 1e-08
decay_rate = 0.1
step_count = 2
masked_score = -1e+30

def rope_tables(positions, head_dim):
    half_dim = head_dim // 2
    frequencies = rope_base ** (-(jnp.arange(half_dim, dtype=jnp.float32) * 2.0) / head_dim)
    angles = positions.astype(jnp.float32)[:, None] * frequencies[None, :]
    angles = jnp.concatenate([angles, angles], axis=1)
    return (jnp.cos(angles)[:, None, :], jnp.sin(angles)[:, None, :])

def rotate_half(vector):
    half_dim = vector.shape[-1] // 2
    return jnp.concatenate([-vector[..., half_dim:], vector[..., :half_dim]], axis=-1)

def apply_rope(vector, cosine, sine_table):
    return vector * cosine + rotate_half(vector) * sine_table

def rope_back(gradient, cosine, sine_table):
    return gradient * cosine - rotate_half(gradient * sine_table)

def norm_back(scaled, normed, inverse):
    return inverse * (scaled - normed * lax.optimization_barrier(jnp.mean(scaled * normed, axis=-1, keepdims=True)))

def adam_step(weight, first_moment, second_moment, gradient):
    new_first = beta_one * first_moment + (1.0 - beta_one) * gradient
    new_second = beta_two * second_moment + (1.0 - beta_two) * gradient * gradient
    first_hat = new_first / (1.0 - beta_one ** step_count)
    second_hat = new_second / (1.0 - beta_two ** step_count)
    updated = weight - learn_rate * (first_hat / (jnp.sqrt(second_hat) + adam_eps) + decay_rate * weight)
    return (updated, new_first, new_second)

def reference(tokens, cotangent, segment_ids, query_weight, key_weight, value_weight, output_weight, gate_weight, upward_weight, downward_weight, querynorm_weight, keynorm_weight, postattention_weight, postfeedforward_weight, query_mean, key_mean, value_mean, output_mean, gate_mean, upward_mean, downward_mean, querynorm_mean, keynorm_mean, postattention_mean, postfeedforward_mean, query_square, key_square, value_square, output_square, gate_square, upward_square, downward_square, querynorm_square, keynorm_square, postattention_square, postfeedforward_square):
    masters = [query_weight, key_weight, value_weight, output_weight, gate_weight, upward_weight, downward_weight, querynorm_weight, keynorm_weight, postattention_weight, postfeedforward_weight]
    first_moments = [query_mean, key_mean, value_mean, output_mean, gate_mean, upward_mean, downward_mean, querynorm_mean, keynorm_mean, postattention_mean, postfeedforward_mean]
    second_moments = [query_square, key_square, value_square, output_square, gate_square, upward_square, downward_square, querynorm_square, keynorm_square, postattention_square, postfeedforward_square]
    halves = [lax.optimization_barrier(weight.astype(jnp.bfloat16)) for weight in masters]
    w_query, w_key, w_value, w_out, w_gate, w_upward, w_down, gain_query, gain_key, gain_attn, gain_ffn = halves
    query_scale = gain_query.astype(jnp.float32).reshape(-1)
    key_scale = gain_key.astype(jnp.float32).reshape(-1)
    attn_gain = gain_attn.astype(jnp.float32)
    ffn_gain = gain_ffn.astype(jnp.float32)
    doc_range = jnp.arange(DOCS, dtype=jnp.int32)
    key_index = jnp.arange(LENGTH, dtype=jnp.int32)
    divisor = math.sqrt(HEAD_DIM)
    f32 = jnp.float32
    b16 = jnp.bfloat16

    def one_sequence(running, operands):
        inputs, cot_rows, documents = operands
        counts = lax.optimization_barrier(jnp.sum((documents[:, None] == doc_range[None, :]).astype(jnp.int32), axis=0)).astype(jnp.int32)
        starts = (jnp.cumsum(counts) - counts).astype(jnp.int32)
        own_start = lax.optimization_barrier(jnp.sum(jnp.where(documents[:, None] == doc_range[None, :], starts[None, :], 0), axis=1)).astype(jnp.int32)
        positions = (key_index - own_start).astype(jnp.int32)
        cosine, sine_table = rope_tables(positions, HEAD_DIM)
        allowed = (key_index[None, :] <= key_index[:, None]) & (documents[None, :] == documents[:, None])

        def head_scores(query_head, key_head):
            scores = jnp.dot(query_head, key_head.T, preferred_element_type=f32) / divisor
            return jnp.where(allowed, scores, masked_score)

        def head_forward(head_ops):
            query_head, key_head, value_head = head_ops
            scores = head_scores(query_head, key_head)
            row_peak = lax.optimization_barrier(jnp.max(scores, axis=1, keepdims=True))
            exponent = jnp.exp(scores - row_peak)
            row_total = lax.optimization_barrier(jnp.sum(exponent, axis=1, keepdims=True))
            soft_half = (exponent / row_total).astype(b16)
            attended_head = jnp.dot(soft_half, value_head, preferred_element_type=f32)
            return (attended_head, (row_peak + jnp.log(row_total))[:, 0])

        def head_backward(head_ops):
            query_head, key_head, value_head, log_head, grad_head, delta_head = head_ops
            scores = head_scores(query_head, key_head)
            soft_back = jnp.exp(scores - log_head[:, None])
            back_half = soft_back.astype(b16)
            grad_value_head = jnp.dot(back_half.T, grad_head, preferred_element_type=f32)
            grad_soft = jnp.dot(grad_head, value_head.T, preferred_element_type=f32)
            grad_scores = (soft_back * (grad_soft - delta_head[:, None]) / divisor).astype(b16)
            grad_query_head = jnp.dot(grad_scores, key_head, preferred_element_type=f32)
            grad_key_head = jnp.dot(grad_scores.T, query_head, preferred_element_type=f32)
            return (grad_query_head, grad_key_head, grad_value_head)
        query_raw = jnp.dot(inputs, w_query, preferred_element_type=f32)
        key_raw = jnp.dot(inputs, w_key, preferred_element_type=f32)
        value_half = jnp.dot(inputs, w_value, preferred_element_type=f32).astype(b16)
        query_inv = lax.rsqrt(lax.optimization_barrier(jnp.mean(query_raw * query_raw, axis=1, keepdims=True)) + norm_eps)
        key_inv = lax.rsqrt(lax.optimization_barrier(jnp.mean(key_raw * key_raw, axis=1, keepdims=True)) + norm_eps)
        query_unit = query_raw * query_inv
        key_unit = key_raw * key_inv
        query_rot = apply_rope((query_unit * query_scale).reshape(LENGTH, HEADS, HEAD_DIM), cosine, sine_table).astype(b16)
        key_rot = apply_rope((key_unit * key_scale).reshape(LENGTH, HEADS, HEAD_DIM), cosine, sine_table).astype(b16)
        query_heads = jnp.transpose(query_rot, (1, 0, 2))
        key_heads = jnp.transpose(key_rot, (1, 0, 2))
        value_heads = jnp.transpose(value_half.reshape(LENGTH, HEADS, HEAD_DIM), (1, 0, 2))
        attended_heads, log_totals = lax.map(head_forward, (query_heads, key_heads, value_heads))
        attended = jnp.transpose(attended_heads, (1, 0, 2)).reshape(LENGTH, D).astype(b16)
        branch = jnp.dot(attended, w_out, preferred_element_type=f32)
        branch_inv = lax.rsqrt(lax.optimization_barrier(jnp.mean(branch * branch, axis=1, keepdims=True)) + norm_eps)
        branch_unit = branch * branch_inv
        residual = inputs.astype(f32) + branch_unit * attn_gain
        residual_half = residual.astype(b16)
        gate_pre = jnp.dot(residual_half, w_gate, preferred_element_type=f32)
        up_pre = jnp.dot(residual_half, w_upward, preferred_element_type=f32)
        gate_sigmoid = jax.nn.sigmoid(gate_pre)
        silu_value = gate_pre * gate_sigmoid
        activated = (silu_value * up_pre).astype(b16)
        ffn_out = jnp.dot(activated, w_down, preferred_element_type=f32)
        ffn_inv = lax.rsqrt(lax.optimization_barrier(jnp.mean(ffn_out * ffn_out, axis=1, keepdims=True)) + norm_eps)
        ffn_unit = ffn_out * ffn_inv
        block_rows = residual + ffn_unit * ffn_gain
        grad_out = cot_rows.astype(f32)
        grad_ffn_gain = lax.optimization_barrier(jnp.sum(grad_out * ffn_unit, axis=0))
        grad_ffn = norm_back(grad_out * ffn_gain, ffn_unit, ffn_inv).astype(b16)
        grad_down = jnp.dot(activated.T, grad_ffn, preferred_element_type=f32)
        grad_act = jnp.dot(grad_ffn, w_down.T, preferred_element_type=f32)
        grad_gate_pre = (grad_act * up_pre * gate_sigmoid * (1.0 + gate_pre * (1.0 - gate_sigmoid))).astype(b16)
        grad_up_pre = (grad_act * silu_value).astype(b16)
        grad_gate = jnp.dot(residual_half.T, grad_gate_pre, preferred_element_type=f32)
        grad_upward = jnp.dot(residual_half.T, grad_up_pre, preferred_element_type=f32)
        back_ffn = jnp.dot(grad_gate_pre, w_gate.T, preferred_element_type=f32) + jnp.dot(grad_up_pre, w_upward.T, preferred_element_type=f32)
        grad_res = grad_out + back_ffn
        grad_attn_gain = lax.optimization_barrier(jnp.sum(grad_res * branch_unit, axis=0))
        grad_branch = norm_back(grad_res * attn_gain, branch_unit, branch_inv).astype(b16)
        grad_outw = jnp.dot(attended.T, grad_branch, preferred_element_type=f32)
        grad_attended = jnp.dot(grad_branch, w_out.T, preferred_element_type=f32).astype(b16)
        row_delta = lax.optimization_barrier(jnp.sum((grad_attended.astype(f32) * attended.astype(f32)).reshape(LENGTH, HEADS, HEAD_DIM), axis=2))
        grad_heads = jnp.transpose(grad_attended.reshape(LENGTH, HEADS, HEAD_DIM), (1, 0, 2))
        grad_query_heads, grad_key_heads, grad_value_heads = lax.map(head_backward, (query_heads, key_heads, value_heads, log_totals, grad_heads, jnp.transpose(row_delta)))
        grad_query_rot = jnp.transpose(grad_query_heads, (1, 0, 2))
        grad_key_rot = jnp.transpose(grad_key_heads, (1, 0, 2))
        grad_value_half = jnp.transpose(grad_value_heads, (1, 0, 2)).astype(b16).reshape(LENGTH, D)
        grad_query_unit = rope_back(grad_query_rot, cosine, sine_table).reshape(LENGTH, D)
        grad_key_unit = rope_back(grad_key_rot, cosine, sine_table).reshape(LENGTH, D)
        grad_gain_query = lax.optimization_barrier(jnp.sum(grad_query_unit * query_unit, axis=0)).reshape(HEADS, HEAD_DIM)
        grad_gain_key = lax.optimization_barrier(jnp.sum(grad_key_unit * key_unit, axis=0)).reshape(HEADS, HEAD_DIM)
        grad_query_raw = norm_back(grad_query_unit * query_scale, query_unit, query_inv).astype(b16)
        grad_key_raw = norm_back(grad_key_unit * key_scale, key_unit, key_inv).astype(b16)
        back_attn = jnp.dot(grad_query_raw, w_query.T, preferred_element_type=f32) + jnp.dot(grad_key_raw, w_key.T, preferred_element_type=f32) + jnp.dot(grad_value_half, w_value.T, preferred_element_type=f32)
        input_rows = grad_res + back_attn
        grad_query_w = jnp.dot(inputs.T, grad_query_raw, preferred_element_type=f32)
        grad_key_w = jnp.dot(inputs.T, grad_key_raw, preferred_element_type=f32)
        grad_value_w = jnp.dot(inputs.T, grad_value_half, preferred_element_type=f32)
        fresh = [grad_query_w, grad_key_w, grad_value_w, grad_outw, grad_gate, grad_upward, grad_down, grad_gain_query, grad_gain_key, grad_attn_gain, grad_ffn_gain]
        return ([total_grad + fresh_grad for total_grad, fresh_grad in zip(running, fresh)], (block_rows, input_rows))
    zero_sums = [jnp.zeros(weight.shape, jnp.float32) for weight in masters]
    grads, outputs = lax.scan(one_sequence, zero_sums, (tokens, cotangent, segment_ids))
    block_out, input_grad = outputs
    stepped = [adam_step(masters[index], first_moments[index], second_moments[index], grads[index]) for index in range(11)]
    updated = [triple[0] for triple in stepped]
    newmean = [triple[1] for triple in stepped]
    newsquare = [triple[2] for triple in stepped]
    return (block_out, input_grad, grads[0], grads[1], grads[2], grads[3], grads[4], grads[5], grads[6], grads[7], grads[8], grads[9], grads[10], updated[0], updated[1], updated[2], updated[3], updated[4], updated[5], updated[6], updated[7], updated[8], updated[9], updated[10], newmean[0], newmean[1], newmean[2], newmean[3], newmean[4], newmean[5], newmean[6], newmean[7], newmean[8], newmean[9], newmean[10], newsquare[0], newsquare[1], newsquare[2], newsquare[3], newsquare[4], newsquare[5], newsquare[6], newsquare[7], newsquare[8], newsquare[9], newsquare[10])
```

```python
import math

import jax
import jax.numpy as jnp
from jax import lax
from jax.sharding import Mesh
from jax.sharding import PartitionSpec as P

DOCS = 3
rope_base = 500000.0
norm_eps = 1e-06
learn_rate = 0.3
beta_one = 0.9
beta_two = 0.95
adam_eps = 1e-08
decay_rate = 0.1
step_count = 2
masked_score = -1e30

f32 = jnp.float32
b16 = jnp.bfloat16

SH, SL, CX, TX, TC = "sh", "sl", "ctx", "tx", "tc"
SHARD = (SH, SL)
TENSOR = (TX, TC)


def dot(a, b, ca, cb):
    return lax.dot_general(a, b, (((ca,), (cb,)), ((), ())), preferred_element_type=f32)


def swap(value, axis):
    return lax.ppermute(value, axis, [(0, 1), (1, 0)])


def pair(mine, other, axis):
    first = lax.axis_index(axis) == 0
    return jnp.where(
        first, jnp.concatenate([mine, other], 0), jnp.concatenate([other, mine], 0)
    )


def gather_axis(value, axis):
    if lax.axis_size(axis) == 2:
        return pair(value, swap(value, axis), axis)
    return lax.all_gather(value, axis, axis=0, tiled=True)


def scatter_axis(value, axis):
    size = lax.axis_size(axis)
    if size != 2:
        return lax.psum_scatter(value.astype(b16), axis, scatter_dimension=0, tiled=True).astype(f32)
    half = value.shape[0] // 2
    index = lax.axis_index(axis)
    mine = lax.dynamic_slice_in_dim(value, index * half, half, 0)
    theirs = lax.dynamic_slice_in_dim(value, (1 - index) * half, half, 0)
    return mine.astype(f32) + swap(theirs.astype(b16), axis).astype(f32)


def rows_sum(value):
    return scatter_axis(scatter_axis(value, TC), TX)


def rows_all(value):
    return gather_axis(gather_axis(value, TX), TC)


def gather_z(value):
    return lax.all_gather(value, SHARD, axis=0, tiled=True)


def scatter_z(value):
    return lax.psum_scatter(value, SHARD, scatter_dimension=0, tiled=True)


def rotate_half(vector):
    half_dim = vector.shape[-1] // 2
    return jnp.concatenate([-vector[..., half_dim:], vector[..., :half_dim]], axis=-1)


def apply_rope(vector, cosine, sine_table):
    return vector * cosine + rotate_half(vector) * sine_table


def rope_back(gradient, cosine, sine_table):
    return gradient * cosine - rotate_half(gradient * sine_table)


def adam_step(weight, first_moment, second_moment, gradient):
    new_first = beta_one * first_moment + (1.0 - beta_one) * gradient
    new_second = beta_two * second_moment + (1.0 - beta_two) * gradient * gradient
    first_hat = new_first / (1.0 - beta_one**step_count)
    second_hat = new_second / (1.0 - beta_two**step_count)
    updated = weight - learn_rate * (
        first_hat / (jnp.sqrt(second_hat) + adam_eps) + decay_rate * weight
    )
    return (updated, new_first, new_second)


def attention_forward(query_rot, keys_all, values_all, docs_here, docs_all, offset):
    row_count, heads_here, head_dim = query_rot.shape
    length = docs_all.shape[0]
    block_rows = min(512, row_count)
    blocks = row_count // block_rows
    key_index = jnp.arange(length, dtype=jnp.int32)
    divisor = math.sqrt(head_dim)
    firsts = jnp.arange(blocks, dtype=jnp.int32) * block_rows
    query_blocks = query_rot.reshape(blocks, block_rows, heads_here, head_dim)
    doc_blocks = docs_here.reshape(blocks, block_rows)

    def block_scores(query_block, first_row, doc_block):
        query_index = offset + first_row + jnp.arange(block_rows, dtype=jnp.int32)
        allowed = (key_index[None, :] <= query_index[:, None]) & (
            docs_all[None, :] == doc_block[:, None]
        )
        scores = (
            jnp.einsum("qhd,khd->hqk", query_block, keys_all, preferred_element_type=f32) / divisor
        )
        return jnp.where(allowed[None, :, :], scores, masked_score)

    def forward_block(operands):
        query_block, first_row, doc_block = operands
        scores = block_scores(query_block, first_row, doc_block)
        row_peak = jnp.max(scores, axis=2, keepdims=True)
        exponent = jnp.exp(scores - row_peak)
        row_total = jnp.sum(exponent, axis=2, keepdims=True)
        soft_half = (exponent / row_total).astype(b16)
        attended_block = jnp.einsum(
            "hqk,khd->qhd", soft_half, values_all, preferred_element_type=f32
        )
        return (attended_block, (row_peak + jnp.log(row_total))[:, :, 0])

    attended_blocks, log_totals = lax.map(forward_block, (query_blocks, firsts, doc_blocks))
    attended = attended_blocks.reshape(row_count, heads_here * head_dim).astype(b16)

    def backward(grad_attended):
        row_delta = jnp.sum(
            (grad_attended.astype(f32) * attended.astype(f32)).reshape(
                row_count, heads_here, head_dim
            ),
            axis=2,
        )
        delta_blocks = row_delta.reshape(blocks, block_rows, heads_here)
        grad_blocks = grad_attended.reshape(blocks, block_rows, heads_here, head_dim)

        def backward_block(state_pair, operands):
            grad_keys, grad_values = state_pair
            query_block, first_row, doc_block, log_block, grad_block, delta_block = operands
            scores = block_scores(query_block, first_row, doc_block)
            soft_back = jnp.exp(scores - log_block[:, :, None])
            back_half = soft_back.astype(b16)
            grad_values = grad_values + jnp.einsum(
                "hqk,qhd->khd", back_half, grad_block, preferred_element_type=f32
            )
            grad_soft = jnp.einsum(
                "qhd,khd->hqk", grad_block, values_all, preferred_element_type=f32
            )
            grad_scores = (
                soft_back * (grad_soft - jnp.transpose(delta_block)[:, :, None]) / divisor
            ).astype(b16)
            grad_query_block = jnp.einsum(
                "hqk,khd->qhd", grad_scores, keys_all, preferred_element_type=f32
            )
            grad_keys = grad_keys + jnp.einsum(
                "hqk,qhd->khd", grad_scores, query_block, preferred_element_type=f32
            )
            return ((grad_keys, grad_values), grad_query_block)

        zero_keys = jnp.zeros((length, heads_here, head_dim), f32)
        (grad_keys, grad_values), grad_query_blocks = lax.scan(
            backward_block,
            (zero_keys, zero_keys),
            (query_blocks, firsts, doc_blocks, log_totals, grad_blocks, delta_blocks),
        )
        return grad_query_blocks.reshape(row_count, heads_here, head_dim), grad_keys, grad_values

    return attended, backward


def shards(tokens, cotangent, segment_ids, *state):
    masters, first_moments, second_moments = state[:11], state[11:22], state[22:33]
    inputs = tokens[0]
    docs_here = segment_ids[0]
    rows, width = inputs.shape
    ring = lax.axis_size(SHARD)
    teams = lax.axis_size(TENSOR)
    y = lax.axis_index(CX)
    piece = masters[0].shape[0]
    local_width = masters[0].shape[1]
    heads_here = masters[7].shape[0]
    head_dim = width // (teams * heads_here)
    block = rows // teams
    my_block = lax.axis_index(TC) * lax.axis_size(TX) + lax.axis_index(TX)

    def halves(value):
        split = value.reshape(value.shape[:-1] + (ring, 2, piece))
        axis = split.ndim - 2
        shape = value.shape[:-1] + (ring * piece,)
        return [
            lax.dynamic_index_in_dim(split, index, axis, keepdims=False).reshape(shape)
            for index in (y, 1 - y)
        ]

    def whole(own, oth):
        lead = own.shape[:-1]
        own, oth = (half.reshape(lead + (ring, 1, piece)) for half in (own, oth))
        axis = own.ndim - 2
        return jnp.where(
            y == 0, jnp.concatenate([own, oth], axis), jnp.concatenate([oth, own], axis)
        ).reshape(lead + (width,))

    def my_rows(value):
        return lax.dynamic_slice_in_dim(value, my_block * block, block, 0)

    pieces = [weight.astype(b16) for weight in masters[:7]]
    qkv_piece = jnp.concatenate(pieces[:3], axis=1)
    out_piece = jnp.transpose(pieces[3])
    gate_piece, up_piece = pieces[4], pieces[5]
    down_piece = jnp.transpose(pieces[6])
    gains = jnp.concatenate([gain.astype(b16).reshape(-1) for gain in masters[7:]])[None]
    docs_all = gather_axis(docs_here, CX)
    gains = gather_axis(gather_axis(gather_axis(gains, CX), SL), SH)
    qkv_own = gather_z(qkv_piece)
    qkv_oth = swap(qkv_own, CX)
    out_own = gather_z(out_piece)
    out_oth = swap(out_own, CX)
    gate_own = gather_z(gate_piece)
    gate_oth = swap(gate_own, CX)
    up_own = gather_z(up_piece)
    up_oth = swap(up_own, CX)
    down_swapped = swap(down_piece, CX)
    down_own = gather_z(down_piece)
    down_oth = gather_z(down_swapped)

    count = heads_here * (masters[7].shape[1])
    head_gain = lambda part: jnp.transpose(
        part.reshape(ring * 2, heads_here, masters[7].shape[1]), (1, 0, 2)
    ).reshape(local_width)
    query_scale = head_gain(gains[:, :count]).astype(f32)
    key_scale = head_gain(gains[:, count : 2 * count]).astype(f32)
    attn_gain = halves(gains[:, 2 * count : 2 * count + piece].reshape(width).astype(f32))
    ffn_gain = halves(gains[:, 2 * count + piece :].reshape(width).astype(f32))

    length = docs_all.shape[0]
    offset = y * rows
    doc_range = jnp.arange(DOCS, dtype=jnp.int32)
    counts = jnp.sum((docs_all[:, None] == doc_range[None, :]).astype(jnp.int32), axis=0)
    starts = jnp.cumsum(counts) - counts
    own_start = jnp.sum(
        jnp.where(docs_here[:, None] == doc_range[None, :], starts[None, :], 0), axis=1
    )
    positions = offset + jnp.arange(rows, dtype=jnp.int32) - own_start
    frequencies = rope_base ** (
        -(jnp.arange(head_dim // 2, dtype=jnp.float32) * 2.0) / head_dim
    )
    angles = positions.astype(f32)[:, None] * frequencies[None, :]
    cosine, sine_table = jnp.cos(angles), jnp.sin(angles)
    cosine = jnp.concatenate([cosine, cosine], axis=1)[:, None, :]
    sine_table = jnp.concatenate([sine_table, sine_table], axis=1)[:, None, :]

    x_half = halves(inputs)
    raw = dot(x_half[0], qkv_own, 1, 0) + dot(x_half[1], qkv_oth, 1, 0)
    query_raw, key_raw = raw[:, :local_width], raw[:, local_width : 2 * local_width]
    value_half = raw[:, 2 * local_width :].astype(b16).reshape(rows, heads_here, head_dim)
    square_sums = lax.psum(
        jnp.stack([jnp.sum(query_raw * query_raw, axis=1), jnp.sum(key_raw * key_raw, axis=1)]),
        TENSOR,
    )
    inverses = lax.rsqrt(square_sums / width + norm_eps)
    query_inv, key_inv = inverses[0][:, None], inverses[1][:, None]
    query_unit = query_raw * query_inv
    key_unit = key_raw * key_inv
    query_rot = apply_rope(
        (query_unit * query_scale).reshape(rows, heads_here, head_dim), cosine, sine_table
    ).astype(b16)
    key_rot = apply_rope(
        (key_unit * key_scale).reshape(rows, heads_here, head_dim), cosine, sine_table
    ).astype(b16)
    keys_all = gather_axis(key_rot, CX)
    values_all = gather_axis(value_half, CX)
    attended, attention_backward = attention_forward(
        query_rot, keys_all, values_all, docs_here, docs_all, offset
    )
    branch = [rows_sum(dot(attended, w, 1, 1)) for w in (out_own, out_oth)]
    mean_of = lambda a, b: sum(jnp.sum(u * v, axis=1, keepdims=True) for u, v in zip(a, b)) / width
    branch_inv = lax.rsqrt(mean_of(branch, branch) + norm_eps)
    branch_unit = [part * branch_inv for part in branch]
    x_rows = halves(my_rows(inputs).astype(f32))
    residual = [x + u * g for x, u, g in zip(x_rows, branch_unit, attn_gain)]
    res_half = [rows_all(part.astype(b16)) for part in residual]

    gate_pre = dot(res_half[0], gate_own, 1, 0) + dot(res_half[1], gate_oth, 1, 0)
    up_pre = dot(res_half[0], up_own, 1, 0) + dot(res_half[1], up_oth, 1, 0)
    gate_sigmoid = jax.nn.sigmoid(gate_pre)
    silu_value = gate_pre * gate_sigmoid
    activated = (silu_value * up_pre).astype(b16)
    ffn_out = [rows_sum(dot(activated, w, 1, 1)) for w in (down_own, down_oth)]
    ffn_inv = lax.rsqrt(mean_of(ffn_out, ffn_out) + norm_eps)
    ffn_unit = [part * ffn_inv for part in ffn_out]
    grad_out = halves(my_rows(cotangent[0]).astype(f32))
    scaled_out = [g * w for g, w in zip(grad_out, ffn_gain)]
    dots = mean_of(scaled_out, ffn_unit)
    d_ffn = [
        rows_all((ffn_inv * (s - u * dots)).astype(b16)) for s, u in zip(scaled_out, ffn_unit)
    ]
    grad_ffn_gain = [jnp.sum(g * u, axis=0) for g, u in zip(grad_out, ffn_unit)]
    block_rows = whole(*[r + u * g for r, u, g in zip(residual, ffn_unit, ffn_gain)])
    block_share = rows_all(block_rows.astype(b16)).astype(f32)

    def finish(own, oth):
        received = swap(oth.astype(b16), CX)
        return scatter_z((own + received.astype(f32)).astype(b16)).astype(f32)

    down_parts = [scatter_z(dot(d, activated, 0, 0).astype(b16)) for d in d_ffn]
    grad_down = down_parts[0].astype(f32) + swap(down_parts[1], CX).astype(f32)
    grad_act = dot(d_ffn[0], down_own, 1, 0) + dot(d_ffn[1], down_oth, 1, 0)
    d_gate = (grad_act * up_pre * gate_sigmoid * (1.0 + gate_pre * (1.0 - gate_sigmoid))).astype(
        b16
    )
    d_up = (grad_act * silu_value).astype(b16)
    back_ffn = [
        rows_sum(dot(d_gate, g, 1, 1) + dot(d_up, u, 1, 1))
        for g, u in ((gate_own, up_own), (gate_oth, up_oth))
    ]
    grad_gate = finish(dot(res_half[0], d_gate, 0, 0), dot(res_half[1], d_gate, 0, 0))
    grad_upward = finish(dot(res_half[0], d_up, 0, 0), dot(res_half[1], d_up, 0, 0))
    grad_res = [g + b for g, b in zip(grad_out, back_ffn)]
    grad_attn_gain = [jnp.sum(g * u, axis=0) for g, u in zip(grad_res, branch_unit)]
    scaled_res = [g * w for g, w in zip(grad_res, attn_gain)]
    dots = mean_of(scaled_res, branch_unit)
    d_branch = [
        rows_all((branch_inv * (s - u * dots)).astype(b16))
        for s, u in zip(scaled_res, branch_unit)
    ]

    d_att = (dot(d_branch[0], out_own, 1, 0) + dot(d_branch[1], out_oth, 1, 0)).astype(b16)
    grad_outw = finish(dot(d_branch[0], attended, 0, 0), dot(d_branch[1], attended, 0, 0))
    grad_query_rot, grad_keys, grad_values = attention_backward(d_att)
    grad_key_rot = scatter_axis(grad_keys, CX)
    d_vals = scatter_axis(grad_values, CX).astype(b16).reshape(rows, local_width)
    grad_query_unit = rope_back(grad_query_rot, cosine, sine_table).reshape(rows, local_width)
    grad_key_unit = rope_back(grad_key_rot, cosine, sine_table).reshape(rows, local_width)
    grad_gain_query = jnp.sum(grad_query_unit * query_unit, axis=0)
    grad_gain_key = jnp.sum(grad_key_unit * key_unit, axis=0)
    scaled_query = grad_query_unit * query_scale
    scaled_key = grad_key_unit * key_scale
    norm_sums = lax.psum(
        jnp.stack(
            [jnp.sum(scaled_query * query_unit, axis=1), jnp.sum(scaled_key * key_unit, axis=1)]
        ),
        TENSOR,
    )
    d_q = (query_inv * (scaled_query - query_unit * (norm_sums[0] / width)[:, None])).astype(b16)
    d_k = (key_inv * (scaled_key - key_unit * (norm_sums[1] / width)[:, None])).astype(b16)
    d_qkv = jnp.concatenate([d_q, d_k, d_vals], axis=1)
    grad_qkv = finish(dot(x_half[0], d_qkv, 0, 0), dot(x_half[1], d_qkv, 0, 0))
    back_attn = [rows_sum(dot(d_qkv, w, 1, 1)) for w in (qkv_own, qkv_oth)]
    input_rows = whole(*[g + b for g, b in zip(grad_res, back_attn)])
    input_share = rows_all(input_rows.astype(b16)).astype(f32)

    index = lax.axis_index(SHARD) * 2 + y
    head_sums = lax.psum(jnp.stack([grad_gain_query, grad_gain_key]), (SH, SL, CX))
    head_sums = head_sums.reshape(2, heads_here, head_dim)
    head_piece = masters[7].shape[1]
    head_sums = lax.dynamic_slice_in_dim(head_sums, index * head_piece, head_piece, 2)
    wide_sums = lax.psum(
        jnp.stack([whole(*grad_attn_gain), whole(*grad_ffn_gain)]), (SH, SL, CX, TX, TC)
    )
    wide_sums = lax.dynamic_slice_in_dim(wide_sums, index * piece, piece, 1)

    grads = [
        grad_qkv[:, :local_width],
        grad_qkv[:, local_width : 2 * local_width],
        grad_qkv[:, 2 * local_width :],
        jnp.transpose(grad_outw),
        grad_gate,
        grad_upward,
        jnp.transpose(grad_down),
        head_sums[0],
        head_sums[1],
        wide_sums[0],
        wide_sums[1],
    ]
    stepped = [
        adam_step(masters[i], first_moments[i], second_moments[i], grads[i]) for i in range(11)
    ]
    return tuple(
        [block_share[None], input_share[None]]
        + grads
        + [triple[part] for part in range(3) for triple in stepped]
    )


def solution(mesh):
    ring, ctx, teams = (mesh.shape[name] for name in mesh.axis_names)
    fine = Mesh(
        mesh.devices.reshape(ring // 2, 2, ctx, teams // 2, 2), (SH, SL, CX, TX, TC)
    )
    owners = (SH, SL, CX)
    column = P(owners, TENSOR)
    row = P(TENSOR, owners)
    vector = P(owners)
    act = P(SHARD, CX, None)
    weights = (column, column, column, row, column, column, row, row, row, vector, vector)
    return jax.shard_map(
        shards,
        mesh=fine,
        in_specs=(act, act, P(SHARD, CX)) + weights * 3,
        out_specs=(act, act) + weights * 4,
        check_vma=False,
    )
```

```python
import functools
import math

import jax
import jax.numpy as jnp
from jax import lax
from jax.experimental import pallas as pl
from jax.experimental.pallas import tpu as pltpu
from jax.sharding import Mesh
from jax.sharding import PartitionSpec as P

DOCS = 3
rope_base = 500000.0
norm_eps = 1e-06
learn_rate = 0.3
beta_one = 0.9
beta_two = 0.95
adam_eps = 1e-08
decay_rate = 0.1
step_count = 2
masked_score = -1e30

f32 = jnp.float32
b16 = jnp.bfloat16
i32 = jnp.int32

SH, SL, CX, TX, TC = "sh", "sl", "ctx", "tx", "tc"
SHARD = (SH, SL)
TENSOR = (TX, TC)
PLANE = (CX, TX, TC)


def dot(a, b, ca, cb):
    return lax.dot_general(a, b, (((ca,), (cb,)), ((), ())), preferred_element_type=f32)


def swap(value, axis):
    return lax.ppermute(value, axis, [(0, 1), (1, 0)])


def pair(mine, other, axis, at=0):
    return jnp.where(
        lax.axis_index(axis) == 0,
        jnp.concatenate([mine, other], at),
        jnp.concatenate([other, mine], at),
    )


def gather_axis(value, axis):
    if lax.axis_size(axis) == 2:
        return pair(value, swap(value, axis), axis)
    return lax.all_gather(value, axis, axis=0, tiled=True)


def sum_axis(value, axis):
    if lax.axis_size(axis) == 2:
        return value + swap(value, axis)
    return lax.psum(value, axis)


def plane_sum(value):
    return sum_axis(sum_axis(sum_axis(value, TC), TX), CX)


def tie(*values):
    return lax.optimization_barrier(values)


def part(value, index, at):
    return lax.dynamic_index_in_dim(value, index, at, keepdims=False)


def rows_all(value):
    return gather_axis(gather_axis(value, TX), TC)


def spread(value, axis):
    if lax.axis_size(TX) == 2:
        half = value.shape[0] // 2
        over_x = swap(value, TX)
        over_y = swap(value, axis)
        near = swap(over_y[:half], TX)
        far = swap(over_x[half:], axis)
        mine = [value, over_x, over_y, near, far]
    else:
        line = lax.all_gather(value, TX, axis=0, tiled=True)
        mine = [line, swap(line, axis)]
    return mine, [swap(block, TC) for block in mine]


def joined(groups):
    return [jnp.concatenate(blocks, 0) for blocks in groups]


def across(mine, theirs):
    return (mine + swap(theirs.astype(b16), TC).astype(f32)).astype(b16)


def collect(both, axis):
    count = lax.axis_size(TX)
    block = both.shape[0] // (2 * count)
    if count == 2:
        half = block // 2
        near = swap(both[3 * block : 3 * block + half], TX)
        far = swap(both[3 * block + half :], axis)
        over_x = jnp.concatenate(
            [both[block : block + half], both[block + half : 2 * block] + far], 0
        )
        over_y = jnp.concatenate(
            [both[2 * block : 2 * block + half] + near, both[2 * block + half : 3 * block]], 0
        )
        return (
            both[:block].astype(f32)
            + swap(over_x, TX).astype(f32)
            + swap(over_y, axis).astype(f32)
        )
    line = both[: count * block] + swap(both[count * block :], axis)
    return lax.psum_scatter(line, TX, scatter_dimension=0, tiled=True).astype(f32)


def block_places(axis):
    count = lax.axis_size(TX)
    spot = jnp.arange(4 * count, dtype=i32)
    side = (spot // (2 * count)) ^ lax.axis_index(axis)
    core = (spot // count % 2) ^ lax.axis_index(TC)
    along = spot % count
    if count == 2:
        along = along ^ lax.axis_index(TX)
    return (core * 2 + side) * count + along


def params(steps):
    return pltpu.CompilerParams(
        dimension_semantics=("arbitrary",) * steps, vmem_limit_bytes=40 * 1024 * 1024
    )


def lasting(us):
    return pl.CostEstimate(flops=0, transcendentals=0, bytes_accessed=int(us * 0.5e6))


def upright(row, columns):
    return jnp.transpose(jnp.broadcast_to(row, (columns, row.shape[1])))


def row_sums(value):
    return jnp.sum(jnp.transpose(value), axis=0, keepdims=True)


def project_body(side, local, remote, weight, raw, squares):
    half = pl.num_programs(0) // 2
    mine = (pl.program_id(0) // half) == side[0]
    raw[...] = dot(jnp.where(mine, local[...], remote[...]), weight[...], 1, 0)
    width = raw.shape[1] // 3
    for which in range(2):
        total = jnp.zeros((raw.shape[0], 128), f32)
        for at in range(which * width, (which + 1) * width, 128):
            total += raw[:, at : at + 128] * raw[:, at : at + 128]
        squares[which : which + 1, :] = row_sums(total)


def project(side, local, remote, weight):
    rows, width = local.shape
    columns = weight.shape[1]
    step = min(256, rows)
    half = rows // step
    tokens = pl.BlockSpec((step, width), lambda i, side: (i % half, 0))
    return pl.pallas_call(
        project_body,
        grid_spec=pltpu.PrefetchScalarGridSpec(
            num_scalar_prefetch=1,
            grid=(2 * half,),
            in_specs=[
                tokens,
                tokens,
                pl.BlockSpec((width, columns), lambda i, side: (0, 0)),
            ],
            out_specs=[
                pl.BlockSpec((step, columns), lambda i, side: (i, 0)),
                pl.BlockSpec((2, step), lambda i, side: (0, i)),
            ],
        ),
        out_shape=[
            jax.ShapeDtypeStruct((2 * rows, columns), f32),
            jax.ShapeDtypeStruct((2, 2 * rows), f32),
        ],
        compiler_params=params(1),
        cost_estimate=lasting(12),
    )(side, local, remote, weight)


def turn(value, cosine, sine):
    return value * cosine + pltpu.roll(value, value.shape[1] // 2, 1) * sine


def turn_back(value, cosine, sine):
    return value * cosine + pltpu.roll(value * sine, value.shape[1] // 2, 1)


def prepare_body(raw, inverse, gain, cosine, sine, query, key, val):
    width = query.shape[1]
    size = cosine.shape[1]
    for which, out in ((0, query), (1, key)):
        scale = upright(inverse[which : which + 1, :], size)
        for at in range(0, width, size):
            unit = raw[:, which * width + at : which * width + at + size] * scale
            out[:, at : at + size] = turn(
                unit * gain[which : which + 1, at : at + size], cosine[...], sine[...]
            ).astype(b16)
    val[...] = raw[:, 2 * width :].astype(b16)


def prepare(raw, inverse, gain, cosine, sine):
    rows, width = raw.shape[0], raw.shape[1] // 3
    size = cosine.shape[1]
    step = min(256, rows)
    by_row = lambda columns: pl.BlockSpec((step, columns), lambda i: (i, 0))
    return pl.pallas_call(
        prepare_body,
        grid=(rows // step,),
        in_specs=[
            by_row(3 * width),
            pl.BlockSpec((2, step), lambda i: (0, i)),
            pl.BlockSpec((2, width), lambda i: (0, 0)),
            by_row(size),
            by_row(size),
        ],
        out_specs=[by_row(width)] * 3,
        out_shape=[jax.ShapeDtypeStruct((rows, width), b16)] * 3,
        compiler_params=params(1),
        cost_estimate=lasting(3),
    )(raw, inverse, gain, cosine, sine)


def allowed(start, first_key, first_query, shape):
    keys = first_key + lax.broadcasted_iota(i32, shape, 0)
    queries = first_query + lax.broadcasted_iota(i32, shape, 1)
    return (keys >= start) & (keys <= queries)


def forward_body(span, spot, low, query, keys, values, start, out, log_total):
    i = pl.program_id(1)
    rows, size = query.shape
    scale = 1.0 / math.sqrt(size)

    def step(j, carry):
        peak, total, summed = carry
        at = pl.multiple_of(j * span, span)
        scores = dot(keys[pl.ds(at, span), :], query[...], 1, 1) * scale
        scores = jnp.where(allowed(start[...], at, i * rows, scores.shape), scores, masked_score)
        new_peak = jnp.maximum(peak, jnp.max(scores, axis=0, keepdims=True))
        shrink = jnp.exp(peak - new_peak)
        exponent = jnp.exp(scores - new_peak)
        total = total * shrink + jnp.sum(exponent, axis=0, keepdims=True)
        summed = summed * shrink + dot(values[pl.ds(at, span), :], exponent.astype(b16), 0, 0)
        return new_peak, total, summed

    begin = (
        jnp.full((1, rows), masked_score, f32),
        jnp.zeros((1, rows), f32),
        jnp.zeros((size, rows), f32),
    )
    last = ((i + 1) * rows + span - 1) // span
    peak, total, summed = lax.fori_loop(low[i], last, step, begin)
    out[...] = jnp.transpose(summed / total).astype(b16)
    log_total[0] = peak + jnp.log(total)


def flash_forward(query, keys, values, start, spot, block, size):
    rows, width = query.shape
    heads = width // size
    blocks = rows // block
    span = min(512, rows)
    low = start.reshape(blocks, block)[:, 0] // span
    return pl.pallas_call(
        functools.partial(forward_body, span),
        grid_spec=pltpu.PrefetchScalarGridSpec(
            num_scalar_prefetch=2,
            grid=(heads, blocks),
            in_specs=[
                pl.BlockSpec((block, size), lambda h, i, spot, low: (i, h)),
                pl.BlockSpec((rows, size), lambda h, i, spot, low: (0, h)),
                pl.BlockSpec((rows, size), lambda h, i, spot, low: (0, h)),
                pl.BlockSpec((1, block), lambda h, i, spot, low: (0, i)),
            ],
            out_specs=[
                pl.BlockSpec((block, size), lambda h, i, spot, low: (spot[i], h)),
                pl.BlockSpec((1, 1, block), lambda h, i, spot, low: (h, 0, i)),
            ],
        ),
        out_shape=[
            jax.ShapeDtypeStruct((rows, width), b16),
            jax.ShapeDtypeStruct((heads, 1, rows), f32),
        ],
        compiler_params=params(2),
        cost_estimate=lasting(18),
    )(spot, low, query, keys, values, start[None])


def backward_body(
    span, spot, low, query, keys, values, start, log_total, grad, out, d_query, d_keys, d_values
):
    i = pl.program_id(1)
    rows, size = query.shape
    scale = 1.0 / math.sqrt(size)

    @pl.when(i == 0)
    def _():
        d_keys[...] = jnp.zeros_like(d_keys)
        d_values[...] = jnp.zeros_like(d_values)

    delta = row_sums(grad[...].astype(f32) * out[...].astype(f32))

    def step(j, summed):
        at = pl.multiple_of(j * span, span)
        here = pl.ds(at, span)
        scores = dot(keys[here, :], query[...], 1, 1) * scale
        mask = allowed(start[...], at, i * rows, scores.shape)
        soft = jnp.where(mask, jnp.exp(scores - log_total[0]), 0.0)
        d_soft = dot(values[here, :], grad[...], 1, 1)
        d_scores = (soft * (d_soft - delta) * scale).astype(b16)
        d_values[here, :] += dot(soft.astype(b16), grad[...], 1, 0)
        d_keys[here, :] += dot(d_scores, query[...], 1, 0)
        return summed + dot(keys[here, :], d_scores, 0, 0)

    last = ((i + 1) * rows + span - 1) // span
    summed = lax.fori_loop(low[i], last, step, jnp.zeros((size, rows), f32))
    d_query[...] = jnp.transpose(summed)


def flash_backward(query, keys, values, start, log_total, grad, out, spot, block, size):
    rows, width = query.shape
    heads = width // size
    blocks = rows // block
    span = min(512, rows)
    low = start.reshape(blocks, block)[:, 0] // span
    natural = pl.BlockSpec((block, size), lambda h, i, spot, low: (i, h))
    moved = pl.BlockSpec((block, size), lambda h, i, spot, low: (spot[i], h))
    full = pl.BlockSpec((rows, size), lambda h, i, spot, low: (0, h))
    return pl.pallas_call(
        functools.partial(backward_body, span),
        grid_spec=pltpu.PrefetchScalarGridSpec(
            num_scalar_prefetch=2,
            grid=(heads, blocks),
            in_specs=[
                natural,
                full,
                full,
                pl.BlockSpec((1, block), lambda h, i, spot, low: (0, i)),
                pl.BlockSpec((1, 1, block), lambda h, i, spot, low: (h, 0, i)),
                moved,
                moved,
            ],
            out_specs=[natural, full, full],
        ),
        out_shape=[jax.ShapeDtypeStruct((rows, width), f32)] * 3,
        compiler_params=params(2),
        cost_estimate=lasting(22),
    )(spot, low, query, keys, values, start[None], log_total, grad, out)


def turned_sums_body(raw, inverse, gain, cosine, sine, d_query, d_key, sums, gains):
    width = d_query.shape[1]
    size = cosine.shape[1]

    @pl.when(pl.program_id(0) == 0)
    def _():
        gains[...] = jnp.zeros_like(gains)

    for which, grad in ((0, d_query), (1, d_key)):
        row = jnp.zeros((raw.shape[0], size), f32)
        scale = upright(inverse[which : which + 1, :], size)
        for at in range(0, width, size):
            unit = raw[:, which * width + at : which * width + at + size] * scale
            product = turn_back(grad[:, at : at + size], cosine[...], sine[...]) * unit
            gains[which : which + 1, at : at + size] += jnp.sum(product, axis=0, keepdims=True)
            row += product * gain[which : which + 1, at : at + size]
        sums[which : which + 1, :] = row_sums(row)


def turned_sums(raw, inverse, gain, cosine, sine, d_query, d_key):
    rows, width = d_query.shape
    size = cosine.shape[1]
    step = min(256, rows)
    by_row = lambda columns: pl.BlockSpec((step, columns), lambda i: (i, 0))
    return pl.pallas_call(
        turned_sums_body,
        grid=(rows // step,),
        in_specs=[
            by_row(3 * width),
            pl.BlockSpec((2, step), lambda i: (0, i)),
            pl.BlockSpec((2, width), lambda i: (0, 0)),
            by_row(size),
            by_row(size),
            by_row(width),
            by_row(width),
        ],
        out_specs=[
            pl.BlockSpec((2, step), lambda i: (0, i)),
            pl.BlockSpec((2, width), lambda i: (0, 0)),
        ],
        out_shape=[
            jax.ShapeDtypeStruct((2, rows), f32),
            jax.ShapeDtypeStruct((2, width), f32),
        ],
        compiler_params=params(1),
        cost_estimate=lasting(4),
    )(raw, inverse, gain, cosine, sine, d_query, d_key)


def raw_grads_body(
    spot, raw, inverse, gain, cosine, sine, d_query, d_key, d_val, means, out, moved
):
    width = d_query.shape[1]
    size = cosine.shape[1]
    for which, grad in ((0, d_query), (1, d_key)):
        scale = upright(inverse[which : which + 1, :], size)
        mean = upright(means[which : which + 1, :], size)
        for at in range(0, width, size):
            place = slice(which * width + at, which * width + at + size)
            unit = raw[:, place] * scale
            scaled = (
                turn_back(grad[:, at : at + size], cosine[...], sine[...])
                * gain[which : which + 1, at : at + size]
            )
            out[:, place] = (scale * (scaled - unit * mean)).astype(b16)
    out[:, 2 * width :] = d_val[...].astype(b16)
    moved[...] = out[...]


def raw_grads(raw, inverse, gain, cosine, sine, d_query, d_key, d_val, means, spot, block):
    rows, width = d_query.shape
    size = cosine.shape[1]
    by_row = lambda columns: pl.BlockSpec((block, columns), lambda i, spot: (i, 0))
    in_line = pl.BlockSpec((2, block), lambda i, spot: (0, i))
    return pl.pallas_call(
        raw_grads_body,
        grid_spec=pltpu.PrefetchScalarGridSpec(
            num_scalar_prefetch=1,
            grid=(rows // block,),
            in_specs=[
                by_row(3 * width),
                in_line,
                pl.BlockSpec((2, width), lambda i, spot: (0, 0)),
                by_row(size),
                by_row(size),
                by_row(width),
                by_row(width),
                by_row(width),
                in_line,
            ],
            out_specs=[
                by_row(3 * width),
                pl.BlockSpec((block, 3 * width), lambda i, spot: (spot[i], 0)),
            ],
        ),
        out_shape=[jax.ShapeDtypeStruct((rows, 3 * width), b16)] * 2,
        compiler_params=params(1),
        cost_estimate=lasting(5),
    )(spot, raw, inverse, gain, cosine, sine, d_query, d_key, d_val, means)


def ffn_forward_body(count, *refs):
    blocks, (w_gate, w_up, full, gate, up, act) = refs[:count], refs[count:]

    @pl.when(pl.program_id(0) == 0)
    def _():
        at = 0
        for block in blocks:
            full[at : at + block.shape[0], :] = block[...]
            at += block.shape[0]

    gate_pre = dot(full[...], w_gate[...], 1, 0)
    up_pre = dot(full[...], w_up[...], 1, 0)
    gate[...] = gate_pre.astype(b16)
    up[...] = up_pre.astype(b16)
    act[...] = (gate_pre * jax.nn.sigmoid(gate_pre) * up_pre).astype(b16)


def ffn_forward(blocks, w_both):
    rows = sum(block.shape[0] for block in blocks)
    width, columns = w_both.shape
    step = min(256, columns // 2)
    count = columns // 2 // step
    out = pl.BlockSpec((rows, step), lambda j: (0, j))
    hidden = jax.ShapeDtypeStruct((rows, columns // 2), b16)
    return pl.pallas_call(
        functools.partial(ffn_forward_body, len(blocks)),
        grid=(count,),
        in_specs=[pl.BlockSpec(block.shape, lambda j: (0, 0)) for block in blocks]
        + [
            pl.BlockSpec((width, step), lambda j: (0, j)),
            pl.BlockSpec((width, step), lambda j: (0, j + count)),
        ],
        out_specs=[pl.BlockSpec((rows, width), lambda j: (0, 0)), out, out, out],
        out_shape=[jax.ShapeDtypeStruct((rows, width), b16), hidden, hidden, hidden],
        compiler_params=params(1),
        cost_estimate=lasting(10),
    )(*blocks, w_both, w_both)


def ffn_backward_body(grad, w_down, gate, up, d_gate, d_up):
    d_act = dot(grad[...], w_down[...], 1, 0)
    gate_pre, up_pre = gate[...].astype(f32), up[...].astype(f32)
    sigmoid = jax.nn.sigmoid(gate_pre)
    d_gate[...] = (d_act * up_pre * sigmoid * (1.0 + gate_pre * (1.0 - sigmoid))).astype(b16)
    d_up[...] = (d_act * gate_pre * sigmoid).astype(b16)


def ffn_backward(grad, w_down, gate, up):
    rows, width = grad.shape
    columns = w_down.shape[1]
    step = min(256, columns)
    out = pl.BlockSpec((rows, step), lambda j: (0, j))
    return pl.pallas_call(
        ffn_backward_body,
        grid=(columns // step,),
        in_specs=[
            pl.BlockSpec((rows, width), lambda j: (0, 0)),
            pl.BlockSpec((width, step), lambda j: (0, j)),
            out,
            out,
        ],
        out_specs=[out, out],
        out_shape=[jax.ShapeDtypeStruct((rows, columns), b16)] * 2,
        compiler_params=params(1),
        cost_estimate=lasting(6),
    )(grad, w_down, gate, up)


def ffn_residual_body(d_gate, d_up, w_gate, w_up, *rest):
    value = dot(d_gate[...], w_gate[...], 1, 1) + dot(d_up[...], w_up[...], 1, 1)
    if len(rest) == 2:
        value += rest[0][...].astype(f32)
    rest[-1][...] = value.astype(b16)


def ffn_residual(d_gate, d_up, w_both, *received):
    rows, columns = d_gate.shape
    width = w_both.shape[0]
    step = min(256, width)
    full = pl.BlockSpec((rows, columns), lambda j: (0, 0))
    out = pl.BlockSpec((rows, step), lambda j: (0, j))
    return pl.pallas_call(
        ffn_residual_body,
        grid=(width // step,),
        in_specs=[
            full,
            full,
            pl.BlockSpec((step, columns), lambda j: (j, 0)),
            pl.BlockSpec((step, columns), lambda j: (j, 1)),
        ]
        + [out] * len(received),
        out_specs=out,
        out_shape=jax.ShapeDtypeStruct((rows, width), b16),
        compiler_params=params(1),
        cost_estimate=lasting(9),
    )(d_gate, d_up, w_both, w_both, *received)


def flip_body(value, out):
    out[...] = jnp.transpose(value[...])


def flip(value):
    rows, columns = value.shape
    step = min(256, columns)
    return pl.pallas_call(
        flip_body,
        grid=(columns // step,),
        in_specs=[pl.BlockSpec((rows, step), lambda i: (0, i))],
        out_specs=pl.BlockSpec((step, rows), lambda i: (i, 0)),
        out_shape=jax.ShapeDtypeStruct((columns, rows), value.dtype),
        compiler_params=params(1),
    )(value)


def adam_step(weight, first_moment, second_moment, gradient):
    new_first = beta_one * first_moment + (1.0 - beta_one) * gradient
    new_second = beta_two * second_moment + (1.0 - beta_two) * gradient * gradient
    first_hat = new_first / (1.0 - beta_one**step_count)
    second_hat = new_second / (1.0 - beta_two**step_count)
    updated = weight - learn_rate * (
        first_hat / (jnp.sqrt(second_hat) + adam_eps) + decay_rate * weight
    )
    return (updated, new_first, new_second)


def assemble_body(flags, mine, theirs, out):
    own = (pl.program_id(0) // flags[1]) == flags[0]
    out[0] = jnp.where(own, mine[...], theirs[...]).astype(f32)


def assemble(mine, theirs, block):
    count = lax.axis_size(TX)
    width = mine.shape[1]
    shift = lax.axis_index(TX) if count == 2 else jnp.zeros((), i32)
    flags = jnp.stack([lax.axis_index(TC), jnp.full((), count, i32), shift])
    here = pl.BlockSpec((block, width), lambda i, flags: ((i % count) ^ flags[2], 0))
    return pl.pallas_call(
        assemble_body,
        grid_spec=pltpu.PrefetchScalarGridSpec(
            num_scalar_prefetch=1,
            grid=(2 * count,),
            in_specs=[here, here],
            out_specs=pl.BlockSpec((1, block, width), lambda i, flags: (0, i, 0)),
        ),
        out_shape=jax.ShapeDtypeStruct((1, 2 * count * block, width), f32),
        compiler_params=params(1),
        cost_estimate=lasting(5),
    )(flags, mine, theirs)


def over_chips(value):
    if lax.axis_size(TX) == 2:
        return jnp.concatenate([value, swap(value, TX)], 0)
    return lax.all_gather(value, TX, axis=0, tiled=True)


def adam_body(turned, flag, weight, first, second, own, other, grad, updated, mean, square):
    value = jnp.where(pl.program_id(0) == flag[0], own[...].astype(f32), other[...].astype(f32))
    if turned:
        value = jnp.transpose(value)
    grad[...] = value
    updated[...], mean[...], square[...] = adam_step(
        weight[...], first[...], second[...], value
    )


def adam(weight, first, second, own, other, flag, turned=False, column=0):
    rows, columns = weight.shape
    if turned:
        half = rows // 2
        step = min(256, half)
        count = half // step
        mine = pl.BlockSpec((step, columns), lambda j, i, flag: (j * count + i, 0))
        halves = pl.BlockSpec((columns, step), lambda j, i, flag: (0, i))
    else:
        half = columns // 2
        step = min(128, rows)
        count = rows // step
        mine = pl.BlockSpec((step, half), lambda j, i, flag: (i, j))
        halves = pl.BlockSpec((step, half), lambda j, i, flag: (i, column))
    return pl.pallas_call(
        functools.partial(adam_body, turned),
        grid_spec=pltpu.PrefetchScalarGridSpec(
            num_scalar_prefetch=1,
            grid=(2, count),
            in_specs=[mine] * 3 + [halves] * 2,
            out_specs=[mine] * 4,
        ),
        out_shape=[jax.ShapeDtypeStruct(weight.shape, f32)] * 4,
        compiler_params=params(2),
        cost_estimate=lasting(weight.size * 8e-6),
    )(flag, weight, first, second, own, other)


def row_mean(a, b):
    return jnp.mean(a * b, axis=1, keepdims=True)


def shards(tokens, cotangent, segment_ids, *state):
    masters, first_moments, second_moments = state[:11], state[11:22], state[22:33]
    inputs = tokens[0]
    docs_here = segment_ids[0]
    rows, width = inputs.shape
    ring = lax.axis_size(SHARD)
    teams = lax.axis_size(TENSOR)
    y = lax.axis_index(CX)
    piece = masters[0].shape[0]
    heads_here = masters[7].shape[0]
    head_piece = masters[7].shape[1]
    size = head_piece * ring * 2
    wide = heads_here * size // 2
    hidden = masters[4].shape[1] // 2
    block = rows // teams
    length = 2 * rows
    my_block = lax.axis_index(TC) * lax.axis_size(TX) + lax.axis_index(TX)

    def my_rows(value):
        return lax.dynamic_slice_in_dim(value, my_block * block, block, 0)

    docs_all = gather_axis(docs_here, CX)
    gains = jnp.concatenate([gain.astype(b16).reshape(-1) for gain in masters[7:]])[None]
    gains = gather_axis(gather_axis(gather_axis(gains, CX), SL), SH).astype(f32)
    gains, docs_all, inputs, *first = tie(gains, docs_all, inputs, *masters[:7])

    def columns_of(weight, index, count):
        return lax.dynamic_slice_in_dim(weight, index * count, count, 1).astype(b16)

    def over_ctx(weights, count):
        mine, theirs = [
            jnp.concatenate([columns_of(w, index, count) for w in weights], axis=1)
            for index in (y, 1 - y)
        ]
        return mine, swap(theirs, CX)

    def over_shard(value):
        return lax.all_gather(value, SHARD, axis=0, tiled=True)

    mine, theirs = over_ctx(first[:3] + [flip(first[3].astype(b16))], wide)
    theirs, local_rows = tie(theirs, my_rows(inputs))
    columns = pair(mine, theirs, CX)
    w_qkv, w_out = over_shard(columns[:, : 3 * wide]), columns[:, 3 * wide :]

    remote, gate_w, up_w, down_w = tie(swap(local_rows, CX), *first[4:])
    remote = gather_axis(remote, TX)
    gate_w = pair(*over_ctx([gate_w], hidden), CX)
    remote, gate_w = tie(remote, gate_w)
    remote = gather_axis(remote, TC)
    w_qkv, remote, w_out, gate_w = tie(w_qkv, remote, w_out, gate_w)
    w_out = over_shard(w_out)
    up_w = pair(*over_ctx([up_w], hidden), CX)
    down_w = pair(*over_ctx([flip(down_w.astype(b16))], hidden), CX)

    count = heads_here * head_piece
    head_gain = jnp.stack(
        [
            part(
                jnp.transpose(
                    gains[:, which * count : (which + 1) * count].reshape(
                        ring * 2, heads_here, head_piece
                    ),
                    (1, 0, 2),
                ).reshape(2, wide),
                y,
                0,
            )
            for which in range(2)
        ]
    )
    attn_gain = gains[:, 2 * count : 2 * count + piece].reshape(1, width)
    ffn_gain = gains[:, 2 * count + piece :].reshape(1, width)

    doc_range = jnp.arange(DOCS, dtype=i32)
    counts = jnp.sum((docs_all[:, None] == doc_range[None, :]).astype(i32), axis=0)
    starts = jnp.cumsum(counts) - counts
    own_start = jnp.sum(
        jnp.where(docs_all[:, None] == doc_range[None, :], starts[None, :], 0), axis=1
    )
    positions = jnp.arange(length, dtype=i32) - own_start
    frequencies = rope_base ** (-(jnp.arange(size // 2, dtype=f32) * 2.0) / size)
    angles = positions.astype(f32)[:, None] * frequencies[None, :]
    cosine, sine = jnp.cos(angles), jnp.sin(angles)
    cosine = jnp.concatenate([cosine, cosine], axis=1)
    sine = jnp.concatenate([-sine, sine], axis=1)

    raw, squares = project(y[None], inputs, remote, w_qkv)
    inverse = lax.rsqrt(plane_sum(squares) / width + norm_eps)
    query, key, val = prepare(raw, inverse, head_gain, cosine, sine)
    query, w_out, gate_w, up_w = tie(query, w_out, gate_w, up_w)
    w_both = over_shard(jnp.concatenate([gate_w, up_w], axis=1))
    spot = block_places(CX)
    attended, log_total = flash_forward(query, key, val, own_start, spot, block, size)
    group = length // 2
    branch = collect(
        across(dot(attended[:group], w_out, 1, 1), dot(attended[group:], w_out, 1, 1)), CX
    )
    branch_inv = lax.rsqrt(row_mean(branch, branch) + norm_eps)
    branch_unit = branch * branch_inv
    residual = my_rows(inputs).astype(f32) + branch_unit * attn_gain
    res, w_both, down_w = tie(residual.astype(b16), w_both, down_w)
    w_down = over_shard(down_w)
    res = spread(res, CX)

    res, gate_pre, up_pre, activated = zip(*[ffn_forward(blocks, w_both) for blocks in res])
    *activated, w_down = tie(*activated, w_down)
    ffn_out = collect(across(*[dot(a, w_down, 1, 1) for a in activated]), CX)
    ffn_inv = lax.rsqrt(row_mean(ffn_out, ffn_out) + norm_eps)
    ffn_unit = ffn_out * ffn_inv
    grad_out = my_rows(cotangent[0]).astype(f32)
    scaled_out = grad_out * ffn_gain
    d_ffn = joined(
        spread(
            (ffn_inv * (scaled_out - ffn_unit * row_mean(scaled_out, ffn_unit))).astype(b16), CX
        )
    )
    grad_ffn_gain = jnp.sum(grad_out * ffn_unit, axis=0)
    block_rows = (residual + ffn_unit * ffn_gain).astype(b16)

    def both(left, right):
        return (dot(left[0], right[0], 0, 0) + dot(left[1], right[1], 0, 0)).astype(b16)

    def to_shard(partial):
        return lax.psum_scatter(partial, SHARD, scatter_dimension=0, tiled=True)

    def to_owner(summed):
        summed = summed.reshape(2, piece, -1)
        return part(summed, y, 0), swap(part(summed, 1 - y, 0), CX)

    *d_ffn, block_rows = tie(*d_ffn, block_rows)
    block_rows = over_chips(block_rows)
    grad_down = both(d_ffn, activated)
    grad_down, *d_ffn = tie(grad_down, *d_ffn)
    grad_down = to_shard(grad_down)
    d_gate, d_up = zip(
        *[ffn_backward(d, w_down, g, u) for d, g, u in zip(d_ffn, gate_pre, up_pre)]
    )
    grad_gate = both(res, d_gate)
    grad_gate = to_shard(grad_gate)
    both_ffn = ffn_residual(
        d_gate[0], d_up[0], w_both, swap(ffn_residual(d_gate[1], d_up[1], w_both), TC)
    )
    both_ffn, grad_down, block_rows, *d_up = tie(both_ffn, grad_down, block_rows, *d_up)
    back_ffn = collect(both_ffn, CX)
    block_theirs = swap(block_rows, TC)
    grad_upward = both(res, d_up)
    grad_res = grad_out + back_ffn
    scaled_res = grad_res * attn_gain
    d_branch = (
        branch_inv * (scaled_res - branch_unit * row_mean(scaled_res, branch_unit))
    ).astype(b16)
    d_branch, grad_upward = tie(d_branch, grad_upward)
    grad_upward = to_shard(grad_upward)
    grad_attn_gain = jnp.sum(grad_res * branch_unit, axis=0)
    triple = lambda i: (masters[i], first_moments[i], second_moments[i])

    *d_branch, grad_gate, grad_down, block_theirs = tie(
        *joined(spread(d_branch, CX)), grad_gate, grad_down, block_theirs
    )
    down_halves, gate_halves = to_owner(grad_down), to_owner(grad_gate)
    d_att = jnp.concatenate([dot(d, w_out, 1, 0).astype(b16) for d in d_branch], 0)
    grad_out_w = both(d_branch, [attended[:group], attended[group:]])
    d_att, grad_out_w = tie(d_att, grad_out_w)
    d_query, d_key, d_val = flash_backward(
        query, key, val, own_start, log_total, d_att, attended, spot, block, size
    )
    grad_out_w = to_shard(grad_out_w)
    d_query, grad_upward, *turned = tie(d_query, grad_upward, *down_halves, *gate_halves)
    down_halves, gate_halves = turned[:2], turned[2:]
    sums, grad_heads = turned_sums(raw, inverse, head_gain, cosine, sine, d_query, d_key)
    plane_sums = plane_sum(
        jnp.concatenate([sums, grad_attn_gain[None], grad_ffn_gain[None]])
    )
    means = plane_sums[:2] / width
    small = jnp.concatenate([plane_sums[2:].reshape(1, -1), grad_heads.reshape(1, -1)], 1)
    small = sum_axis(sum_axis(small, SL), SH)
    means, grad_out_w, grad_upward = tie(means, grad_out_w, grad_upward)
    d_qkv, moved = raw_grads(
        raw, inverse, head_gain, cosine, sine, d_query, d_key, d_val, means, spot, block
    )

    sides = d_qkv.reshape(2, rows, 3 * wide)
    grad_qkv = both((inputs, remote), (part(sides, y, 0), part(sides, 1 - y, 0)))
    grad_qkv, moved = tie(grad_qkv, moved)
    grad_qkv = to_shard(grad_qkv)
    up_halves = to_owner(grad_upward)
    both_attn = across(dot(moved[:group], w_qkv, 1, 1), dot(moved[group:], w_qkv, 1, 1))
    both_attn, *up_halves = tie(both_attn, *up_halves)
    back_attn = collect(both_attn, CX)
    down_step = adam(*triple(6), *down_halves, y[None], turned=True)
    gate_step = adam(*triple(4), *gate_halves, y[None])
    up_step = adam(*triple(5), *up_halves, y[None])
    block_share = assemble(block_rows, block_theirs, block)
    back_attn, small, block_share, *turned = tie(
        back_attn, small, block_share, *down_step, *gate_step, *up_step
    )
    down_step, gate_step, up_step = turned[:4], turned[4:8], turned[8:]
    out_step = adam(*triple(3), *to_owner(grad_out_w), y[None], turned=True)
    grad_qkv = to_owner(grad_qkv)
    input_rows = over_chips((grad_res + back_attn).astype(b16))
    input_share = assemble(input_rows, swap(input_rows, TC), block)

    index = lax.axis_index(SHARD) * 2 + y
    wide_sums = lax.dynamic_slice_in_dim(
        small[0, : 2 * width].reshape(2, width), index * piece, piece, 1
    )
    head_sums = small[0, 2 * width :].reshape(2, 1, heads_here // 2, size)
    head_sums = pair(head_sums, swap(head_sums, CX), CX, 1).reshape(2, heads_here, size)
    head_sums = lax.dynamic_slice_in_dim(head_sums, index * head_piece, head_piece, 2)

    stepped = [adam(*triple(i), *grad_qkv, y[None], column=i) for i in range(3)]
    stepped += [out_step, gate_step, up_step, down_step]
    for i, grad in enumerate((head_sums[0], head_sums[1], wide_sums[0], wide_sums[1])):
        stepped.append((grad,) + adam_step(*triple(7 + i), grad))
    return tuple(
        [block_share, input_share]
        + [result[which] for which in range(4) for result in stepped]
    )


def solution(mesh):
    ring, ctx, teams = (mesh.shape[name] for name in mesh.axis_names)
    fine = Mesh(
        mesh.devices.reshape(ring // 2, 2, ctx, teams // 2, 2), (SH, SL, CX, TX, TC)
    )
    owners = (SH, SL, CX)
    column = P(owners, TENSOR)
    row = P(TENSOR, owners)
    vector = P(owners)
    act = P(SHARD, CX, None)
    weights = (column, column, column, row, column, column, row, row, row, vector, vector)
    return jax.shard_map(
        shards,
        mesh=fine,
        in_specs=(act, act, P(SHARD, CX)) + weights * 3,
        out_specs=(act, act) + weights * 4,
        check_vma=False,
    )
```

```python
import functools
import math

import jax
import jax.numpy as jnp
from jax import lax
from jax.experimental import pallas as pl
from jax.experimental.pallas import tpu as pltpu
from jax.sharding import Mesh
from jax.sharding import PartitionSpec as P

DOCS = 3
rope_base = 500000.0
norm_eps = 1e-06
learn_rate = 0.3
beta_one = 0.9
beta_two = 0.95
adam_eps = 1e-08
decay_rate = 0.1
step_count = 2
masked_score = -1e30

f32 = jnp.float32
b16 = jnp.bfloat16
i32 = jnp.int32

SH, SL, CX, TX, TC = "sh", "sl", "ctx", "tx", "tc"
SHARD = (SH, SL)
TENSOR = (TX, TC)
PLANE = (CX, TX, TC)


def dot(a, b, ca, cb):
    return lax.dot_general(a, b, (((ca,), (cb,)), ((), ())), preferred_element_type=f32)


def swap(value, axis):
    return lax.ppermute(value, axis, [(0, 1), (1, 0)])


def pair(mine, other, axis, at=0):
    return jnp.where(
        lax.axis_index(axis) == 0,
        jnp.concatenate([mine, other], at),
        jnp.concatenate([other, mine], at),
    )


def gather_axis(value, axis):
    if lax.axis_size(axis) == 2:
        return pair(value, swap(value, axis), axis)
    return lax.all_gather(value, axis, axis=0, tiled=True)


def sum_axis(value, axis):
    if lax.axis_size(axis) == 2:
        return value + swap(value, axis)
    return lax.psum(value, axis)


def plane_sum(value):
    return sum_axis(sum_axis(sum_axis(value, TC), TX), CX)


def tie(*values):
    return lax.optimization_barrier(values)


def part(value, index, at):
    return lax.dynamic_index_in_dim(value, index, at, keepdims=False)


def rows_all(value):
    return gather_axis(gather_axis(value, TX), TC)


def spread(value, axis):
    if lax.axis_size(TX) == 2:
        half = value.shape[0] // 2
        over_x = swap(value, TX)
        over_y = swap(value, axis)
        near = swap(over_y[:half], TX)
        far = swap(over_x[half:], axis)
        mine = [value, over_x, over_y, near, far]
    else:
        line = lax.all_gather(value, TX, axis=0, tiled=True)
        mine = [line, swap(line, axis)]
    return mine, [swap(block, TC) for block in mine]


def joined(groups):
    return [jnp.concatenate(blocks, 0) for blocks in groups]


def across(mine, theirs):
    return (mine + swap(theirs.astype(b16), TC).astype(f32)).astype(b16)


def collect(both, axis):
    count = lax.axis_size(TX)
    block = both.shape[0] // (2 * count)
    if count == 2:
        half = block // 2
        near = swap(both[3 * block : 3 * block + half], TX)
        far = swap(both[3 * block + half :], axis)
        over_x = jnp.concatenate(
            [both[block : block + half], both[block + half : 2 * block] + far], 0
        )
        over_y = jnp.concatenate(
            [both[2 * block : 2 * block + half] + near, both[2 * block + half : 3 * block]], 0
        )
        return (
            both[:block].astype(f32)
            + swap(over_x, TX).astype(f32)
            + swap(over_y, axis).astype(f32)
        )
    line = both[: count * block] + swap(both[count * block :], axis)
    return lax.psum_scatter(line, TX, scatter_dimension=0, tiled=True).astype(f32)


def block_places(axis):
    count = lax.axis_size(TX)
    spot = jnp.arange(4 * count, dtype=i32)
    side = (spot // (2 * count)) ^ lax.axis_index(axis)
    core = (spot // count % 2) ^ lax.axis_index(TC)
    along = spot % count
    if count == 2:
        along = along ^ lax.axis_index(TX)
    return (core * 2 + side) * count + along


def params(steps, mebibytes=30):
    return pltpu.CompilerParams(
        dimension_semantics=("arbitrary",) * steps, vmem_limit_bytes=mebibytes * 1024 * 1024
    )


def lasting(us):
    return pl.CostEstimate(flops=0, transcendentals=0, bytes_accessed=int(us * 0.5e6))


def upright(row, columns):
    return jnp.transpose(jnp.broadcast_to(row, (columns, row.shape[1])))


def row_sums(value):
    return jnp.sum(jnp.transpose(value), axis=0, keepdims=True)


def project_body(side, local, remote, weight, raw, squares):
    half = pl.num_programs(0) // 2
    mine = (pl.program_id(0) // half) == side[0]
    raw[...] = dot(jnp.where(mine, local[...], remote[...]), weight[...], 1, 0)
    width = raw.shape[1] // 3
    for which in range(2):
        total = jnp.zeros((raw.shape[0], 128), f32)
        for at in range(which * width, (which + 1) * width, 128):
            total += raw[:, at : at + 128] * raw[:, at : at + 128]
        squares[which : which + 1, :] = row_sums(total)


def project(side, local, remote, weight):
    rows, width = local.shape
    columns = weight.shape[1] // 4 * 3
    step = min(256, rows)
    half = rows // step
    tokens = pl.BlockSpec((step, width), lambda i, side: (i % half, 0))
    return pl.pallas_call(
        project_body,
        grid_spec=pltpu.PrefetchScalarGridSpec(
            num_scalar_prefetch=1,
            grid=(2 * half,),
            in_specs=[
                tokens,
                tokens,
                pl.BlockSpec((width, columns), lambda i, side: (0, 0)),
            ],
            out_specs=[
                pl.BlockSpec((step, columns), lambda i, side: (i, 0)),
                pl.BlockSpec((2, step), lambda i, side: (0, i)),
            ],
        ),
        out_shape=[
            jax.ShapeDtypeStruct((2 * rows, columns), f32),
            jax.ShapeDtypeStruct((2, 2 * rows), f32),
        ],
        compiler_params=params(1),
        cost_estimate=lasting(12),
    )(side, local, remote, weight)


def turn(value, cosine, sine):
    return value * cosine + pltpu.roll(value, value.shape[1] // 2, 1) * sine


def turn_back(value, cosine, sine):
    return value * cosine + pltpu.roll(value * sine, value.shape[1] // 2, 1)


def prepare_body(raw, inverse, gain, cosine, sine, query, key, val):
    width = query.shape[1]
    size = cosine.shape[1]
    for which, out in ((0, query), (1, key)):
        scale = upright(inverse[which : which + 1, :], size)
        for at in range(0, width, size):
            unit = raw[:, which * width + at : which * width + at + size] * scale
            out[:, at : at + size] = turn(
                unit * gain[which : which + 1, at : at + size], cosine[...], sine[...]
            ).astype(b16)
    val[...] = raw[:, 2 * width :].astype(b16)


def prepare(raw, inverse, gain, cosine, sine):
    rows, width = raw.shape[0], raw.shape[1] // 3
    size = cosine.shape[1]
    step = min(256, rows)
    by_row = lambda columns: pl.BlockSpec((step, columns), lambda i: (i, 0))
    return pl.pallas_call(
        prepare_body,
        grid=(rows // step,),
        in_specs=[
            by_row(3 * width),
            pl.BlockSpec((2, step), lambda i: (0, i)),
            pl.BlockSpec((2, width), lambda i: (0, 0)),
            by_row(size),
            by_row(size),
        ],
        out_specs=[by_row(width)] * 3,
        out_shape=[jax.ShapeDtypeStruct((rows, width), b16)] * 3,
        compiler_params=params(1),
        cost_estimate=lasting(3),
    )(raw, inverse, gain, cosine, sine)


def allowed(start, first_key, first_query, shape):
    keys = first_key + lax.broadcasted_iota(i32, shape, 0)
    queries = first_query + lax.broadcasted_iota(i32, shape, 1)
    return (keys >= start) & (keys <= queries)


def forward_body(span, size, spot, low, query, keys, values, start, out, log_total):
    i = pl.program_id(0)
    rows = query.shape[0]
    scale = 1.0 / math.sqrt(size)
    heads = [slice(at, at + size) for at in range(0, query.shape[1], size)]

    def step(j, carry):
        at = pl.multiple_of(j * span, span)
        here = pl.ds(at, span)
        mask = allowed(start[...], at, i * rows, (span, rows))
        after = []
        for head, (peak, total, summed) in zip(heads, carry):
            scores = dot(keys[here, head], query[:, head], 1, 1) * scale
            scores = jnp.where(mask, scores, masked_score)
            new_peak = jnp.maximum(peak, jnp.max(scores, axis=0, keepdims=True))
            shrink = jnp.exp(peak - new_peak)
            exponent = jnp.exp(scores - new_peak)
            total = total * shrink + jnp.sum(exponent, axis=0, keepdims=True)
            summed = summed * shrink + dot(values[here, head], exponent.astype(b16), 0, 0)
            after.append((new_peak, total, summed))
        return tuple(after)

    begin = (
        jnp.full((1, rows), masked_score, f32),
        jnp.zeros((1, rows), f32),
        jnp.zeros((size, rows), f32),
    )
    last = ((i + 1) * rows + span - 1) // span
    carry = lax.fori_loop(low[i], last, step, (begin,) * len(heads))
    for at, (head, (peak, total, summed)) in enumerate(zip(heads, carry)):
        out[:, head] = jnp.transpose(summed / total).astype(b16)
        log_total[at : at + 1, :] = peak + jnp.log(total)


def flash_forward(query, keys, values, start, spot, block, size):
    rows, width = query.shape
    heads = width // size
    blocks = rows // block
    span = min(512, rows)
    low = start.reshape(blocks, block)[:, 0] // span
    full = pl.BlockSpec((rows, width), lambda i, spot, low: (0, 0))
    return pl.pallas_call(
        functools.partial(forward_body, span, size),
        grid_spec=pltpu.PrefetchScalarGridSpec(
            num_scalar_prefetch=2,
            grid=(blocks,),
            in_specs=[
                pl.BlockSpec((block, width), lambda i, spot, low: (i, 0)),
                full,
                full,
                pl.BlockSpec((1, block), lambda i, spot, low: (0, i)),
            ],
            out_specs=[
                pl.BlockSpec((block, width), lambda i, spot, low: (spot[i], 0)),
                pl.BlockSpec((heads, block), lambda i, spot, low: (0, i)),
            ],
        ),
        out_shape=[
            jax.ShapeDtypeStruct((rows, width), b16),
            jax.ShapeDtypeStruct((heads, rows), f32),
        ],
        compiler_params=params(1),
        cost_estimate=lasting(18),
    )(spot, low, query, keys, values, start[None])


def backward_body(
    span,
    size,
    spot,
    low,
    query,
    keys,
    values,
    start,
    log_total,
    grad,
    out,
    d_query,
    d_keys,
    d_values,
):
    i = pl.program_id(0)
    rows = query.shape[0]
    scale = 1.0 / math.sqrt(size)
    heads = [slice(at, at + size) for at in range(0, query.shape[1], size)]

    @pl.when(i == 0)
    def _():
        d_keys[...] = jnp.zeros_like(d_keys)
        d_values[...] = jnp.zeros_like(d_values)

    deltas = [row_sums(grad[:, head].astype(f32) * out[:, head].astype(f32)) for head in heads]

    def step(j, carry):
        at = pl.multiple_of(j * span, span)
        here = pl.ds(at, span)
        mask = allowed(start[...], at, i * rows, (span, rows))
        after = []
        for which, (head, summed) in enumerate(zip(heads, carry)):
            scores = dot(keys[here, head], query[:, head], 1, 1) * scale
            soft = jnp.where(mask, jnp.exp(scores - log_total[which : which + 1, :]), 0.0)
            d_soft = dot(values[here, head], grad[:, head], 1, 1)
            d_scores = (soft * (d_soft - deltas[which]) * scale).astype(b16)
            d_values[here, head] += dot(soft.astype(b16), grad[:, head], 1, 0)
            d_keys[here, head] += dot(d_scores, query[:, head], 1, 0)
            after.append(summed + dot(keys[here, head], d_scores, 0, 0))
        return tuple(after)

    last = ((i + 1) * rows + span - 1) // span
    carry = lax.fori_loop(
        low[i], last, step, (jnp.zeros((size, rows), f32),) * len(heads)
    )
    for head, summed in zip(heads, carry):
        d_query[:, head] = jnp.transpose(summed)


def flash_backward(query, keys, values, start, log_total, grad, out, spot, block, size):
    rows, width = query.shape
    heads = width // size
    blocks = rows // block
    span = min(512, rows)
    low = start.reshape(blocks, block)[:, 0] // span
    natural = pl.BlockSpec((block, width), lambda i, spot, low: (i, 0))
    moved = pl.BlockSpec((block, width), lambda i, spot, low: (spot[i], 0))
    full = pl.BlockSpec((rows, width), lambda i, spot, low: (0, 0))
    return pl.pallas_call(
        functools.partial(backward_body, span, size),
        grid_spec=pltpu.PrefetchScalarGridSpec(
            num_scalar_prefetch=2,
            grid=(blocks,),
            in_specs=[
                natural,
                full,
                full,
                pl.BlockSpec((1, block), lambda i, spot, low: (0, i)),
                pl.BlockSpec((heads, block), lambda i, spot, low: (0, i)),
                moved,
                moved,
            ],
            out_specs=[natural, full, full],
        ),
        out_shape=[jax.ShapeDtypeStruct((rows, width), f32)] * 3,
        compiler_params=params(1),
        cost_estimate=lasting(22),
    )(spot, low, query, keys, values, start[None], log_total, grad, out)


def turned_sums_body(raw, inverse, gain, cosine, sine, d_query, d_key, sums, gains):
    width = d_query.shape[1]
    size = cosine.shape[1]

    @pl.when(pl.program_id(0) == 0)
    def _():
        gains[...] = jnp.zeros_like(gains)

    for which, grad in ((0, d_query), (1, d_key)):
        row = jnp.zeros((raw.shape[0], size), f32)
        scale = upright(inverse[which : which + 1, :], size)
        for at in range(0, width, size):
            unit = raw[:, which * width + at : which * width + at + size] * scale
            product = turn_back(grad[:, at : at + size], cosine[...], sine[...]) * unit
            gains[which : which + 1, at : at + size] += jnp.sum(product, axis=0, keepdims=True)
            row += product * gain[which : which + 1, at : at + size]
        sums[which : which + 1, :] = row_sums(row)


def turned_sums(raw, inverse, gain, cosine, sine, d_query, d_key):
    rows, width = d_query.shape
    size = cosine.shape[1]
    step = min(256, rows)
    by_row = lambda columns: pl.BlockSpec((step, columns), lambda i: (i, 0))
    return pl.pallas_call(
        turned_sums_body,
        grid=(rows // step,),
        in_specs=[
            by_row(3 * width),
            pl.BlockSpec((2, step), lambda i: (0, i)),
            pl.BlockSpec((2, width), lambda i: (0, 0)),
            by_row(size),
            by_row(size),
            by_row(width),
            by_row(width),
        ],
        out_specs=[
            pl.BlockSpec((2, step), lambda i: (0, i)),
            pl.BlockSpec((2, width), lambda i: (0, 0)),
        ],
        out_shape=[
            jax.ShapeDtypeStruct((2, rows), f32),
            jax.ShapeDtypeStruct((2, width), f32),
        ],
        compiler_params=params(1),
        cost_estimate=lasting(4),
    )(raw, inverse, gain, cosine, sine, d_query, d_key)


def raw_grads_body(
    spot, raw, inverse, gain, cosine, sine, d_query, d_key, d_val, means, out, moved
):
    width = d_query.shape[1]
    size = cosine.shape[1]
    for which, grad in ((0, d_query), (1, d_key)):
        scale = upright(inverse[which : which + 1, :], size)
        mean = upright(means[which : which + 1, :], size)
        for at in range(0, width, size):
            place = slice(which * width + at, which * width + at + size)
            unit = raw[:, place] * scale
            scaled = (
                turn_back(grad[:, at : at + size], cosine[...], sine[...])
                * gain[which : which + 1, at : at + size]
            )
            out[:, place] = (scale * (scaled - unit * mean)).astype(b16)
    out[:, 2 * width :] = d_val[...].astype(b16)
    moved[...] = out[...]


def raw_grads(raw, inverse, gain, cosine, sine, d_query, d_key, d_val, means, spot, block):
    rows, width = d_query.shape
    size = cosine.shape[1]
    by_row = lambda columns: pl.BlockSpec((block, columns), lambda i, spot: (i, 0))
    in_line = pl.BlockSpec((2, block), lambda i, spot: (0, i))
    return pl.pallas_call(
        raw_grads_body,
        grid_spec=pltpu.PrefetchScalarGridSpec(
            num_scalar_prefetch=1,
            grid=(rows // block,),
            in_specs=[
                by_row(3 * width),
                in_line,
                pl.BlockSpec((2, width), lambda i, spot: (0, 0)),
                by_row(size),
                by_row(size),
                by_row(width),
                by_row(width),
                by_row(width),
                in_line,
            ],
            out_specs=[
                by_row(3 * width),
                pl.BlockSpec((block, 3 * width), lambda i, spot: (spot[i], 0)),
            ],
        ),
        out_shape=[jax.ShapeDtypeStruct((rows, 3 * width), b16)] * 2,
        compiler_params=params(1),
        cost_estimate=lasting(5),
    )(spot, raw, inverse, gain, cosine, sine, d_query, d_key, d_val, means)


def ffn_forward_body(count, *refs):
    blocks, (w_gate, w_up, full, gate, up, act) = refs[:count], refs[count:]

    @pl.when(pl.program_id(0) == 0)
    def _():
        at = 0
        for block in blocks:
            full[at : at + block.shape[0], :] = block[...]
            at += block.shape[0]

    gate_pre = dot(full[...], w_gate[...], 1, 0)
    up_pre = dot(full[...], w_up[...], 1, 0)
    gate[...] = gate_pre.astype(b16)
    up[...] = up_pre.astype(b16)
    act[...] = (gate_pre * jax.nn.sigmoid(gate_pre) * up_pre).astype(b16)


def ffn_forward(blocks, w_both):
    rows = sum(block.shape[0] for block in blocks)
    width, columns = w_both.shape
    step = min(256, columns // 2)
    count = columns // 2 // step
    out = pl.BlockSpec((rows, step), lambda j: (0, j))
    hidden = jax.ShapeDtypeStruct((rows, columns // 2), b16)
    return pl.pallas_call(
        functools.partial(ffn_forward_body, len(blocks)),
        grid=(count,),
        in_specs=[pl.BlockSpec(block.shape, lambda j: (0, 0)) for block in blocks]
        + [
            pl.BlockSpec((width, step), lambda j: (0, j)),
            pl.BlockSpec((width, step), lambda j: (0, j + count)),
        ],
        out_specs=[pl.BlockSpec((rows, width), lambda j: (0, 0)), out, out, out],
        out_shape=[jax.ShapeDtypeStruct((rows, width), b16), hidden, hidden, hidden],
        compiler_params=params(1),
        cost_estimate=lasting(10),
    )(*blocks, w_both, w_both)


def ffn_backward_body(grad, w_down, gate, up, d_gate, d_up):
    d_act = dot(grad[...], w_down[...], 1, 0)
    gate_pre, up_pre = gate[...].astype(f32), up[...].astype(f32)
    sigmoid = jax.nn.sigmoid(gate_pre)
    d_gate[...] = (d_act * up_pre * sigmoid * (1.0 + gate_pre * (1.0 - sigmoid))).astype(b16)
    d_up[...] = (d_act * gate_pre * sigmoid).astype(b16)


def ffn_backward(grad, w_down, gate, up):
    rows, width = grad.shape
    columns = w_down.shape[1]
    step = min(256, columns)
    out = pl.BlockSpec((rows, step), lambda j: (0, j))
    return pl.pallas_call(
        ffn_backward_body,
        grid=(columns // step,),
        in_specs=[
            pl.BlockSpec((rows, width), lambda j: (0, 0)),
            pl.BlockSpec((width, step), lambda j: (0, j)),
            out,
            out,
        ],
        out_specs=[out, out],
        out_shape=[jax.ShapeDtypeStruct((rows, columns), b16)] * 2,
        compiler_params=params(1),
        cost_estimate=lasting(6),
    )(grad, w_down, gate, up)


def ffn_residual_body(d_gate, d_up, w_gate, w_up, *rest):
    value = dot(d_gate[...], w_gate[...], 1, 1) + dot(d_up[...], w_up[...], 1, 1)
    if len(rest) == 2:
        value += rest[0][...].astype(f32)
    rest[-1][...] = value.astype(b16)


def ffn_residual(d_gate, d_up, w_both, *received):
    rows, columns = d_gate.shape
    width = w_both.shape[0]
    step = min(256, width)
    full = pl.BlockSpec((rows, columns), lambda j: (0, 0))
    out = pl.BlockSpec((rows, step), lambda j: (0, j))
    return pl.pallas_call(
        ffn_residual_body,
        grid=(width // step,),
        in_specs=[
            full,
            full,
            pl.BlockSpec((step, columns), lambda j: (j, 0)),
            pl.BlockSpec((step, columns), lambda j: (j, 1)),
        ]
        + [out] * len(received),
        out_specs=out,
        out_shape=jax.ShapeDtypeStruct((rows, width), b16),
        compiler_params=params(1),
        cost_estimate=lasting(9),
    )(d_gate, d_up, w_both, w_both, *received)


def columns_body(side, query, key, val, out_weight, out):
    width = query.shape[1]
    for at, piece in enumerate((query, key, val)):
        out[:, at * width : (at + 1) * width] = piece[...].astype(b16)
    out[:, 3 * width :] = jnp.transpose(out_weight[...]).astype(b16)


def attention_columns(side, query, key, val, out_weight):
    piece, width = query.shape[0], query.shape[1] // 2
    upper = pl.BlockSpec((piece, width), lambda i, side: (0, side[0]))
    return pl.pallas_call(
        columns_body,
        grid_spec=pltpu.PrefetchScalarGridSpec(
            num_scalar_prefetch=1,
            grid=(1,),
            in_specs=[
                upper,
                upper,
                upper,
                pl.BlockSpec((width, piece), lambda i, side: (side[0], 0)),
            ],
            out_specs=pl.BlockSpec((piece, 4 * width), lambda i, side: (0, 0)),
        ),
        out_shape=jax.ShapeDtypeStruct((piece, 4 * width), b16),
        compiler_params=params(1, 60),
        cost_estimate=lasting(2),
    )(side, query, key, val, out_weight)


def paired_columns_body(side, query, key, val, out_weight, other, out):
    @pl.when(pl.program_id(0) == side[0])
    def _():
        columns_body(side, query, key, val, out_weight, out)

    @pl.when(pl.program_id(0) != side[0])
    def _():
        out[...] = other[...]


def paired_columns(side, query, key, val, out_weight, other):
    piece, width = query.shape[0], query.shape[1] // 2
    upper = pl.BlockSpec((piece, width), lambda i, side: (0, side[0]))
    return pl.pallas_call(
        paired_columns_body,
        grid_spec=pltpu.PrefetchScalarGridSpec(
            num_scalar_prefetch=1,
            grid=(2,),
            in_specs=[
                upper,
                upper,
                upper,
                pl.BlockSpec((width, piece), lambda i, side: (side[0], 0)),
                pl.BlockSpec((piece, 4 * width), lambda i, side: (0, 0)),
            ],
            out_specs=pl.BlockSpec((piece, 4 * width), lambda i, side: (i, 0)),
        ),
        out_shape=jax.ShapeDtypeStruct((2 * piece, 4 * width), b16),
        compiler_params=params(1, 60),
        cost_estimate=lasting(2),
    )(side, query, key, val, out_weight, other)


def flip_body(value, out):
    out[...] = jnp.transpose(value[...])


def flip(value):
    rows, columns = value.shape
    step = min(256, columns)
    return pl.pallas_call(
        flip_body,
        grid=(columns // step,),
        in_specs=[pl.BlockSpec((rows, step), lambda i: (0, i))],
        out_specs=pl.BlockSpec((step, rows), lambda i: (i, 0)),
        out_shape=jax.ShapeDtypeStruct((columns, rows), value.dtype),
        compiler_params=params(1),
    )(value)


def adam_step(weight, first_moment, second_moment, gradient):
    new_first = beta_one * first_moment + (1.0 - beta_one) * gradient
    new_second = beta_two * second_moment + (1.0 - beta_two) * gradient * gradient
    first_hat = new_first / (1.0 - beta_one**step_count)
    second_hat = new_second / (1.0 - beta_two**step_count)
    updated = weight - learn_rate * (
        first_hat / (jnp.sqrt(second_hat) + adam_eps) + decay_rate * weight
    )
    return (updated, new_first, new_second)


def assemble_body(flags, mine, theirs, out):
    own = (pl.program_id(0) // flags[1]) == flags[0]
    out[0] = jnp.where(own, mine[...], theirs[...]).astype(f32)


def assemble(mine, theirs, block):
    count = lax.axis_size(TX)
    width = mine.shape[1]
    shift = lax.axis_index(TX) if count == 2 else jnp.zeros((), i32)
    flags = jnp.stack([lax.axis_index(TC), jnp.full((), count, i32), shift])
    here = pl.BlockSpec((block, width), lambda i, flags: ((i % count) ^ flags[2], 0))
    return pl.pallas_call(
        assemble_body,
        grid_spec=pltpu.PrefetchScalarGridSpec(
            num_scalar_prefetch=1,
            grid=(2 * count,),
            in_specs=[here, here],
            out_specs=pl.BlockSpec((1, block, width), lambda i, flags: (0, i, 0)),
        ),
        out_shape=jax.ShapeDtypeStruct((1, 2 * count * block, width), f32),
        compiler_params=params(1),
        cost_estimate=lasting(5),
    )(flags, mine, theirs)


def over_chips(value):
    if lax.axis_size(TX) == 2:
        return jnp.concatenate([value, swap(value, TX)], 0)
    return lax.all_gather(value, TX, axis=0, tiled=True)


def adam_body(turned, flag, weight, first, second, own, other, grad, updated, mean, square):
    value = jnp.where(pl.program_id(0) == flag[0], own[...].astype(f32), other[...].astype(f32))
    if turned:
        value = jnp.transpose(value)
    grad[...] = value
    updated[...], mean[...], square[...] = adam_step(
        weight[...], first[...], second[...], value
    )


def adam(weight, first, second, own, other, flag, turned=False, column=0):
    rows, columns = weight.shape
    if turned:
        half = rows // 2
        step = min(256, half)
        count = half // step
        mine = pl.BlockSpec((step, columns), lambda j, i, flag: (j * count + i, 0))
        halves = pl.BlockSpec((columns, step), lambda j, i, flag: (0, column * count + i))
        both = pl.BlockSpec(
            (None, columns, step), lambda j, i, flag: (flag[0], 0, column * count + i)
        )
    else:
        half = columns // 2
        step = min(128, rows)
        count = rows // step
        mine = pl.BlockSpec((step, half), lambda j, i, flag: (i, j))
        halves = pl.BlockSpec((step, half), lambda j, i, flag: (i, column))
        both = pl.BlockSpec((None, step, half), lambda j, i, flag: (flag[0], i, column))
    return pl.pallas_call(
        functools.partial(adam_body, turned),
        grid_spec=pltpu.PrefetchScalarGridSpec(
            num_scalar_prefetch=1,
            grid=(2, count),
            in_specs=[mine] * 3 + [both, halves],
            out_specs=[mine] * 4,
        ),
        out_shape=[jax.ShapeDtypeStruct(weight.shape, f32)] * 4,
        compiler_params=params(2),
        cost_estimate=lasting(weight.size * 8e-6),
    )(flag, weight, first, second, own, other)


def row_mean(a, b):
    return jnp.mean(a * b, axis=1, keepdims=True)


def shards(tokens, cotangent, segment_ids, *state):
    masters, first_moments, second_moments = state[:11], state[11:22], state[22:33]
    inputs = tokens[0]
    docs_here = segment_ids[0]
    rows, width = inputs.shape
    ring = lax.axis_size(SHARD)
    teams = lax.axis_size(TENSOR)
    y = lax.axis_index(CX)
    piece = masters[0].shape[0]
    heads_here = masters[7].shape[0]
    head_piece = masters[7].shape[1]
    size = head_piece * ring * 2
    wide = heads_here * size // 2
    hidden = masters[4].shape[1] // 2
    block = rows // teams
    length = 2 * rows
    my_block = lax.axis_index(TC) * lax.axis_size(TX) + lax.axis_index(TX)

    def my_rows(value):
        return lax.dynamic_slice_in_dim(value, my_block * block, block, 0)

    docs_all = gather_axis(docs_here, CX)
    gains = jnp.concatenate([gain.astype(b16).reshape(-1) for gain in masters[7:]])[None]
    gains = gather_axis(gather_axis(gather_axis(gains, CX), SL), SH).astype(f32)
    first = list(masters[:7])

    def columns_of(weight, index, count):
        return lax.dynamic_slice_in_dim(weight, index * count, count, 1).astype(b16)

    def over_ctx(weights, count):
        mine, theirs = [
            jnp.concatenate([columns_of(w, index, count) for w in weights], axis=1)
            for index in (y, 1 - y)
        ]
        return mine, swap(theirs, CX)

    def over_shard(value):
        return lax.all_gather(value, SHARD, axis=0, tiled=True)

    theirs = swap(attention_columns(1 - y[None], *first[:4]), CX)
    theirs, local_rows, gains, docs_all = tie(theirs, my_rows(inputs), gains, docs_all)
    w_attn = over_shard(paired_columns(y[None], *first[:4], theirs))

    remote, gate_w, up_w, down_w = tie(swap(local_rows, CX), *first[4:])
    remote = gather_axis(remote, TX)
    gate_w = pair(*over_ctx([gate_w], hidden), CX)
    remote, gate_w = tie(remote, gate_w)
    remote = gather_axis(remote, TC)
    up_w = pair(*over_ctx([up_w], hidden), CX)
    w_attn, remote, w_both = tie(w_attn, remote, jnp.concatenate([gate_w, up_w], axis=1))
    w_both = over_shard(w_both)
    w_qkv, w_out = w_attn[:, : 3 * wide], w_attn[:, 3 * wide :]
    down_w = pair(*over_ctx([flip(down_w.astype(b16))], hidden), CX)

    count = heads_here * head_piece
    head_gain = jnp.stack(
        [
            part(
                jnp.transpose(
                    gains[:, which * count : (which + 1) * count].reshape(
                        ring * 2, heads_here, head_piece
                    ),
                    (1, 0, 2),
                ).reshape(2, wide),
                y,
                0,
            )
            for which in range(2)
        ]
    )
    attn_gain = gains[:, 2 * count : 2 * count + piece].reshape(1, width)
    ffn_gain = gains[:, 2 * count + piece :].reshape(1, width)

    doc_range = jnp.arange(DOCS, dtype=i32)
    counts = jnp.sum((docs_all[:, None] == doc_range[None, :]).astype(i32), axis=0)
    starts = jnp.cumsum(counts) - counts
    own_start = jnp.sum(
        jnp.where(docs_all[:, None] == doc_range[None, :], starts[None, :], 0), axis=1
    )
    positions = jnp.arange(length, dtype=i32) - own_start
    frequencies = rope_base ** (-(jnp.arange(size // 2, dtype=f32) * 2.0) / size)
    angles = positions.astype(f32)[:, None] * frequencies[None, :]
    cosine, sine = jnp.cos(angles), jnp.sin(angles)
    cosine = jnp.concatenate([cosine, cosine], axis=1)
    sine = jnp.concatenate([-sine, sine], axis=1)

    raw, squares = project(y[None], inputs, remote, w_attn)
    inverse = lax.rsqrt(plane_sum(squares) / width + norm_eps)
    query, key, val = prepare(raw, inverse, head_gain, cosine, sine)
    query, down_w = tie(query, down_w)
    spot = block_places(CX)
    attended, log_total = flash_forward(query, key, val, own_start, spot, block, size)
    group = length // 2
    branch = collect(
        across(dot(attended[:group], w_out, 1, 1), dot(attended[group:], w_out, 1, 1)), CX
    )
    branch_inv = lax.rsqrt(row_mean(branch, branch) + norm_eps)
    branch_unit = branch * branch_inv
    residual = my_rows(inputs).astype(f32) + branch_unit * attn_gain
    res, w_both, down_w = tie(residual.astype(b16), w_both, down_w)
    w_down = over_shard(down_w)
    res = spread(res, CX)

    res, gate_pre, up_pre, activated = zip(*[ffn_forward(blocks, w_both) for blocks in res])
    *activated, w_down = tie(*activated, w_down)
    ffn_out = collect(across(*[dot(a, w_down, 1, 1) for a in activated]), CX)
    ffn_inv = lax.rsqrt(row_mean(ffn_out, ffn_out) + norm_eps)
    ffn_unit = ffn_out * ffn_inv
    grad_out = my_rows(cotangent[0]).astype(f32)
    scaled_out = grad_out * ffn_gain
    d_ffn = joined(
        spread(
            (ffn_inv * (scaled_out - ffn_unit * row_mean(scaled_out, ffn_unit))).astype(b16), CX
        )
    )
    grad_ffn_gain = jnp.sum(grad_out * ffn_unit, axis=0)
    block_rows = (residual + ffn_unit * ffn_gain).astype(b16)

    def both(left, right):
        return (dot(left[0], right[0], 0, 0) + dot(left[1], right[1], 0, 0)).astype(b16)

    def to_shard(partial):
        return lax.psum_scatter(partial, SHARD, scatter_dimension=0, tiled=True)

    def to_owner(summed):
        summed = summed.reshape(2, piece, -1)
        return summed, swap(part(summed, 1 - y, 0), CX)

    *d_ffn, block_rows = tie(*d_ffn, block_rows)
    block_rows = over_chips(block_rows)
    grad_down = both(d_ffn, activated)
    grad_down, *d_ffn = tie(grad_down, *d_ffn)
    grad_down = to_shard(grad_down)
    d_gate, d_up = zip(
        *[ffn_backward(d, w_down, g, u) for d, g, u in zip(d_ffn, gate_pre, up_pre)]
    )
    block_rows, *turned = tie(block_rows, *d_gate, *d_up)
    d_gate, d_up = turned[:2], turned[2:]
    theirs, *turned = tie(ffn_residual(d_gate[1], d_up[1], w_both), *d_gate)
    d_gate = turned
    grad_gate = dot(res[0], d_gate[0], 0, 0)
    theirs, grad_gate = tie(swap(theirs, TC), grad_gate)
    both_ffn = ffn_residual(d_gate[0], d_up[0], w_both, theirs)
    both_ffn, *turned = tie(both_ffn, *d_gate, *d_up)
    d_gate, d_up = turned[:2], turned[2:]
    grad_gate = (grad_gate + dot(res[1], d_gate[1], 0, 0)).astype(b16)
    grad_gate = to_shard(grad_gate)
    back_ffn = collect(both_ffn, CX)
    block_theirs = swap(block_rows, TC)
    grad_upward = both(res, d_up)
    grad_res = grad_out + back_ffn
    scaled_res = grad_res * attn_gain
    d_branch = (
        branch_inv * (scaled_res - branch_unit * row_mean(scaled_res, branch_unit))
    ).astype(b16)
    d_branch, grad_upward = tie(d_branch, grad_upward)
    grad_upward = to_shard(grad_upward)
    grad_attn_gain = jnp.sum(grad_res * branch_unit, axis=0)
    triple = lambda i: (masters[i], first_moments[i], second_moments[i])

    *d_branch, grad_gate, grad_down, block_theirs = tie(
        *joined(spread(d_branch, CX)), grad_gate, grad_down, block_theirs
    )
    down_halves, gate_halves = to_owner(grad_down), to_owner(grad_gate)
    d_att = jnp.concatenate([dot(d, w_out, 1, 0).astype(b16) for d in d_branch], 0)
    d_query, d_key, d_val = flash_backward(
        query, key, val, own_start, log_total, d_att, attended, spot, block, size
    )
    d_query, *turned = tie(d_query, *d_branch, *down_halves, *gate_halves)
    d_branch, down_halves, gate_halves = turned[:2], turned[2:4], turned[4:]
    grad_out_w = both(d_branch, [attended[:group], attended[group:]])
    d_query, grad_out_w = tie(d_query, grad_out_w)
    sums, grad_heads = turned_sums(raw, inverse, head_gain, cosine, sine, d_query, d_key)
    plane_sums = plane_sum(
        jnp.concatenate([sums, grad_attn_gain[None], grad_ffn_gain[None]])
    )
    means = plane_sums[:2] / width
    small = jnp.concatenate([plane_sums[2:].reshape(1, -1), grad_heads.reshape(1, -1)], 1)
    small = sum_axis(sum_axis(small, SL), SH)
    d_qkv, moved = raw_grads(
        raw, inverse, head_gain, cosine, sine, d_query, d_key, d_val, means, spot, block
    )

    sides = d_qkv.reshape(2, rows, 3 * wide)
    grad_qkv = both((inputs, remote), (part(sides, y, 0), part(sides, 1 - y, 0)))
    grad_attn = to_shard(jnp.concatenate([grad_qkv, grad_out_w], axis=1))
    both_attn = across(dot(moved[:group], w_qkv, 1, 1), dot(moved[group:], w_qkv, 1, 1))
    both_attn, grad_upward = tie(both_attn, grad_upward)
    back_attn = collect(both_attn, CX)
    down_step = adam(*triple(6), *down_halves, y[None], turned=True)
    gate_step = adam(*triple(4), *gate_halves, y[None])
    block_share = assemble(block_rows, block_theirs, block)
    back_attn, small, grad_upward, *turned = tie(
        back_attn, small, grad_upward, *down_step, *gate_step
    )
    down_step, gate_step = turned[:4], turned[4:]
    input_rows = over_chips((grad_res + back_attn).astype(b16))
    up_step = adam(*triple(5), *to_owner(grad_upward), y[None])
    input_rows, grad_attn, block_share, *up_step = tie(
        input_rows, grad_attn, block_share, *up_step
    )
    attn_halves = to_owner(grad_attn)
    input_share = assemble(input_rows, swap(input_rows, TC), block)
    input_share, *attn_halves = tie(input_share, *attn_halves)

    index = lax.axis_index(SHARD) * 2 + y
    wide_sums = lax.dynamic_slice_in_dim(
        small[0, : 2 * width].reshape(2, width), index * piece, piece, 1
    )
    head_sums = small[0, 2 * width :].reshape(2, 1, heads_here // 2, size)
    head_sums = pair(head_sums, swap(head_sums, CX), CX, 1).reshape(2, heads_here, size)
    head_sums = lax.dynamic_slice_in_dim(head_sums, index * head_piece, head_piece, 2)

    stepped = [adam(*triple(i), *attn_halves, y[None], i == 3, i) for i in range(4)]
    stepped += [gate_step, up_step, down_step]
    for i, grad in enumerate((head_sums[0], head_sums[1], wide_sums[0], wide_sums[1])):
        stepped.append((grad,) + adam_step(*triple(7 + i), grad))
    return tuple(
        [block_share, input_share]
        + [result[which] for which in range(4) for result in stepped]
    )


def solution(mesh):
    ring, ctx, teams = (mesh.shape[name] for name in mesh.axis_names)
    fine = Mesh(
        mesh.devices.reshape(ring // 2, 2, ctx, teams // 2, 2), (SH, SL, CX, TX, TC)
    )
    owners = (SH, SL, CX)
    column = P(owners, TENSOR)
    row = P(TENSOR, owners)
    vector = P(owners)
    act = P(SHARD, CX, None)
    weights = (column, column, column, row, column, column, row, row, row, vector, vector)
    return jax.shard_map(
        shards,
        mesh=fine,
        in_specs=(act, act, P(SHARD, CX)) + weights * 3,
        out_specs=(act, act) + weights * 4,
        check_vma=False,
    )
```

```python
import functools
import math

import jax
import jax.numpy as jnp
from jax import lax
from jax.experimental import pallas as pl
from jax.experimental.pallas import tpu as pltpu
from jax.sharding import Mesh
from jax.sharding import PartitionSpec as P

DOCS = 3
rope_base = 500000.0
norm_eps = 1e-06
learn_rate = 0.3
beta_one = 0.9
beta_two = 0.95
adam_eps = 1e-08
decay_rate = 0.1
step_count = 2
masked_score = -1e30

f32 = jnp.float32
b16 = jnp.bfloat16
i32 = jnp.int32

SH, SL, CX, TX, TC = "sh", "sl", "ctx", "tx", "tc"
SHARD = (SH, SL)
TENSOR = (TX, TC)
PLANE = (CX, TX, TC)


def dot(a, b, ca, cb):
    return lax.dot_general(a, b, (((ca,), (cb,)), ((), ())), preferred_element_type=f32)


def swap(value, axis):
    return lax.ppermute(value, axis, [(0, 1), (1, 0)])


def pair(mine, other, axis, at=0):
    return jnp.where(
        lax.axis_index(axis) == 0,
        jnp.concatenate([mine, other], at),
        jnp.concatenate([other, mine], at),
    )


def gather_axis(value, axis):
    if lax.axis_size(axis) == 2:
        return pair(value, swap(value, axis), axis)
    return lax.all_gather(value, axis, axis=0, tiled=True)


def sum_axis(value, axis):
    if lax.axis_size(axis) == 2:
        return value + swap(value, axis)
    return lax.psum(value, axis)


def plane_sum(value):
    return sum_axis(sum_axis(sum_axis(value, TC), TX), CX)


def tie(*values):
    return lax.optimization_barrier(values)


def part(value, index, at):
    return lax.dynamic_index_in_dim(value, index, at, keepdims=False)


def rows_all(value):
    return gather_axis(gather_axis(value, TX), TC)


def spread(value, axis):
    if lax.axis_size(TX) == 2:
        half = value.shape[0] // 2
        over_x = swap(value, TX)
        over_y = swap(value, axis)
        over_x, over_y = tie(over_x, over_y)
        near, far = tie(swap(over_y[:half], TX), swap(over_x[half:], axis))
        mine = [value, over_x, over_y, near, far]
    else:
        line = lax.all_gather(value, TX, axis=0, tiled=True)
        mine = [line, swap(line, axis)]
    return mine, [swap(block, TC) for block in mine]


def joined(groups):
    return [jnp.concatenate(blocks, 0) for blocks in groups]


def joined_halves(groups):
    if len(groups[0]) != 5:
        return joined(groups)
    out = []
    for first, second, third, near, far in groups:
        half = near.shape[0]
        upper = [block[:half] for block in (first, second, third)] + [near]
        lower = [block[half:] for block in (first, second, third)] + [far]
        out.append(jnp.concatenate(upper + lower, 0))
    return out


def across(mine, theirs):
    return (mine + swap(theirs.astype(b16), TC).astype(f32)).astype(b16)


def collect(both, axis):
    count = lax.axis_size(TX)
    block = both.shape[0] // (2 * count)
    if count == 2:
        half = block // 2
        near = swap(both[3 * block : 3 * block + half], TX)
        far = swap(both[3 * block + half :], axis)
        over_x = jnp.concatenate(
            [both[block : block + half], both[block + half : 2 * block] + far], 0
        )
        over_y = jnp.concatenate(
            [both[2 * block : 2 * block + half] + near, both[2 * block + half : 3 * block]], 0
        )
        return (
            both[:block].astype(f32)
            + swap(over_x, TX).astype(f32)
            + swap(over_y, axis).astype(f32)
        )
    line = both[: count * block] + swap(both[count * block :], axis)
    return lax.psum_scatter(line, TX, scatter_dimension=0, tiled=True).astype(f32)


def collect_halves(both, axis, *later):
    if lax.axis_size(TX) != 2:
        return (collect(both, axis), *later)
    h = both.shape[0] // 8
    near, far, *later = tie(swap(both[3 * h : 4 * h], TX), swap(both[7 * h :], axis), *later)
    over_x = jnp.concatenate([both[h : 2 * h], both[5 * h : 6 * h] + far], 0)
    over_y = jnp.concatenate([both[2 * h : 3 * h] + near, both[6 * h : 7 * h]], 0)
    total = (
        jnp.concatenate([both[:h], both[4 * h : 5 * h]], 0).astype(f32)
        + swap(over_x, TX).astype(f32)
        + swap(over_y, axis).astype(f32)
    )
    return (total, *later)


def block_places(axis):
    count = lax.axis_size(TX)
    spot = jnp.arange(4 * count, dtype=i32)
    side = (spot // (2 * count)) ^ lax.axis_index(axis)
    core = (spot // count % 2) ^ lax.axis_index(TC)
    along = spot % count
    if count == 2:
        along = along ^ lax.axis_index(TX)
    return (core * 2 + side) * count + along


def params(steps, mebibytes=30):
    return pltpu.CompilerParams(
        dimension_semantics=("arbitrary",) * steps, vmem_limit_bytes=mebibytes * 1024 * 1024
    )


def lasting(us):
    return pl.CostEstimate(flops=0, transcendentals=0, bytes_accessed=int(us * 0.5e6))


def upright(row, columns):
    return jnp.transpose(jnp.broadcast_to(row, (columns, row.shape[1])))


def row_sums(value):
    return jnp.sum(jnp.transpose(value), axis=0, keepdims=True)


def project_body(side, local, remote, weight, raw, squares):
    half = pl.num_programs(0) // 2
    mine = (pl.program_id(0) // half) == side[0]
    raw[...] = dot(jnp.where(mine, local[...], remote[...]), weight[...], 1, 0)
    width = raw.shape[1] // 3
    for which in range(2):
        total = jnp.zeros((raw.shape[0], 128), f32)
        for at in range(which * width, (which + 1) * width, 128):
            total += raw[:, at : at + 128] * raw[:, at : at + 128]
        squares[which : which + 1, :] = row_sums(total)


def project(side, local, remote, weight):
    rows, width = local.shape
    columns = weight.shape[1] // 4 * 3
    step = min(256, rows)
    half = rows // step
    tokens = pl.BlockSpec((step, width), lambda i, side: (i % half, 0))
    return pl.pallas_call(
        project_body,
        grid_spec=pltpu.PrefetchScalarGridSpec(
            num_scalar_prefetch=1,
            grid=(2 * half,),
            in_specs=[
                tokens,
                tokens,
                pl.BlockSpec((width, columns), lambda i, side: (0, 0)),
            ],
            out_specs=[
                pl.BlockSpec((step, columns), lambda i, side: (i, 0)),
                pl.BlockSpec((2, step), lambda i, side: (0, i)),
            ],
        ),
        out_shape=[
            jax.ShapeDtypeStruct((2 * rows, columns), f32),
            jax.ShapeDtypeStruct((2, 2 * rows), f32),
        ],
        compiler_params=params(1),
        cost_estimate=lasting(12),
    )(side, local, remote, weight)


def turn(value, cosine, sine):
    return value * cosine + pltpu.roll(value, value.shape[1] // 2, 1) * sine


def turn_back(value, cosine, sine):
    return value * cosine + pltpu.roll(value * sine, value.shape[1] // 2, 1)


def prepare_body(raw, inverse, gain, cosine, sine, query, key, val):
    width = query.shape[1]
    size = cosine.shape[1]
    for which, out in ((0, query), (1, key)):
        scale = upright(inverse[which : which + 1, :], size)
        for at in range(0, width, size):
            unit = raw[:, which * width + at : which * width + at + size] * scale
            out[:, at : at + size] = turn(
                unit * gain[which : which + 1, at : at + size], cosine[...], sine[...]
            ).astype(b16)
    val[...] = raw[:, 2 * width :].astype(b16)


def prepare(raw, inverse, gain, cosine, sine):
    rows, width = raw.shape[0], raw.shape[1] // 3
    size = cosine.shape[1]
    step = min(256, rows)
    by_row = lambda columns: pl.BlockSpec((step, columns), lambda i: (i, 0))
    return pl.pallas_call(
        prepare_body,
        grid=(rows // step,),
        in_specs=[
            by_row(3 * width),
            pl.BlockSpec((2, step), lambda i: (0, i)),
            pl.BlockSpec((2, width), lambda i: (0, 0)),
            by_row(size),
            by_row(size),
        ],
        out_specs=[by_row(width)] * 3,
        out_shape=[jax.ShapeDtypeStruct((rows, width), b16)] * 3,
        compiler_params=params(1),
        cost_estimate=lasting(3),
    )(raw, inverse, gain, cosine, sine)


def allowed(start, first_key, first_query, shape):
    keys = first_key + lax.broadcasted_iota(i32, shape, 0)
    queries = first_query + lax.broadcasted_iota(i32, shape, 1)
    return (keys >= start) & (keys <= queries)


def forward_body(span, size, spot, low, query, keys, values, start, out, log_total):
    i = pl.program_id(0)
    rows = query.shape[0]
    scale = 1.0 / math.sqrt(size)
    heads = [slice(at, at + size) for at in range(0, query.shape[1], size)]

    def step(j, carry):
        at = pl.multiple_of(j * span, span)
        here = pl.ds(at, span)
        mask = allowed(start[...], at, i * rows, (span, rows))
        after = []
        for head, (peak, total, summed) in zip(heads, carry):
            scores = dot(keys[here, head], query[:, head], 1, 1) * scale
            scores = jnp.where(mask, scores, masked_score)
            new_peak = jnp.maximum(peak, jnp.max(scores, axis=0, keepdims=True))
            shrink = jnp.exp(peak - new_peak)
            exponent = jnp.exp(scores - new_peak)
            total = total * shrink + jnp.sum(exponent, axis=0, keepdims=True)
            summed = summed * shrink + dot(values[here, head], exponent.astype(b16), 0, 0)
            after.append((new_peak, total, summed))
        return tuple(after)

    begin = (
        jnp.full((1, rows), masked_score, f32),
        jnp.zeros((1, rows), f32),
        jnp.zeros((size, rows), f32),
    )
    last = ((i + 1) * rows + span - 1) // span
    carry = lax.fori_loop(low[i], last, step, (begin,) * len(heads))
    for at, (head, (peak, total, summed)) in enumerate(zip(heads, carry)):
        out[:, head] = jnp.transpose(summed / total).astype(b16)
        log_total[at : at + 1, :] = peak + jnp.log(total)


def flash_forward(query, keys, values, start, spot, block, size):
    rows, width = query.shape
    heads = width // size
    blocks = rows // block
    span = min(512, rows)
    low = start.reshape(blocks, block)[:, 0] // span
    full = pl.BlockSpec((rows, width), lambda i, spot, low: (0, 0))
    return pl.pallas_call(
        functools.partial(forward_body, span, size),
        grid_spec=pltpu.PrefetchScalarGridSpec(
            num_scalar_prefetch=2,
            grid=(blocks,),
            in_specs=[
                pl.BlockSpec((block, width), lambda i, spot, low: (i, 0)),
                full,
                full,
                pl.BlockSpec((1, block), lambda i, spot, low: (0, i)),
            ],
            out_specs=[
                pl.BlockSpec((block, width), lambda i, spot, low: (spot[i], 0)),
                pl.BlockSpec((heads, block), lambda i, spot, low: (0, i)),
            ],
        ),
        out_shape=[
            jax.ShapeDtypeStruct((rows, width), b16),
            jax.ShapeDtypeStruct((heads, rows), f32),
        ],
        compiler_params=params(1),
        cost_estimate=lasting(18),
    )(spot, low, query, keys, values, start[None])


def backward_body(
    span,
    size,
    spot,
    low,
    query,
    keys,
    values,
    start,
    log_total,
    grad,
    out,
    d_query,
    d_keys,
    d_values,
):
    i = pl.program_id(0)
    rows = query.shape[0]
    scale = 1.0 / math.sqrt(size)
    heads = [slice(at, at + size) for at in range(0, query.shape[1], size)]

    @pl.when(i == 0)
    def _():
        d_keys[...] = jnp.zeros_like(d_keys)
        d_values[...] = jnp.zeros_like(d_values)

    deltas = [row_sums(grad[:, head].astype(f32) * out[:, head].astype(f32)) for head in heads]

    def step(j, carry):
        at = pl.multiple_of(j * span, span)
        here = pl.ds(at, span)
        mask = allowed(start[...], at, i * rows, (span, rows))
        after = []
        for which, (head, summed) in enumerate(zip(heads, carry)):
            scores = dot(keys[here, head], query[:, head], 1, 1) * scale
            soft = jnp.where(mask, jnp.exp(scores - log_total[which : which + 1, :]), 0.0)
            d_soft = dot(values[here, head], grad[:, head], 1, 1)
            d_scores = (soft * (d_soft - deltas[which]) * scale).astype(b16)
            d_values[here, head] += dot(soft.astype(b16), grad[:, head], 1, 0)
            d_keys[here, head] += dot(d_scores, query[:, head], 1, 0)
            after.append(summed + dot(keys[here, head], d_scores, 0, 0))
        return tuple(after)

    last = ((i + 1) * rows + span - 1) // span
    carry = lax.fori_loop(
        low[i], last, step, (jnp.zeros((size, rows), f32),) * len(heads)
    )
    for head, summed in zip(heads, carry):
        d_query[:, head] = jnp.transpose(summed)


def flash_backward(query, keys, values, start, log_total, grad, out, spot, block, size):
    rows, width = query.shape
    heads = width // size
    blocks = rows // block
    span = min(512, rows)
    low = start.reshape(blocks, block)[:, 0] // span
    natural = pl.BlockSpec((block, width), lambda i, spot, low: (i, 0))
    moved = pl.BlockSpec((block, width), lambda i, spot, low: (spot[i], 0))
    full = pl.BlockSpec((rows, width), lambda i, spot, low: (0, 0))
    return pl.pallas_call(
        functools.partial(backward_body, span, size),
        grid_spec=pltpu.PrefetchScalarGridSpec(
            num_scalar_prefetch=2,
            grid=(blocks,),
            in_specs=[
                natural,
                full,
                full,
                pl.BlockSpec((1, block), lambda i, spot, low: (0, i)),
                pl.BlockSpec((heads, block), lambda i, spot, low: (0, i)),
                moved,
                moved,
            ],
            out_specs=[natural, full, full],
        ),
        out_shape=[jax.ShapeDtypeStruct((rows, width), f32)] * 3,
        compiler_params=params(1),
        cost_estimate=lasting(22),
    )(spot, low, query, keys, values, start[None], log_total, grad, out)


def turned_sums_body(raw, inverse, gain, cosine, sine, d_query, d_key, sums, gains):
    width = d_query.shape[1]
    size = cosine.shape[1]

    @pl.when(pl.program_id(0) == 0)
    def _():
        gains[...] = jnp.zeros_like(gains)

    for which, grad in ((0, d_query), (1, d_key)):
        row = jnp.zeros((raw.shape[0], size), f32)
        scale = upright(inverse[which : which + 1, :], size)
        for at in range(0, width, size):
            unit = raw[:, which * width + at : which * width + at + size] * scale
            product = turn_back(grad[:, at : at + size], cosine[...], sine[...]) * unit
            gains[which : which + 1, at : at + size] += jnp.sum(product, axis=0, keepdims=True)
            row += product * gain[which : which + 1, at : at + size]
        sums[which : which + 1, :] = row_sums(row)


def turned_sums(raw, inverse, gain, cosine, sine, d_query, d_key):
    rows, width = d_query.shape
    size = cosine.shape[1]
    step = min(256, rows)
    by_row = lambda columns: pl.BlockSpec((step, columns), lambda i: (i, 0))
    return pl.pallas_call(
        turned_sums_body,
        grid=(rows // step,),
        in_specs=[
            by_row(3 * width),
            pl.BlockSpec((2, step), lambda i: (0, i)),
            pl.BlockSpec((2, width), lambda i: (0, 0)),
            by_row(size),
            by_row(size),
            by_row(width),
            by_row(width),
        ],
        out_specs=[
            pl.BlockSpec((2, step), lambda i: (0, i)),
            pl.BlockSpec((2, width), lambda i: (0, 0)),
        ],
        out_shape=[
            jax.ShapeDtypeStruct((2, rows), f32),
            jax.ShapeDtypeStruct((2, width), f32),
        ],
        compiler_params=params(1),
        cost_estimate=lasting(4),
    )(raw, inverse, gain, cosine, sine, d_query, d_key)


def raw_grads_body(
    spot, raw, inverse, gain, cosine, sine, d_query, d_key, d_val, means, out, moved
):
    width = d_query.shape[1]
    size = cosine.shape[1]
    for which, grad in ((0, d_query), (1, d_key)):
        scale = upright(inverse[which : which + 1, :], size)
        mean = upright(means[which : which + 1, :], size)
        for at in range(0, width, size):
            place = slice(which * width + at, which * width + at + size)
            unit = raw[:, place] * scale
            scaled = (
                turn_back(grad[:, at : at + size], cosine[...], sine[...])
                * gain[which : which + 1, at : at + size]
            )
            out[:, place] = (scale * (scaled - unit * mean)).astype(b16)
    out[:, 2 * width :] = d_val[...].astype(b16)
    moved[...] = out[...]


def raw_grads(raw, inverse, gain, cosine, sine, d_query, d_key, d_val, means, spot, block):
    rows, width = d_query.shape
    size = cosine.shape[1]
    by_row = lambda columns: pl.BlockSpec((block, columns), lambda i, spot: (i, 0))
    in_line = pl.BlockSpec((2, block), lambda i, spot: (0, i))
    return pl.pallas_call(
        raw_grads_body,
        grid_spec=pltpu.PrefetchScalarGridSpec(
            num_scalar_prefetch=1,
            grid=(rows // block,),
            in_specs=[
                by_row(3 * width),
                in_line,
                pl.BlockSpec((2, width), lambda i, spot: (0, 0)),
                by_row(size),
                by_row(size),
                by_row(width),
                by_row(width),
                by_row(width),
                in_line,
            ],
            out_specs=[
                by_row(3 * width),
                pl.BlockSpec((block, 3 * width), lambda i, spot: (spot[i], 0)),
            ],
        ),
        out_shape=[jax.ShapeDtypeStruct((rows, 3 * width), b16)] * 2,
        compiler_params=params(1),
        cost_estimate=lasting(5),
    )(spot, raw, inverse, gain, cosine, sine, d_query, d_key, d_val, means)


def ffn_forward_body(count, *refs):
    blocks, (w_gate, w_up, full, gate, up, act) = refs[:count], refs[count:]

    @pl.when(pl.program_id(0) == 0)
    def _():
        if count == 5:
            half = blocks[3].shape[0]
            parts = [block.at[:half] for block in blocks[:3]] + [blocks[3]]
            parts += [block.at[half:] for block in blocks[:3]] + [blocks[4]]
        else:
            parts = blocks
        at = 0
        for block in parts:
            full[at : at + block.shape[0], :] = block[...]
            at += block.shape[0]

    gate_pre = dot(full[...], w_gate[...], 1, 0)
    up_pre = dot(full[...], w_up[...], 1, 0)
    gate[...] = gate_pre.astype(b16)
    up[...] = up_pre.astype(b16)
    act[...] = (gate_pre * jax.nn.sigmoid(gate_pre) * up_pre).astype(b16)


def ffn_forward(blocks, w_both):
    rows = sum(block.shape[0] for block in blocks)
    width, columns = w_both.shape
    step = min(256, columns // 2)
    count = columns // 2 // step
    out = pl.BlockSpec((rows, step), lambda j: (0, j))
    hidden = jax.ShapeDtypeStruct((rows, columns // 2), b16)
    return pl.pallas_call(
        functools.partial(ffn_forward_body, len(blocks)),
        grid=(count,),
        in_specs=[pl.BlockSpec(block.shape, lambda j: (0, 0)) for block in blocks]
        + [
            pl.BlockSpec((width, step), lambda j: (0, j)),
            pl.BlockSpec((width, step), lambda j: (0, j + count)),
        ],
        out_specs=[pl.BlockSpec((rows, width), lambda j: (0, 0)), out, out, out],
        out_shape=[jax.ShapeDtypeStruct((rows, width), b16), hidden, hidden, hidden],
        compiler_params=params(1),
        cost_estimate=lasting(10),
    )(*blocks, w_both, w_both)


def joined_dot_body(*refs):
    blocks, (weight, full, out) = refs[:-3], refs[-3:]
    at = 0
    for block in blocks:
        rows = pl.ds(at, block.shape[0])
        full[rows, :] = block[...]
        out[rows, :] = dot(block[...], weight[...], 1, 0).astype(b16)
        at += block.shape[0]


def joined_dot(blocks, weight):
    rows = sum(block.shape[0] for block in blocks)
    width, columns = weight.shape
    whole = lambda shape: pl.BlockSpec(shape, lambda i: (0, 0))
    return pl.pallas_call(
        joined_dot_body,
        grid=(1,),
        in_specs=[whole(block.shape) for block in blocks] + [whole(weight.shape)],
        out_specs=[whole((rows, width)), whole((rows, columns))],
        out_shape=[
            jax.ShapeDtypeStruct((rows, width), b16),
            jax.ShapeDtypeStruct((rows, columns), b16),
        ],
        compiler_params=params(1),
        cost_estimate=lasting(4),
    )(*blocks, weight)


def ffn_backward_body(grad, w_down, gate, up, d_gate, d_up):
    d_act = dot(grad[...], w_down[...], 1, 0)
    gate_pre, up_pre = gate[...].astype(f32), up[...].astype(f32)
    sigmoid = jax.nn.sigmoid(gate_pre)
    d_gate[...] = (d_act * up_pre * sigmoid * (1.0 + gate_pre * (1.0 - sigmoid))).astype(b16)
    d_up[...] = (d_act * gate_pre * sigmoid).astype(b16)


def ffn_backward(grad, w_down, gate, up):
    rows, width = grad.shape
    columns = w_down.shape[1]
    step = min(256, columns)
    out = pl.BlockSpec((rows, step), lambda j: (0, j))
    return pl.pallas_call(
        ffn_backward_body,
        grid=(columns // step,),
        in_specs=[
            pl.BlockSpec((rows, width), lambda j: (0, 0)),
            pl.BlockSpec((width, step), lambda j: (0, j)),
            out,
            out,
        ],
        out_specs=[out, out],
        out_shape=[jax.ShapeDtypeStruct((rows, columns), b16)] * 2,
        compiler_params=params(1),
        cost_estimate=lasting(6),
    )(grad, w_down, gate, up)


def ffn_residual_body(d_gate, d_up, w_gate, w_up, *rest):
    value = dot(d_gate[...], w_gate[...], 1, 1) + dot(d_up[...], w_up[...], 1, 1)
    if len(rest) == 2:
        value += rest[0][...].astype(f32)
    rest[-1][...] = value.astype(b16)


def ffn_residual(d_gate, d_up, w_both, *received):
    rows, columns = d_gate.shape
    width = w_both.shape[0]
    step = min(256, width)
    full = pl.BlockSpec((rows, columns), lambda j: (0, 0))
    out = pl.BlockSpec((rows, step), lambda j: (0, j))
    return pl.pallas_call(
        ffn_residual_body,
        grid=(width // step,),
        in_specs=[
            full,
            full,
            pl.BlockSpec((step, columns), lambda j: (j, 0)),
            pl.BlockSpec((step, columns), lambda j: (j, 1)),
        ]
        + [out] * len(received),
        out_specs=out,
        out_shape=jax.ShapeDtypeStruct((rows, width), b16),
        compiler_params=params(1),
        cost_estimate=lasting(9),
    )(d_gate, d_up, w_both, w_both, *received)


def columns_body(side, query, key, val, out_weight, out):
    width = query.shape[1]
    for at, piece in enumerate((query, key, val)):
        out[:, at * width : (at + 1) * width] = piece[...].astype(b16)
    out[:, 3 * width :] = jnp.transpose(out_weight[...]).astype(b16)


def attention_columns(side, query, key, val, out_weight):
    piece, width = query.shape[0], query.shape[1] // 2
    upper = pl.BlockSpec((piece, width), lambda i, side: (0, side[0]))
    return pl.pallas_call(
        columns_body,
        grid_spec=pltpu.PrefetchScalarGridSpec(
            num_scalar_prefetch=1,
            grid=(1,),
            in_specs=[
                upper,
                upper,
                upper,
                pl.BlockSpec((width, piece), lambda i, side: (side[0], 0)),
            ],
            out_specs=pl.BlockSpec((piece, 4 * width), lambda i, side: (0, 0)),
        ),
        out_shape=jax.ShapeDtypeStruct((piece, 4 * width), b16),
        compiler_params=params(1, 60),
        cost_estimate=lasting(2),
    )(side, query, key, val, out_weight)


def flip_body(value, out):
    out[...] = jnp.transpose(value[...])


def flip(value):
    rows, columns = value.shape
    step = min(256, columns)
    return pl.pallas_call(
        flip_body,
        grid=(columns // step,),
        in_specs=[pl.BlockSpec((rows, step), lambda i: (0, i))],
        out_specs=pl.BlockSpec((step, rows), lambda i: (i, 0)),
        out_shape=jax.ShapeDtypeStruct((columns, rows), value.dtype),
        compiler_params=params(1),
    )(value)


def adam_step(weight, first_moment, second_moment, gradient):
    new_first = beta_one * first_moment + (1.0 - beta_one) * gradient
    new_second = beta_two * second_moment + (1.0 - beta_two) * gradient * gradient
    first_hat = new_first / (1.0 - beta_one**step_count)
    second_hat = new_second / (1.0 - beta_two**step_count)
    updated = weight - learn_rate * (
        first_hat / (jnp.sqrt(second_hat) + adam_eps) + decay_rate * weight
    )
    return (updated, new_first, new_second)


def assemble_body(count, flags, *refs):
    out = refs[-1]
    spot = pl.program_id(0)
    theirs = ((spot // count) != flags[0]).astype(i32)
    place = theirs * count + ((spot % count) ^ flags[1])
    for at, block in enumerate(refs[:-1]):

        @pl.when(place == at)
        def _(block=block):
            out[0] = block[...].astype(f32)


def assemble(mine, theirs):
    count = len(mine)
    block, width = mine[0].shape
    shift = lax.axis_index(TX) if count == 2 else jnp.zeros((), i32)
    return pl.pallas_call(
        functools.partial(assemble_body, count),
        grid_spec=pltpu.PrefetchScalarGridSpec(
            num_scalar_prefetch=1,
            grid=(2 * count,),
            in_specs=[pl.BlockSpec((block, width), lambda i, flags: (0, 0))] * (2 * count),
            out_specs=pl.BlockSpec((1, block, width), lambda i, flags: (0, i, 0)),
        ),
        out_shape=jax.ShapeDtypeStruct((1, 2 * count * block, width), f32),
        compiler_params=params(1),
        cost_estimate=lasting(5),
    )(jnp.stack([lax.axis_index(TC), shift]), *mine, *theirs)


def over_chips(value):
    count = lax.axis_size(TX)
    if count == 2:
        return [value, swap(value, TX)]
    return jnp.split(lax.all_gather(value, TX, axis=0, tiled=True), count)


def over_core(blocks):
    return [swap(block, TC) for block in blocks]


def adam_body(turned, flag, weight, first, second, own, other, grad, updated, mean, square):
    value = jnp.where(pl.program_id(0) == flag[0], own[...].astype(f32), other[...].astype(f32))
    if turned:
        value = jnp.transpose(value)
    grad[...] = value
    updated[...], mean[...], square[...] = adam_step(
        weight[...], first[...], second[...], value
    )


def adam(weight, first, second, own, other, flag, turned=False, column=0):
    rows, columns = weight.shape
    if turned:
        half = rows // 2
        step = min(256, half)
        count = half // step
        mine = pl.BlockSpec((step, columns), lambda j, i, flag: (j * count + i, 0))
        halves = pl.BlockSpec((columns, step), lambda j, i, flag: (0, column * count + i))
        both = pl.BlockSpec(
            (None, columns, step), lambda j, i, flag: (flag[0], 0, column * count + i)
        )
    else:
        half = columns // 2
        step = min(128, rows)
        count = rows // step
        mine = pl.BlockSpec((step, half), lambda j, i, flag: (i, j))
        halves = pl.BlockSpec((step, half), lambda j, i, flag: (i, column))
        both = pl.BlockSpec((None, step, half), lambda j, i, flag: (flag[0], i, column))
    return pl.pallas_call(
        functools.partial(adam_body, turned),
        grid_spec=pltpu.PrefetchScalarGridSpec(
            num_scalar_prefetch=1,
            grid=(2, count),
            in_specs=[mine] * 3 + [both, halves],
            out_specs=[mine] * 4,
        ),
        out_shape=[jax.ShapeDtypeStruct(weight.shape, f32)] * 4,
        compiler_params=params(2),
        cost_estimate=lasting(weight.size * 8e-6),
    )(flag, weight, first, second, own, other)


def row_mean(a, b):
    return jnp.mean(a * b, axis=1, keepdims=True)


def shards(tokens, cotangent, segment_ids, *state):
    masters, first_moments, second_moments = state[:11], state[11:22], state[22:33]
    inputs = tokens[0]
    docs_here = segment_ids[0]
    rows, width = inputs.shape
    ring = lax.axis_size(SHARD)
    teams = lax.axis_size(TENSOR)
    y = lax.axis_index(CX)
    piece = masters[0].shape[0]
    heads_here = masters[7].shape[0]
    head_piece = masters[7].shape[1]
    size = head_piece * ring * 2
    wide = heads_here * size // 2
    hidden = masters[4].shape[1] // 2
    block = rows // teams
    length = 2 * rows
    my_block = lax.axis_index(TC) * lax.axis_size(TX) + lax.axis_index(TX)

    def my_rows(value):
        return lax.dynamic_slice_in_dim(value, my_block * block, block, 0)

    docs_all = gather_axis(docs_here, CX)
    gains = jnp.concatenate([gain.astype(b16).reshape(-1) for gain in masters[7:]])[None]
    gains = gather_axis(gather_axis(gather_axis(gains, CX), SL), SH).astype(f32)
    first = list(masters[:7])

    def columns_of(weight, index, count):
        return lax.dynamic_slice_in_dim(weight, index * count, count, 1).astype(b16)

    def over_ctx(weights, count):
        mine, theirs = [
            jnp.concatenate([columns_of(w, index, count) for w in weights], axis=1)
            for index in (y, 1 - y)
        ]
        return mine, swap(theirs, CX)

    def over_shard(value):
        return lax.all_gather(value, SHARD, axis=0, tiled=True)

    attn_own = over_shard(attention_columns(y[None], *first[:4]))
    theirs = swap(attention_columns(1 - y[None], *first[:4]), CX)
    theirs, local_rows, gains, docs_all = tie(theirs, my_rows(inputs), gains, docs_all)
    theirs, attn_own = tie(theirs, attn_own)
    attn_other = over_shard(theirs)

    remote, gate_w, up_w, down_w = tie(swap(local_rows, CX), *first[4:])
    remote = gather_axis(remote, TX)
    gate_w = pair(*over_ctx([gate_w], hidden), CX)
    remote, gate_w = tie(remote, gate_w)
    remote = gather_axis(remote, TC)
    up_w = pair(*over_ctx([up_w], hidden), CX)
    attn_other, remote, w_both = tie(
        attn_other, remote, jnp.concatenate([gate_w, up_w], axis=1)
    )
    w_both = over_shard(w_both)
    w_attn = pair(
        *[value.reshape(ring, 1, piece, 4 * wide) for value in (attn_own, attn_other)], CX, 1
    ).reshape(width, 4 * wide)
    w_qkv, w_out = w_attn[:, : 3 * wide], w_attn[:, 3 * wide :]
    down_w = pair(*over_ctx([flip(down_w.astype(b16))], hidden), CX)

    count = heads_here * head_piece
    head_gain = jnp.stack(
        [
            part(
                jnp.transpose(
                    gains[:, which * count : (which + 1) * count].reshape(
                        ring * 2, heads_here, head_piece
                    ),
                    (1, 0, 2),
                ).reshape(2, wide),
                y,
                0,
            )
            for which in range(2)
        ]
    )
    attn_gain = gains[:, 2 * count : 2 * count + piece].reshape(1, width)
    ffn_gain = gains[:, 2 * count + piece :].reshape(1, width)

    doc_range = jnp.arange(DOCS, dtype=i32)
    counts = jnp.sum((docs_all[:, None] == doc_range[None, :]).astype(i32), axis=0)
    starts = jnp.cumsum(counts) - counts
    own_start = jnp.sum(
        jnp.where(docs_all[:, None] == doc_range[None, :], starts[None, :], 0), axis=1
    )
    positions = jnp.arange(length, dtype=i32) - own_start
    frequencies = rope_base ** (-(jnp.arange(size // 2, dtype=f32) * 2.0) / size)
    angles = positions.astype(f32)[:, None] * frequencies[None, :]
    cosine, sine = jnp.cos(angles), jnp.sin(angles)
    cosine = jnp.concatenate([cosine, cosine], axis=1)
    sine = jnp.concatenate([-sine, sine], axis=1)

    raw, squares = project(y[None], inputs, remote, w_attn)
    inverse = lax.rsqrt(plane_sum(squares) / width + norm_eps)
    query, key, val = prepare(raw, inverse, head_gain, cosine, sine)
    query, down_w = tie(query, down_w)
    spot = block_places(CX)
    attended, log_total = flash_forward(query, key, val, own_start, spot, block, size)
    group = length // 2
    branch = collect(
        across(dot(attended[:group], w_out, 1, 1), dot(attended[group:], w_out, 1, 1)), CX
    )
    branch_inv = lax.rsqrt(row_mean(branch, branch) + norm_eps)
    branch_unit = branch * branch_inv
    residual = my_rows(inputs).astype(f32) + branch_unit * attn_gain
    res, w_both, down_w = tie(residual.astype(b16), w_both, down_w)
    w_down = over_shard(down_w)
    res = spread(res, CX)

    res, gate_pre, up_pre, activated = zip(*[ffn_forward(blocks, w_both) for blocks in res])
    *activated, w_down = tie(*activated, w_down)
    parts = 2 if lax.axis_size(TX) == 2 else 1
    grad_out = my_rows(cotangent[0]).astype(f32)
    d_ffn, block_rows, grad_ffn_gain = [], [], 0.0
    for mine, theirs, rows_in, cot in zip(
        *[jnp.split(value, parts) for value in (*activated, residual, grad_out)]
    ):
        ffn_out = collect(across(dot(mine, w_down, 1, 1), dot(theirs, w_down, 1, 1)), CX)
        ffn_inv = lax.rsqrt(row_mean(ffn_out, ffn_out) + norm_eps)
        ffn_unit = ffn_out * ffn_inv
        scaled_out = cot * ffn_gain
        d_ffn.append(
            (ffn_inv * (scaled_out - ffn_unit * row_mean(scaled_out, ffn_unit))).astype(b16)
        )
        grad_ffn_gain = grad_ffn_gain + jnp.sum(cot * ffn_unit, axis=0)
        block_rows.append((rows_in + ffn_unit * ffn_gain).astype(b16))
    d_ffn = joined_halves(spread(jnp.concatenate(d_ffn, 0), CX))
    block_rows = jnp.concatenate(block_rows, 0)

    def both(left, right):
        return (dot(left[0], right[0], 0, 0) + dot(left[1], right[1], 0, 0)).astype(b16)

    def to_shard(partial):
        return lax.psum_scatter(partial, SHARD, scatter_dimension=0, tiled=True)

    def to_owner(summed):
        summed = summed.reshape(2, piece, -1)
        return summed, swap(part(summed, 1 - y, 0), CX)

    *d_ffn, block_rows = tie(*d_ffn, block_rows)
    block_rows = over_chips(block_rows)
    grad_down = both(d_ffn, activated)
    grad_down, *d_ffn = tie(grad_down, *d_ffn)
    grad_down = to_shard(grad_down)
    d_gate, d_up = zip(
        *[ffn_backward(d, w_down, g, u) for d, g, u in zip(d_ffn, gate_pre, up_pre)]
    )
    *block_rows, d_gate0, d_gate1, d_up0, d_up1 = tie(*block_rows, *d_gate, *d_up)
    d_gate, d_up = [d_gate0, d_gate1], [d_up0, d_up1]
    theirs, *turned = tie(ffn_residual(d_gate[1], d_up[1], w_both), *d_gate)
    d_gate = turned
    grad_gate = dot(res[0], d_gate[0], 0, 0).astype(b16)
    theirs, grad_gate = tie(swap(theirs, TC), grad_gate)
    both_ffn = ffn_residual(d_gate[0], d_up[0], w_both, theirs)
    both_ffn, *turned = tie(both_ffn, *d_gate, *d_up)
    d_gate, d_up = turned[:2], turned[2:]
    grad_gate = (grad_gate.astype(f32) + dot(res[1], d_gate[1], 0, 0)).astype(b16)
    grad_gate = to_shard(grad_gate)
    back_ffn, *d_up = collect_halves(both_ffn, CX, *d_up)
    block_theirs = over_core(block_rows)
    grad_upward = both(res, d_up)
    grad_res = grad_out + back_ffn
    scaled_res = grad_res * attn_gain
    d_branch = (
        branch_inv * (scaled_res - branch_unit * row_mean(scaled_res, branch_unit))
    ).astype(b16)
    d_branch, grad_upward, grad_down = tie(d_branch, grad_upward, grad_down)
    down_halves = to_owner(grad_down)
    grad_upward = to_shard(grad_upward)
    grad_attn_gain = jnp.sum(grad_res * branch_unit, axis=0)
    triple = lambda i: (masters[i], first_moments[i], second_moments[i])

    d_branch, d_att = zip(*[joined_dot(blocks, w_out) for blocks in spread(d_branch, CX)])
    *d_branch, grad_gate = tie(*d_branch, grad_gate)
    gate_halves = to_owner(grad_gate)
    d_att = jnp.concatenate(d_att, 0)
    d_query, d_key, d_val = flash_backward(
        query, key, val, own_start, log_total, d_att, attended, spot, block, size
    )
    d_query, *turned = tie(d_query, *d_branch, *down_halves, *gate_halves)
    d_branch, down_halves, gate_halves = turned[:2], turned[2:4], turned[4:]
    grad_out_w = both(d_branch, [attended[:group], attended[group:]])
    d_query, grad_out_w = tie(d_query, grad_out_w)
    sums, grad_heads = turned_sums(raw, inverse, head_gain, cosine, sine, d_query, d_key)
    plane_sums = plane_sum(
        jnp.concatenate([sums, grad_attn_gain[None], grad_ffn_gain[None]])
    )
    means = plane_sums[:2] / width
    small = jnp.concatenate([plane_sums[2:].reshape(1, -1), grad_heads.reshape(1, -1)], 1)
    small = sum_axis(sum_axis(small, SL), SH)
    d_qkv, moved = raw_grads(
        raw, inverse, head_gain, cosine, sine, d_query, d_key, d_val, means, spot, block
    )

    sides = d_qkv.reshape(2, rows, 3 * wide)
    grad_qkv = both((inputs, remote), (part(sides, y, 0), part(sides, 1 - y, 0)))
    grad_attn, grad_upward = tie(
        jnp.concatenate([grad_qkv, grad_out_w], axis=1), grad_upward
    )
    grad_attn = to_shard(grad_attn)
    both_attn = across(dot(moved[:group], w_qkv, 1, 1), dot(moved[group:], w_qkv, 1, 1))
    back_attn = collect(both_attn, CX)
    down_step = adam(*triple(6), *down_halves, y[None], turned=True)
    gate_step = adam(*triple(4), *gate_halves, y[None])
    block_share = assemble(block_rows, block_theirs)
    back_attn, small, block_share, grad_upward, *turned = tie(
        back_attn, small, block_share, grad_upward, *down_step, *gate_step
    )
    down_step, gate_step = turned[:4], turned[4:]
    up_step = adam(*triple(5), *to_owner(grad_upward), y[None])
    input_rows = over_chips((grad_res + back_attn).astype(b16))
    index = lax.axis_index(SHARD) * 2 + y
    wide_sums = lax.dynamic_slice_in_dim(
        small[0, : 2 * width].reshape(2, width), index * piece, piece, 1
    )
    head_sums = small[0, 2 * width :].reshape(2, 1, heads_here // 2, size)
    head_sums = pair(head_sums, swap(head_sums, CX), CX, 1).reshape(2, heads_here, size)
    head_sums = lax.dynamic_slice_in_dim(head_sums, index * head_piece, head_piece, 2)

    gain_steps = []
    for i, grad in enumerate((head_sums[0], head_sums[1], wide_sums[0], wide_sums[1])):
        gain_steps += (grad,) + adam_step(*triple(7 + i), grad)
    _, *turned = tie(grad_attn[:1, :1], *gain_steps, *up_step, *input_rows)
    gain_steps, up_step, input_rows = turned[:16], turned[16:20], turned[20:]
    attn_halves = to_owner(grad_attn)
    input_share = assemble(input_rows, over_core(input_rows))
    stepped = [adam(*triple(i), *attn_halves, y[None], i == 3, i) for i in range(4)]
    stepped += [gate_step, up_step, down_step]
    stepped += [gain_steps[at : at + 4] for at in range(0, 16, 4)]
    return tuple(
        [block_share, input_share]
        + [result[which] for which in range(4) for result in stepped]
    )


def solution(mesh):
    ring, ctx, teams = (mesh.shape[name] for name in mesh.axis_names)
    fine = Mesh(
        mesh.devices.reshape(ring // 2, 2, ctx, teams // 2, 2), (SH, SL, CX, TX, TC)
    )
    owners = (SH, SL, CX)
    column = P(owners, TENSOR)
    row = P(TENSOR, owners)
    vector = P(owners)
    act = P(SHARD, CX, None)
    weights = (column, column, column, row, column, column, row, row, row, vector, vector)
    return jax.shard_map(
        shards,
        mesh=fine,
        in_specs=(act, act, P(SHARD, CX)) + weights * 3,
        out_specs=(act, act) + weights * 4,
        check_vma=False,
    )
```

```python
import functools
import math

import jax
import jax.numpy as jnp
from jax import lax
from jax.experimental import pallas as pl
from jax.experimental.pallas import tpu as pltpu
from jax.sharding import Mesh
from jax.sharding import PartitionSpec as P

DOCS = 3
rope_base = 500000.0
norm_eps = 1e-06
learn_rate = 0.3
beta_one = 0.9
beta_two = 0.95
adam_eps = 1e-08
decay_rate = 0.1
step_count = 2
masked_score = -1e30

f32 = jnp.float32
b16 = jnp.bfloat16
i32 = jnp.int32

SH, SL, CX, TX, TC = "sh", "sl", "ctx", "tx", "tc"
SHARD = (SH, SL)
TENSOR = (TX, TC)
PLANE = (CX, TX, TC)


def dot(a, b, ca, cb):
    return lax.dot_general(a, b, (((ca,), (cb,)), ((), ())), preferred_element_type=f32)


def swap(value, axis):
    return lax.ppermute(value, axis, [(0, 1), (1, 0)])


def pair(mine, other, axis, at=0):
    return jnp.where(
        lax.axis_index(axis) == 0,
        jnp.concatenate([mine, other], at),
        jnp.concatenate([other, mine], at),
    )


def gather_axis(value, axis):
    if lax.axis_size(axis) == 2:
        return pair(value, swap(value, axis), axis)
    return lax.all_gather(value, axis, axis=0, tiled=True)


def sum_axis(value, axis):
    if lax.axis_size(axis) == 2:
        return value + swap(value, axis)
    return lax.psum(value, axis)


def plane_sum(value):
    return sum_axis(sum_axis(sum_axis(value, TC), TX), CX)


def tie(*values):
    return lax.optimization_barrier(values)


def part(value, index, at):
    return lax.dynamic_index_in_dim(value, index, at, keepdims=False)


def rows_all(value):
    return gather_axis(gather_axis(value, TX), TC)


def spread(value, axis):
    if lax.axis_size(TX) == 2:
        half = value.shape[0] // 2
        over_x = swap(value, TX)
        over_y = swap(value, axis)
        over_x, over_y = tie(over_x, over_y)
        near, far = tie(swap(over_y[:half], TX), swap(over_x[half:], axis))
        mine = [value, over_x, over_y, near, far]
    else:
        line = lax.all_gather(value, TX, axis=0, tiled=True)
        mine = [line, swap(line, axis)]
    return mine, [swap(block, TC) for block in mine]


def joined(groups):
    return [jnp.concatenate(blocks, 0) for blocks in groups]


def joined_halves(groups):
    if len(groups[0]) != 5:
        return joined(groups)
    out = []
    for first, second, third, near, far in groups:
        half = near.shape[0]
        upper = [block[:half] for block in (first, second, third)] + [near]
        lower = [block[half:] for block in (first, second, third)] + [far]
        out.append(jnp.concatenate(upper + lower, 0))
    return out


def across(mine, theirs):
    return (mine + swap(theirs.astype(b16), TC).astype(f32)).astype(b16)


def collect(both, axis):
    count = lax.axis_size(TX)
    block = both.shape[0] // (2 * count)
    if count == 2:
        half = block // 2
        near = swap(both[3 * block : 3 * block + half], TX)
        far = swap(both[3 * block + half :], axis)
        over_x = jnp.concatenate(
            [both[block : block + half], both[block + half : 2 * block] + far], 0
        )
        over_y = jnp.concatenate(
            [both[2 * block : 2 * block + half] + near, both[2 * block + half : 3 * block]], 0
        )
        return (
            both[:block].astype(f32)
            + swap(over_x, TX).astype(f32)
            + swap(over_y, axis).astype(f32)
        )
    line = both[: count * block] + swap(both[count * block :], axis)
    return lax.psum_scatter(line, TX, scatter_dimension=0, tiled=True).astype(f32)


def collect_halves(both, axis, *later):
    h = both.shape[0] // 8
    near, far, *later = tie(swap(both[3 * h : 4 * h], TX), swap(both[7 * h :], axis), *later)
    over_x = jnp.concatenate([both[h : 2 * h], both[5 * h : 6 * h] + far], 0)
    over_y = jnp.concatenate([both[2 * h : 3 * h] + near, both[6 * h : 7 * h]], 0)
    return (both, swap(over_x, TX), swap(over_y, axis), *later)


def block_places(axis):
    count = lax.axis_size(TX)
    spot = jnp.arange(4 * count, dtype=i32)
    side = (spot // (2 * count)) ^ lax.axis_index(axis)
    core = (spot // count % 2) ^ lax.axis_index(TC)
    along = spot % count
    if count == 2:
        along = along ^ lax.axis_index(TX)
    return (core * 2 + side) * count + along


def params(steps, mebibytes=30):
    return pltpu.CompilerParams(
        dimension_semantics=("arbitrary",) * steps, vmem_limit_bytes=mebibytes * 1024 * 1024
    )


def lasting(us):
    return pl.CostEstimate(flops=0, transcendentals=0, bytes_accessed=int(us * 0.5e6))


def upright(row, columns):
    return jnp.transpose(jnp.broadcast_to(row, (columns, row.shape[1])))


def row_sums(value):
    return jnp.sum(jnp.transpose(value), axis=0, keepdims=True)


def project_body(side, local, remote, weight, raw, squares):
    half = pl.num_programs(0) // 2
    mine = (pl.program_id(0) // half) == side[0]
    raw[...] = dot(jnp.where(mine, local[...], remote[...]), weight[...], 1, 0)
    width = raw.shape[1] // 3
    for which in range(2):
        total = jnp.zeros((raw.shape[0], 128), f32)
        for at in range(which * width, (which + 1) * width, 128):
            total += raw[:, at : at + 128] * raw[:, at : at + 128]
        squares[which : which + 1, :] = row_sums(total)


def project(side, local, remote, weight):
    rows, width = local.shape
    columns = weight.shape[1] // 4 * 3
    step = min(256, rows)
    half = rows // step
    tokens = pl.BlockSpec((step, width), lambda i, side: (i % half, 0))
    return pl.pallas_call(
        project_body,
        grid_spec=pltpu.PrefetchScalarGridSpec(
            num_scalar_prefetch=1,
            grid=(2 * half,),
            in_specs=[
                tokens,
                tokens,
                pl.BlockSpec((width, columns), lambda i, side: (0, 0)),
            ],
            out_specs=[
                pl.BlockSpec((step, columns), lambda i, side: (i, 0)),
                pl.BlockSpec((2, step), lambda i, side: (0, i)),
            ],
        ),
        out_shape=[
            jax.ShapeDtypeStruct((2 * rows, columns), f32),
            jax.ShapeDtypeStruct((2, 2 * rows), f32),
        ],
        compiler_params=params(1),
        cost_estimate=lasting(12),
    )(side, local, remote, weight)


def turn(value, cosine, sine):
    return value * cosine + pltpu.roll(value, value.shape[1] // 2, 1) * sine


def turn_back(value, cosine, sine):
    return value * cosine + pltpu.roll(value * sine, value.shape[1] // 2, 1)


def prepare_body(raw, inverse, gain, cosine, sine, query, key, val):
    width = query.shape[1]
    size = cosine.shape[1]
    for which, out in ((0, query), (1, key)):
        scale = upright(inverse[which : which + 1, :], size)
        for at in range(0, width, size):
            unit = raw[:, which * width + at : which * width + at + size] * scale
            out[:, at : at + size] = turn(
                unit * gain[which : which + 1, at : at + size], cosine[...], sine[...]
            ).astype(b16)
    val[...] = raw[:, 2 * width :].astype(b16)


def prepare(raw, inverse, gain, cosine, sine):
    rows, width = raw.shape[0], raw.shape[1] // 3
    size = cosine.shape[1]
    step = min(256, rows)
    by_row = lambda columns: pl.BlockSpec((step, columns), lambda i: (i, 0))
    return pl.pallas_call(
        prepare_body,
        grid=(rows // step,),
        in_specs=[
            by_row(3 * width),
            pl.BlockSpec((2, step), lambda i: (0, i)),
            pl.BlockSpec((2, width), lambda i: (0, 0)),
            by_row(size),
            by_row(size),
        ],
        out_specs=[by_row(width)] * 3,
        out_shape=[jax.ShapeDtypeStruct((rows, width), b16)] * 3,
        compiler_params=params(1),
        cost_estimate=lasting(3),
    )(raw, inverse, gain, cosine, sine)


def allowed(start, first_key, first_query, shape):
    keys = first_key + lax.broadcasted_iota(i32, shape, 0)
    queries = first_query + lax.broadcasted_iota(i32, shape, 1)
    return (keys >= start) & (keys <= queries)


def forward_body(span, size, spot, low, query, keys, values, start, out, log_total):
    i = pl.program_id(0)
    rows = query.shape[0]
    scale = 1.0 / math.sqrt(size)
    heads = [slice(at, at + size) for at in range(0, query.shape[1], size)]

    def step(j, carry):
        at = pl.multiple_of(j * span, span)
        here = pl.ds(at, span)
        mask = allowed(start[...], at, i * rows, (span, rows))
        after = []
        for head, (peak, total, summed) in zip(heads, carry):
            scores = dot(keys[here, head], query[:, head], 1, 1) * scale
            scores = jnp.where(mask, scores, masked_score)
            new_peak = jnp.maximum(peak, jnp.max(scores, axis=0, keepdims=True))
            shrink = jnp.exp(peak - new_peak)
            exponent = jnp.exp(scores - new_peak)
            total = total * shrink + jnp.sum(exponent, axis=0, keepdims=True)
            summed = summed * shrink + dot(values[here, head], exponent.astype(b16), 0, 0)
            after.append((new_peak, total, summed))
        return tuple(after)

    begin = (
        jnp.full((1, rows), masked_score, f32),
        jnp.zeros((1, rows), f32),
        jnp.zeros((size, rows), f32),
    )
    last = ((i + 1) * rows + span - 1) // span
    carry = lax.fori_loop(low[i], last, step, (begin,) * len(heads))
    for at, (head, (peak, total, summed)) in enumerate(zip(heads, carry)):
        out[:, head] = jnp.transpose(summed / total).astype(b16)
        log_total[at : at + 1, :] = peak + jnp.log(total)


def flash_forward(query, keys, values, start, spot, block, size):
    rows, width = query.shape
    heads = width // size
    blocks = rows // block
    span = min(512, rows)
    low = start.reshape(blocks, block)[:, 0] // span
    full = pl.BlockSpec((rows, width), lambda i, spot, low: (0, 0))
    return pl.pallas_call(
        functools.partial(forward_body, span, size),
        grid_spec=pltpu.PrefetchScalarGridSpec(
            num_scalar_prefetch=2,
            grid=(blocks,),
            in_specs=[
                pl.BlockSpec((block, width), lambda i, spot, low: (i, 0)),
                full,
                full,
                pl.BlockSpec((1, block), lambda i, spot, low: (0, i)),
            ],
            out_specs=[
                pl.BlockSpec((block, width), lambda i, spot, low: (spot[i], 0)),
                pl.BlockSpec((heads, block), lambda i, spot, low: (0, i)),
            ],
        ),
        out_shape=[
            jax.ShapeDtypeStruct((rows, width), b16),
            jax.ShapeDtypeStruct((heads, rows), f32),
        ],
        compiler_params=params(1),
        cost_estimate=lasting(18),
    )(spot, low, query, keys, values, start[None])


def backward_body(
    span,
    size,
    spot,
    low,
    query,
    keys,
    values,
    start,
    log_total,
    grad,
    out,
    d_query,
    d_keys,
    d_values,
):
    i = pl.program_id(0)
    rows = query.shape[0]
    scale = 1.0 / math.sqrt(size)
    heads = [slice(at, at + size) for at in range(0, query.shape[1], size)]

    @pl.when(i == 0)
    def _():
        d_keys[...] = jnp.zeros_like(d_keys)
        d_values[...] = jnp.zeros_like(d_values)

    deltas = [row_sums(grad[:, head].astype(f32) * out[:, head].astype(f32)) for head in heads]

    def step(j, carry):
        at = pl.multiple_of(j * span, span)
        here = pl.ds(at, span)
        mask = allowed(start[...], at, i * rows, (span, rows))
        after = []
        for which, (head, summed) in enumerate(zip(heads, carry)):
            scores = dot(keys[here, head], query[:, head], 1, 1) * scale
            soft = jnp.where(mask, jnp.exp(scores - log_total[which : which + 1, :]), 0.0)
            d_soft = dot(values[here, head], grad[:, head], 1, 1)
            d_scores = (soft * (d_soft - deltas[which]) * scale).astype(b16)
            d_values[here, head] += dot(soft.astype(b16), grad[:, head], 1, 0)
            d_keys[here, head] += dot(d_scores, query[:, head], 1, 0)
            after.append(summed + dot(keys[here, head], d_scores, 0, 0))
        return tuple(after)

    last = ((i + 1) * rows + span - 1) // span
    carry = lax.fori_loop(
        low[i], last, step, (jnp.zeros((size, rows), f32),) * len(heads)
    )
    for head, summed in zip(heads, carry):
        d_query[:, head] = jnp.transpose(summed)


def flash_backward(query, keys, values, start, log_total, grad, out, spot, block, size):
    rows, width = query.shape
    heads = width // size
    blocks = rows // block
    span = min(512, rows)
    low = start.reshape(blocks, block)[:, 0] // span
    natural = pl.BlockSpec((block, width), lambda i, spot, low: (i, 0))
    moved = pl.BlockSpec((block, width), lambda i, spot, low: (spot[i], 0))
    full = pl.BlockSpec((rows, width), lambda i, spot, low: (0, 0))
    return pl.pallas_call(
        functools.partial(backward_body, span, size),
        grid_spec=pltpu.PrefetchScalarGridSpec(
            num_scalar_prefetch=2,
            grid=(blocks,),
            in_specs=[
                natural,
                full,
                full,
                pl.BlockSpec((1, block), lambda i, spot, low: (0, i)),
                pl.BlockSpec((heads, block), lambda i, spot, low: (0, i)),
                moved,
                moved,
            ],
            out_specs=[natural, full, full],
        ),
        out_shape=[jax.ShapeDtypeStruct((rows, width), f32)] * 3,
        compiler_params=params(1),
        cost_estimate=lasting(22),
    )(spot, low, query, keys, values, start[None], log_total, grad, out)


def turned_sums_body(raw, inverse, gain, cosine, sine, d_query, d_key, sums, gains):
    width = d_query.shape[1]
    size = cosine.shape[1]

    @pl.when(pl.program_id(0) == 0)
    def _():
        gains[...] = jnp.zeros_like(gains)

    for which, grad in ((0, d_query), (1, d_key)):
        row = jnp.zeros((raw.shape[0], size), f32)
        scale = upright(inverse[which : which + 1, :], size)
        for at in range(0, width, size):
            unit = raw[:, which * width + at : which * width + at + size] * scale
            product = turn_back(grad[:, at : at + size], cosine[...], sine[...]) * unit
            gains[which : which + 1, at : at + size] += jnp.sum(product, axis=0, keepdims=True)
            row += product * gain[which : which + 1, at : at + size]
        sums[which : which + 1, :] = row_sums(row)


def turned_sums(raw, inverse, gain, cosine, sine, d_query, d_key):
    rows, width = d_query.shape
    size = cosine.shape[1]
    step = min(256, rows)
    by_row = lambda columns: pl.BlockSpec((step, columns), lambda i: (i, 0))
    return pl.pallas_call(
        turned_sums_body,
        grid=(rows // step,),
        in_specs=[
            by_row(3 * width),
            pl.BlockSpec((2, step), lambda i: (0, i)),
            pl.BlockSpec((2, width), lambda i: (0, 0)),
            by_row(size),
            by_row(size),
            by_row(width),
            by_row(width),
        ],
        out_specs=[
            pl.BlockSpec((2, step), lambda i: (0, i)),
            pl.BlockSpec((2, width), lambda i: (0, 0)),
        ],
        out_shape=[
            jax.ShapeDtypeStruct((2, rows), f32),
            jax.ShapeDtypeStruct((2, width), f32),
        ],
        compiler_params=params(1),
        cost_estimate=lasting(4),
    )(raw, inverse, gain, cosine, sine, d_query, d_key)


def raw_grads_body(
    spot, raw, inverse, gain, cosine, sine, d_query, d_key, d_val, means, out, moved
):
    width = d_query.shape[1]
    size = cosine.shape[1]
    for which, grad in ((0, d_query), (1, d_key)):
        scale = upright(inverse[which : which + 1, :], size)
        mean = upright(means[which : which + 1, :], size)
        for at in range(0, width, size):
            place = slice(which * width + at, which * width + at + size)
            unit = raw[:, place] * scale
            scaled = (
                turn_back(grad[:, at : at + size], cosine[...], sine[...])
                * gain[which : which + 1, at : at + size]
            )
            out[:, place] = (scale * (scaled - unit * mean)).astype(b16)
    out[:, 2 * width :] = d_val[...].astype(b16)
    moved[...] = out[...]


def raw_grads(raw, inverse, gain, cosine, sine, d_query, d_key, d_val, means, spot, block):
    rows, width = d_query.shape
    size = cosine.shape[1]
    by_row = lambda columns: pl.BlockSpec((block, columns), lambda i, spot: (i, 0))
    in_line = pl.BlockSpec((2, block), lambda i, spot: (0, i))
    return pl.pallas_call(
        raw_grads_body,
        grid_spec=pltpu.PrefetchScalarGridSpec(
            num_scalar_prefetch=1,
            grid=(rows // block,),
            in_specs=[
                by_row(3 * width),
                in_line,
                pl.BlockSpec((2, width), lambda i, spot: (0, 0)),
                by_row(size),
                by_row(size),
                by_row(width),
                by_row(width),
                by_row(width),
                in_line,
            ],
            out_specs=[
                by_row(3 * width),
                pl.BlockSpec((block, 3 * width), lambda i, spot: (spot[i], 0)),
            ],
        ),
        out_shape=[jax.ShapeDtypeStruct((rows, 3 * width), b16)] * 2,
        compiler_params=params(1),
        cost_estimate=lasting(5),
    )(spot, raw, inverse, gain, cosine, sine, d_query, d_key, d_val, means)


def ffn_forward_body(count, *refs):
    blocks, (w_gate, w_up, full, gate, up, act) = refs[:count], refs[count:]

    @pl.when(pl.program_id(0) == 0)
    def _():
        if count == 5:
            half = blocks[3].shape[0]
            parts = [block.at[:half] for block in blocks[:3]] + [blocks[3]]
            parts += [block.at[half:] for block in blocks[:3]] + [blocks[4]]
        else:
            parts = blocks
        at = 0
        for block in parts:
            full[at : at + block.shape[0], :] = block[...]
            at += block.shape[0]

    gate_pre = dot(full[...], w_gate[...], 1, 0)
    up_pre = dot(full[...], w_up[...], 1, 0)
    gate[...] = gate_pre.astype(b16)
    up[...] = up_pre.astype(b16)
    act[...] = (gate_pre * jax.nn.sigmoid(gate_pre) * up_pre).astype(b16)


def ffn_forward(blocks, w_both):
    rows = sum(block.shape[0] for block in blocks)
    width, columns = w_both.shape
    step = min(256, columns // 2)
    count = columns // 2 // step
    out = pl.BlockSpec((rows, step), lambda j: (0, j))
    hidden = jax.ShapeDtypeStruct((rows, columns // 2), b16)
    return pl.pallas_call(
        functools.partial(ffn_forward_body, len(blocks)),
        grid=(count,),
        in_specs=[pl.BlockSpec(block.shape, lambda j: (0, 0)) for block in blocks]
        + [
            pl.BlockSpec((width, step), lambda j: (0, j)),
            pl.BlockSpec((width, step), lambda j: (0, j + count)),
        ],
        out_specs=[pl.BlockSpec((rows, width), lambda j: (0, 0)), out, out, out],
        out_shape=[jax.ShapeDtypeStruct((rows, width), b16), hidden, hidden, hidden],
        compiler_params=params(1),
        cost_estimate=lasting(10),
    )(*blocks, w_both, w_both)


def branch_back_body(
    both, from_x, from_y, cot, unit, inverse, gain, grad_res, d_branch, grad_gain
):
    @pl.when(pl.program_id(0) == 0)
    def _():
        grad_gain[...] = jnp.zeros_like(grad_gain)

    total = both[...].astype(f32) + from_x[...].astype(f32) + from_y[...].astype(f32)
    total += cot[...].astype(f32)
    grad_res[...] = total
    grad_gain[...] += jnp.sum(total * unit[...], axis=0, keepdims=True)
    scaled = total * gain[...]
    mean = jnp.mean(scaled * unit[...], axis=1, keepdims=True)
    d_branch[...] = (inverse[...] * (scaled - unit[...] * mean)).astype(b16)


def branch_back(both, from_x, from_y, cot, unit, inverse, gain):
    rows, width = unit.shape
    half = rows // 2
    by_row = pl.BlockSpec((half, width), lambda i: (i, 0))
    line = pl.BlockSpec((1, width), lambda i: (0, 0))
    return pl.pallas_call(
        branch_back_body,
        grid=(2,),
        in_specs=[
            pl.BlockSpec((half, width), lambda i: (4 * i, 0)),
            by_row,
            by_row,
            by_row,
            by_row,
            pl.BlockSpec((half, 1), lambda i: (i, 0)),
            line,
        ],
        out_specs=[by_row, by_row, line],
        out_shape=[
            jax.ShapeDtypeStruct((rows, width), f32),
            jax.ShapeDtypeStruct((rows, width), b16),
            jax.ShapeDtypeStruct((1, width), f32),
        ],
        compiler_params=params(1, 60),
        cost_estimate=lasting(4),
    )(both, from_x, from_y, cot, unit, inverse, gain)


def joined_dot_body(*refs):
    blocks, (weight, full, out) = refs[:-3], refs[-3:]
    at = 0
    for block in blocks:
        rows = pl.ds(at, block.shape[0])
        full[rows, :] = block[...]
        out[rows, :] = dot(block[...], weight[...], 1, 0).astype(b16)
        at += block.shape[0]


def joined_dot(blocks, weight):
    rows = sum(block.shape[0] for block in blocks)
    width, columns = weight.shape
    whole = lambda shape: pl.BlockSpec(shape, lambda i: (0, 0))
    return pl.pallas_call(
        joined_dot_body,
        grid=(1,),
        in_specs=[whole(block.shape) for block in blocks] + [whole(weight.shape)],
        out_specs=[whole((rows, width)), whole((rows, columns))],
        out_shape=[
            jax.ShapeDtypeStruct((rows, width), b16),
            jax.ShapeDtypeStruct((rows, columns), b16),
        ],
        compiler_params=params(1),
        cost_estimate=lasting(4),
    )(*blocks, weight)


def ffn_backward_body(grad, w_down, gate, up, d_gate, d_up):
    d_act = dot(grad[...], w_down[...], 1, 0)
    gate_pre, up_pre = gate[...].astype(f32), up[...].astype(f32)
    sigmoid = jax.nn.sigmoid(gate_pre)
    d_gate[...] = (d_act * up_pre * sigmoid * (1.0 + gate_pre * (1.0 - sigmoid))).astype(b16)
    d_up[...] = (d_act * gate_pre * sigmoid).astype(b16)


def ffn_backward(grad, w_down, gate, up):
    rows, width = grad.shape
    columns = w_down.shape[1]
    step = min(256, columns)
    out = pl.BlockSpec((rows, step), lambda j: (0, j))
    return pl.pallas_call(
        ffn_backward_body,
        grid=(columns // step,),
        in_specs=[
            pl.BlockSpec((rows, width), lambda j: (0, 0)),
            pl.BlockSpec((width, step), lambda j: (0, j)),
            out,
            out,
        ],
        out_specs=[out, out],
        out_shape=[jax.ShapeDtypeStruct((rows, columns), b16)] * 2,
        compiler_params=params(1),
        cost_estimate=lasting(6),
    )(grad, w_down, gate, up)


def ffn_residual_body(d_gate, d_up, w_gate, w_up, *rest):
    value = dot(d_gate[...], w_gate[...], 1, 1) + dot(d_up[...], w_up[...], 1, 1)
    if len(rest) == 2:
        value += rest[0][...].astype(f32)
    rest[-1][...] = value.astype(b16)


def ffn_residual(d_gate, d_up, w_both, *received):
    rows, columns = d_gate.shape
    width = w_both.shape[0]
    step = min(256, width)
    full = pl.BlockSpec((rows, columns), lambda j: (0, 0))
    out = pl.BlockSpec((rows, step), lambda j: (0, j))
    return pl.pallas_call(
        ffn_residual_body,
        grid=(width // step,),
        in_specs=[
            full,
            full,
            pl.BlockSpec((step, columns), lambda j: (j, 0)),
            pl.BlockSpec((step, columns), lambda j: (j, 1)),
        ]
        + [out] * len(received),
        out_specs=out,
        out_shape=jax.ShapeDtypeStruct((rows, width), b16),
        compiler_params=params(1),
        cost_estimate=lasting(9),
    )(d_gate, d_up, w_both, w_both, *received)


def columns_body(side, query, key, val, out_weight, out):
    width = query.shape[1]
    for at, piece in enumerate((query, key, val)):
        out[:, at * width : (at + 1) * width] = piece[...].astype(b16)
    out[:, 3 * width :] = jnp.transpose(out_weight[...]).astype(b16)


def attention_columns(side, query, key, val, out_weight):
    piece, width = query.shape[0], query.shape[1] // 2
    upper = pl.BlockSpec((piece, width), lambda i, side: (0, side[0]))
    return pl.pallas_call(
        columns_body,
        grid_spec=pltpu.PrefetchScalarGridSpec(
            num_scalar_prefetch=1,
            grid=(1,),
            in_specs=[
                upper,
                upper,
                upper,
                pl.BlockSpec((width, piece), lambda i, side: (side[0], 0)),
            ],
            out_specs=pl.BlockSpec((piece, 4 * width), lambda i, side: (0, 0)),
        ),
        out_shape=jax.ShapeDtypeStruct((piece, 4 * width), b16),
        compiler_params=params(1, 60),
        cost_estimate=lasting(2),
    )(side, query, key, val, out_weight)


def flip_body(value, out):
    out[...] = jnp.transpose(value[...])


def flip(value):
    rows, columns = value.shape
    step = min(256, columns)
    return pl.pallas_call(
        flip_body,
        grid=(columns // step,),
        in_specs=[pl.BlockSpec((rows, step), lambda i: (0, i))],
        out_specs=pl.BlockSpec((step, rows), lambda i: (i, 0)),
        out_shape=jax.ShapeDtypeStruct((columns, rows), value.dtype),
        compiler_params=params(1),
    )(value)


def adam_step(weight, first_moment, second_moment, gradient):
    new_first = beta_one * first_moment + (1.0 - beta_one) * gradient
    new_second = beta_two * second_moment + (1.0 - beta_two) * gradient * gradient
    first_hat = new_first / (1.0 - beta_one**step_count)
    second_hat = new_second / (1.0 - beta_two**step_count)
    updated = weight - learn_rate * (
        first_hat / (jnp.sqrt(second_hat) + adam_eps) + decay_rate * weight
    )
    return (updated, new_first, new_second)


def assemble_body(count, flags, *refs):
    out = refs[-1]
    spot = pl.program_id(0)
    theirs = ((spot // count) != flags[0]).astype(i32)
    place = theirs * count + ((spot % count) ^ flags[1])
    for at, block in enumerate(refs[:-1]):

        @pl.when(place == at)
        def _(block=block):
            out[0] = block[...].astype(f32)


def assemble(mine, theirs):
    count = len(mine)
    block, width = mine[0].shape
    shift = lax.axis_index(TX) if count == 2 else jnp.zeros((), i32)
    return pl.pallas_call(
        functools.partial(assemble_body, count),
        grid_spec=pltpu.PrefetchScalarGridSpec(
            num_scalar_prefetch=1,
            grid=(2 * count,),
            in_specs=[pl.BlockSpec((block, width), lambda i, flags: (0, 0))] * (2 * count),
            out_specs=pl.BlockSpec((1, block, width), lambda i, flags: (0, i, 0)),
        ),
        out_shape=jax.ShapeDtypeStruct((1, 2 * count * block, width), f32),
        compiler_params=params(1),
        cost_estimate=lasting(5),
    )(jnp.stack([lax.axis_index(TC), shift]), *mine, *theirs)


def over_chips(value):
    count = lax.axis_size(TX)
    if count == 2:
        return [value, swap(value, TX)]
    return jnp.split(lax.all_gather(value, TX, axis=0, tiled=True), count)


def over_core(blocks):
    return [swap(block, TC) for block in blocks]


def adam_body(turned, flag, weight, first, second, own, other, grad, updated, mean, square):
    value = jnp.where(pl.program_id(0) == flag[0], own[...].astype(f32), other[...].astype(f32))
    if turned:
        value = jnp.transpose(value)
    grad[...] = value
    updated[...], mean[...], square[...] = adam_step(
        weight[...], first[...], second[...], value
    )


def adam(weight, first, second, own, other, flag, turned=False, column=0):
    rows, columns = weight.shape
    if turned:
        half = rows // 2
        step = min(256, half)
        count = half // step
        mine = pl.BlockSpec((step, columns), lambda j, i, flag: (j * count + i, 0))
        halves = pl.BlockSpec((columns, step), lambda j, i, flag: (0, column * count + i))
        both = pl.BlockSpec(
            (None, columns, step), lambda j, i, flag: (flag[0], 0, column * count + i)
        )
    else:
        half = columns // 2
        step = min(128, rows)
        count = rows // step
        mine = pl.BlockSpec((step, half), lambda j, i, flag: (i, j))
        halves = pl.BlockSpec((step, half), lambda j, i, flag: (i, column))
        both = pl.BlockSpec((None, step, half), lambda j, i, flag: (flag[0], i, column))
    return pl.pallas_call(
        functools.partial(adam_body, turned),
        grid_spec=pltpu.PrefetchScalarGridSpec(
            num_scalar_prefetch=1,
            grid=(2, count),
            in_specs=[mine] * 3 + [both, halves],
            out_specs=[mine] * 4,
        ),
        out_shape=[jax.ShapeDtypeStruct(weight.shape, f32)] * 4,
        compiler_params=params(2),
        cost_estimate=lasting(weight.size * 8e-6),
    )(flag, weight, first, second, own, other)


def attention_adam_body(flag, *refs):
    states, (own, other), outs = refs[:12], refs[12:14], refs[14:]
    mine = pl.program_id(0) == flag[0]
    width = states[0].shape[1]
    for which in range(4):
        columns = slice(which * width, (which + 1) * width)
        value = jnp.where(mine, own[:, columns].astype(f32), other[:, columns].astype(f32))
        if which == 3:
            value = jnp.transpose(value)
        outs[4 * which][...] = value
        stepped = adam_step(*[ref[...] for ref in states[3 * which : 3 * which + 3]], value)
        for at in range(3):
            outs[4 * which + 1 + at][...] = stepped[at]


def attention_adam(states, own, other, flag):
    piece, width = states[0][0].shape[0], states[0][0].shape[1] // 2
    across_columns = pl.BlockSpec((piece, width), lambda j, flag: (0, j))
    across_rows = pl.BlockSpec((width, piece), lambda j, flag: (j, 0))
    specs = [across_columns] * 3 + [across_rows]
    shapes = [jax.ShapeDtypeStruct(state[0].shape, f32) for state in states]
    out = pl.pallas_call(
        attention_adam_body,
        grid_spec=pltpu.PrefetchScalarGridSpec(
            num_scalar_prefetch=1,
            grid=(2,),
            in_specs=[spec for spec in specs for _ in range(3)]
            + [
                pl.BlockSpec((None, piece, 4 * width), lambda j, flag: (flag[0], 0, 0)),
                pl.BlockSpec((piece, 4 * width), lambda j, flag: (0, 0)),
            ],
            out_specs=[spec for spec in specs for _ in range(4)],
        ),
        out_shape=[shape for shape in shapes for _ in range(4)],
        compiler_params=params(1, 40),
        cost_estimate=lasting(6),
    )(flag, *[array for state in states for array in state], own, other)
    return [out[at : at + 4] for at in range(0, 16, 4)]


def row_mean(a, b):
    return jnp.mean(a * b, axis=1, keepdims=True)


def shards(tokens, cotangent, segment_ids, *state):
    masters, first_moments, second_moments = state[:11], state[11:22], state[22:33]
    inputs = tokens[0]
    docs_here = segment_ids[0]
    rows, width = inputs.shape
    ring = lax.axis_size(SHARD)
    teams = lax.axis_size(TENSOR)
    y = lax.axis_index(CX)
    piece = masters[0].shape[0]
    heads_here = masters[7].shape[0]
    head_piece = masters[7].shape[1]
    size = head_piece * ring * 2
    wide = heads_here * size // 2
    hidden = masters[4].shape[1] // 2
    block = rows // teams
    length = 2 * rows
    my_block = lax.axis_index(TC) * lax.axis_size(TX) + lax.axis_index(TX)

    def my_rows(value):
        return lax.dynamic_slice_in_dim(value, my_block * block, block, 0)

    docs_all = gather_axis(docs_here, CX)
    gains = jnp.concatenate([gain.astype(b16).reshape(-1) for gain in masters[7:]])[None]
    gains = gather_axis(gather_axis(gather_axis(gains, CX), SL), SH).astype(f32)
    first = list(masters[:7])

    def columns_of(weight, index, count):
        return lax.dynamic_slice_in_dim(weight, index * count, count, 1).astype(b16)

    def over_ctx(weights, count):
        mine, theirs = [
            jnp.concatenate([columns_of(w, index, count) for w in weights], axis=1)
            for index in (y, 1 - y)
        ]
        return mine, swap(theirs, CX)

    def over_shard(value):
        return lax.all_gather(value, SHARD, axis=0, tiled=True)

    attn_own = over_shard(attention_columns(y[None], *first[:4]))
    theirs = swap(attention_columns(1 - y[None], *first[:4]), CX)
    theirs, local_rows, gains, docs_all = tie(theirs, my_rows(inputs), gains, docs_all)
    theirs, attn_own = tie(theirs, attn_own)
    attn_other = over_shard(theirs)

    remote, gate_w, up_w, down_w = tie(swap(local_rows, CX), *first[4:])
    remote = gather_axis(remote, TX)
    gate_w = pair(*over_ctx([gate_w], hidden), CX)
    remote, gate_w = tie(remote, gate_w)
    remote = gather_axis(remote, TC)
    up_w = pair(*over_ctx([up_w], hidden), CX)
    attn_other, remote, w_both = tie(
        attn_other, remote, jnp.concatenate([gate_w, up_w], axis=1)
    )
    w_both = over_shard(w_both)
    w_attn = pair(
        *[value.reshape(ring, 1, piece, 4 * wide) for value in (attn_own, attn_other)], CX, 1
    ).reshape(width, 4 * wide)
    w_qkv, w_out = w_attn[:, : 3 * wide], w_attn[:, 3 * wide :]
    down_w = pair(*over_ctx([flip(down_w.astype(b16))], hidden), CX)

    count = heads_here * head_piece
    head_gain = jnp.stack(
        [
            part(
                jnp.transpose(
                    gains[:, which * count : (which + 1) * count].reshape(
                        ring * 2, heads_here, head_piece
                    ),
                    (1, 0, 2),
                ).reshape(2, wide),
                y,
                0,
            )
            for which in range(2)
        ]
    )
    attn_gain = gains[:, 2 * count : 2 * count + piece].reshape(1, width)
    ffn_gain = gains[:, 2 * count + piece :].reshape(1, width)

    doc_range = jnp.arange(DOCS, dtype=i32)
    counts = jnp.sum((docs_all[:, None] == doc_range[None, :]).astype(i32), axis=0)
    starts = jnp.cumsum(counts) - counts
    own_start = jnp.sum(
        jnp.where(docs_all[:, None] == doc_range[None, :], starts[None, :], 0), axis=1
    )
    positions = jnp.arange(length, dtype=i32) - own_start
    frequencies = rope_base ** (-(jnp.arange(size // 2, dtype=f32) * 2.0) / size)
    angles = positions.astype(f32)[:, None] * frequencies[None, :]
    cosine, sine = jnp.cos(angles), jnp.sin(angles)
    cosine = jnp.concatenate([cosine, cosine], axis=1)
    sine = jnp.concatenate([-sine, sine], axis=1)

    raw, squares = project(y[None], inputs, remote, w_attn)
    inverse = lax.rsqrt(plane_sum(squares) / width + norm_eps)
    query, key, val = prepare(raw, inverse, head_gain, cosine, sine)
    query, down_w = tie(query, down_w)
    spot = block_places(CX)
    attended, log_total = flash_forward(query, key, val, own_start, spot, block, size)
    group = length // 2
    branch = collect(
        across(dot(attended[:group], w_out, 1, 1), dot(attended[group:], w_out, 1, 1)), CX
    )
    branch_inv = lax.rsqrt(row_mean(branch, branch) + norm_eps)
    branch_unit = branch * branch_inv
    residual = my_rows(inputs).astype(f32) + branch_unit * attn_gain
    res, w_both, down_w = tie(residual.astype(b16), w_both, down_w)
    w_down = over_shard(down_w)
    res = spread(res, CX)

    res, gate_pre, up_pre, activated = zip(*[ffn_forward(blocks, w_both) for blocks in res])
    *activated, w_down = tie(*activated, w_down)
    parts = 2 if lax.axis_size(TX) == 2 else 1
    grad_out = my_rows(cotangent[0]).astype(f32)
    d_ffn, block_rows, grad_ffn_gain = [], [], 0.0
    for mine, theirs, rows_in, cot in zip(
        *[jnp.split(value, parts) for value in (*activated, residual, grad_out)]
    ):
        ffn_out = collect(across(dot(mine, w_down, 1, 1), dot(theirs, w_down, 1, 1)), CX)
        ffn_inv = lax.rsqrt(row_mean(ffn_out, ffn_out) + norm_eps)
        ffn_unit = ffn_out * ffn_inv
        scaled_out = cot * ffn_gain
        d_ffn.append(
            (ffn_inv * (scaled_out - ffn_unit * row_mean(scaled_out, ffn_unit))).astype(b16)
        )
        grad_ffn_gain = grad_ffn_gain + jnp.sum(cot * ffn_unit, axis=0)
        block_rows.append((rows_in + ffn_unit * ffn_gain).astype(b16))
    d_ffn = joined_halves(spread(jnp.concatenate(d_ffn, 0), CX))
    block_rows = jnp.concatenate(block_rows, 0)

    def both(left, right):
        return (dot(left[0], right[0], 0, 0) + dot(left[1], right[1], 0, 0)).astype(b16)

    def to_shard(partial):
        return lax.psum_scatter(partial, SHARD, scatter_dimension=0, tiled=True)

    def to_owner(summed):
        summed = summed.reshape(2, piece, -1)
        return summed, swap(part(summed, 1 - y, 0), CX)

    *d_ffn, block_rows = tie(*d_ffn, block_rows)
    block_rows = over_chips(block_rows)
    grad_down = both(d_ffn, activated)
    grad_down, *d_ffn = tie(grad_down, *d_ffn)
    grad_down = to_shard(grad_down)
    d_gate, d_up = zip(
        *[ffn_backward(d, w_down, g, u) for d, g, u in zip(d_ffn, gate_pre, up_pre)]
    )
    *block_rows, d_gate0, d_gate1, d_up0, d_up1 = tie(*block_rows, *d_gate, *d_up)
    d_gate, d_up = [d_gate0, d_gate1], [d_up0, d_up1]
    theirs, *turned = tie(ffn_residual(d_gate[1], d_up[1], w_both), *d_gate)
    d_gate = turned
    grad_gate = dot(res[0], d_gate[0], 0, 0).astype(b16)
    theirs, grad_gate = tie(swap(theirs, TC), grad_gate)
    both_ffn = ffn_residual(d_gate[0], d_up[0], w_both, theirs)
    both_ffn, *turned = tie(both_ffn, *d_gate, *d_up)
    d_gate, d_up = turned[:2], turned[2:]
    grad_gate = (grad_gate.astype(f32) + dot(res[1], d_gate[1], 0, 0)).astype(b16)
    grad_gate = to_shard(grad_gate)
    if parts == 2:
        *collected, d_up0, d_up1 = collect_halves(both_ffn, CX, *d_up)
        d_up = [d_up0, d_up1]
        grad_res, d_branch, grad_attn_gain = branch_back(
            *collected, my_rows(cotangent[0]), branch_unit, branch_inv, attn_gain
        )
        grad_attn_gain = grad_attn_gain[0]
    else:
        grad_res = grad_out + collect(both_ffn, CX)
        scaled_res = grad_res * attn_gain
        d_branch = (
            branch_inv * (scaled_res - branch_unit * row_mean(scaled_res, branch_unit))
        ).astype(b16)
        grad_attn_gain = jnp.sum(grad_res * branch_unit, axis=0)
    block_theirs = over_core(block_rows)
    grad_upward = both(res, d_up)
    d_branch, grad_upward, grad_down = tie(d_branch, grad_upward, grad_down)
    down_halves = to_owner(grad_down)
    grad_upward = to_shard(grad_upward)
    triple = lambda i: (masters[i], first_moments[i], second_moments[i])

    d_branch, d_att = zip(*[joined_dot(blocks, w_out) for blocks in spread(d_branch, CX)])
    *d_branch, grad_gate = tie(*d_branch, grad_gate)
    gate_halves = to_owner(grad_gate)
    d_att = jnp.concatenate(d_att, 0)
    d_query, d_key, d_val = flash_backward(
        query, key, val, own_start, log_total, d_att, attended, spot, block, size
    )
    d_query, *turned = tie(d_query, *d_branch, *down_halves, *gate_halves)
    d_branch, down_halves, gate_halves = turned[:2], turned[2:4], turned[4:]
    grad_out_w = both(d_branch, [attended[:group], attended[group:]])
    d_query, grad_out_w = tie(d_query, grad_out_w)
    sums, grad_heads = turned_sums(raw, inverse, head_gain, cosine, sine, d_query, d_key)
    plane_sums = plane_sum(
        jnp.concatenate([sums, grad_attn_gain[None], grad_ffn_gain[None]])
    )
    means = plane_sums[:2] / width
    small = jnp.concatenate([plane_sums[2:].reshape(1, -1), grad_heads.reshape(1, -1)], 1)
    small = sum_axis(sum_axis(small, SL), SH)
    d_qkv, moved = raw_grads(
        raw, inverse, head_gain, cosine, sine, d_query, d_key, d_val, means, spot, block
    )

    sides = d_qkv.reshape(2, rows, 3 * wide)
    grad_qkv = both((inputs, remote), (part(sides, y, 0), part(sides, 1 - y, 0)))
    grad_attn, grad_upward = tie(
        jnp.concatenate([grad_qkv, grad_out_w], axis=1), grad_upward
    )
    grad_attn = to_shard(grad_attn)
    both_attn = across(dot(moved[:group], w_qkv, 1, 1), dot(moved[group:], w_qkv, 1, 1))
    back_attn = collect(both_attn, CX)
    down_step = adam(*triple(6), *down_halves, y[None], turned=True)
    gate_step = adam(*triple(4), *gate_halves, y[None])
    block_share = assemble(block_rows, block_theirs)
    back_attn, small, block_share, grad_upward, *turned = tie(
        back_attn, small, block_share, grad_upward, *down_step, *gate_step
    )
    down_step, gate_step = turned[:4], turned[4:]
    up_step = adam(*triple(5), *to_owner(grad_upward), y[None])
    input_rows = over_chips((grad_res + back_attn).astype(b16))
    index = lax.axis_index(SHARD) * 2 + y
    wide_sums = lax.dynamic_slice_in_dim(
        small[0, : 2 * width].reshape(2, width), index * piece, piece, 1
    )
    head_sums = small[0, 2 * width :].reshape(2, 1, heads_here // 2, size)
    head_sums = pair(head_sums, swap(head_sums, CX), CX, 1).reshape(2, heads_here, size)
    head_sums = lax.dynamic_slice_in_dim(head_sums, index * head_piece, head_piece, 2)

    gain_steps = []
    for i, grad in enumerate((head_sums[0], head_sums[1], wide_sums[0], wide_sums[1])):
        gain_steps += (grad,) + adam_step(*triple(7 + i), grad)
    _, *turned = tie(grad_attn[:1, :1], *gain_steps, *up_step, *input_rows)
    gain_steps, up_step, input_rows = turned[:16], turned[16:20], turned[20:]
    attn_halves = to_owner(grad_attn)
    input_share = assemble(input_rows, over_core(input_rows))
    stepped = attention_adam([triple(i) for i in range(4)], *attn_halves, y[None])
    stepped += [gate_step, up_step, down_step]
    stepped += [gain_steps[at : at + 4] for at in range(0, 16, 4)]
    return tuple(
        [block_share, input_share]
        + [result[which] for which in range(4) for result in stepped]
    )


def solution(mesh):
    ring, ctx, teams = (mesh.shape[name] for name in mesh.axis_names)
    fine = Mesh(
        mesh.devices.reshape(ring // 2, 2, ctx, teams // 2, 2), (SH, SL, CX, TX, TC)
    )
    owners = (SH, SL, CX)
    column = P(owners, TENSOR)
    row = P(TENSOR, owners)
    vector = P(owners)
    act = P(SHARD, CX, None)
    weights = (column, column, column, row, column, column, row, row, row, vector, vector)
    return jax.shard_map(
        shards,
        mesh=fine,
        in_specs=(act, act, P(SHARD, CX)) + weights * 3,
        out_specs=(act, act) + weights * 4,
        check_vma=False,
    )
```

```python
import functools
import math

import jax
import jax.numpy as jnp
from jax import lax
from jax.experimental import pallas as pl
from jax.experimental.pallas import tpu as pltpu
from jax.sharding import Mesh
from jax.sharding import PartitionSpec as P

DOCS = 3
rope_base = 500000.0
norm_eps = 1e-06
learn_rate = 0.3
beta_one = 0.9
beta_two = 0.95
adam_eps = 1e-08
decay_rate = 0.1
step_count = 2
masked_score = -1e30

f32 = jnp.float32
b16 = jnp.bfloat16
i32 = jnp.int32

SH, SL, CX, TX, TC = "sh", "sl", "ctx", "tx", "tc"
SHARD = (SH, SL)
TENSOR = (TX, TC)
PLANE = (CX, TX, TC)


def dot(a, b, ca, cb):
    return lax.dot_general(a, b, (((ca,), (cb,)), ((), ())), preferred_element_type=f32)


def swap(value, axis):
    return lax.ppermute(value, axis, [(0, 1), (1, 0)])


def pair(mine, other, axis, at=0):
    return jnp.where(
        lax.axis_index(axis) == 0,
        jnp.concatenate([mine, other], at),
        jnp.concatenate([other, mine], at),
    )


def gather_axis(value, axis):
    if lax.axis_size(axis) == 2:
        return pair(value, swap(value, axis), axis)
    return lax.all_gather(value, axis, axis=0, tiled=True)


def sum_axis(value, axis):
    if lax.axis_size(axis) == 2:
        return value + swap(value, axis)
    return lax.psum(value, axis)


def plane_sum(value):
    return sum_axis(sum_axis(sum_axis(value, TC), TX), CX)


def tie(*values):
    return lax.optimization_barrier(values)


def part(value, index, at):
    return lax.dynamic_index_in_dim(value, index, at, keepdims=False)


def rows_all(value):
    return gather_axis(gather_axis(value, TX), TC)


def spread(value, axis):
    if lax.axis_size(TX) == 2:
        half = value.shape[0] // 2
        over_x = swap(value, TX)
        over_y = swap(value, axis)
        over_x, over_y = tie(over_x, over_y)
        near, far = tie(swap(over_y[:half], TX), swap(over_x[half:], axis))
        mine = [value, over_x, over_y, near, far]
    else:
        line = lax.all_gather(value, TX, axis=0, tiled=True)
        mine = [line, swap(line, axis)]
    return mine, [swap(block, TC) for block in mine]


def joined(groups):
    return [jnp.concatenate(blocks, 0) for blocks in groups]


def joined_halves(groups):
    if len(groups[0]) != 5:
        return joined(groups)
    out = []
    for first, second, third, near, far in groups:
        half = near.shape[0]
        upper = [block[:half] for block in (first, second, third)] + [near]
        lower = [block[half:] for block in (first, second, third)] + [far]
        out.append(jnp.concatenate(upper + lower, 0))
    return out


def across(mine, theirs):
    return (mine + swap(theirs.astype(b16), TC).astype(f32)).astype(b16)


def collect(both, axis):
    count = lax.axis_size(TX)
    block = both.shape[0] // (2 * count)
    if count == 2:
        half = block // 2
        near = swap(both[3 * block : 3 * block + half], TX)
        far = swap(both[3 * block + half :], axis)
        over_x = jnp.concatenate(
            [both[block : block + half], both[block + half : 2 * block] + far], 0
        )
        over_y = jnp.concatenate(
            [both[2 * block : 2 * block + half] + near, both[2 * block + half : 3 * block]], 0
        )
        return (
            both[:block].astype(f32)
            + swap(over_x, TX).astype(f32)
            + swap(over_y, axis).astype(f32)
        )
    line = both[: count * block] + swap(both[count * block :], axis)
    return lax.psum_scatter(line, TX, scatter_dimension=0, tiled=True).astype(f32)


def collect_halves(both, axis, *later):
    h = both.shape[0] // 8
    near, far, *later = tie(swap(both[3 * h : 4 * h], TX), swap(both[7 * h :], axis), *later)
    over_x = jnp.concatenate([both[h : 2 * h], both[5 * h : 6 * h] + far], 0)
    over_y = jnp.concatenate([both[2 * h : 3 * h] + near, both[6 * h : 7 * h]], 0)
    return (both, swap(over_x, TX), swap(over_y, axis), *later)


def block_places(axis):
    count = lax.axis_size(TX)
    spot = jnp.arange(4 * count, dtype=i32)
    side = (spot // (2 * count)) ^ lax.axis_index(axis)
    core = (spot // count % 2) ^ lax.axis_index(TC)
    along = spot % count
    if count == 2:
        along = along ^ lax.axis_index(TX)
    return (core * 2 + side) * count + along


def params(steps, mebibytes=30):
    return pltpu.CompilerParams(
        dimension_semantics=("arbitrary",) * steps, vmem_limit_bytes=mebibytes * 1024 * 1024
    )


def lasting(us):
    return pl.CostEstimate(flops=0, transcendentals=0, bytes_accessed=int(us * 0.5e6))


def upright(row, columns):
    return jnp.transpose(jnp.broadcast_to(row, (columns, row.shape[1])))


def row_sums(value):
    return jnp.sum(jnp.transpose(value), axis=0, keepdims=True)


def project_body(side, local, remote, weight, raw, squares):
    half = pl.num_programs(0) // 2
    mine = (pl.program_id(0) // half) == side[0]
    raw[...] = dot(jnp.where(mine, local[...], remote[...]), weight[...], 1, 0)
    width = raw.shape[1] // 3
    for which in range(2):
        total = jnp.zeros((raw.shape[0], 128), f32)
        for at in range(which * width, (which + 1) * width, 128):
            total += raw[:, at : at + 128] * raw[:, at : at + 128]
        squares[which : which + 1, :] = row_sums(total)


def project(side, local, remote, weight):
    rows, width = local.shape
    columns = weight.shape[1] // 4 * 3
    step = min(256, rows)
    half = rows // step
    tokens = pl.BlockSpec((step, width), lambda i, side: (i % half, 0))
    return pl.pallas_call(
        project_body,
        grid_spec=pltpu.PrefetchScalarGridSpec(
            num_scalar_prefetch=1,
            grid=(2 * half,),
            in_specs=[
                tokens,
                tokens,
                pl.BlockSpec((width, columns), lambda i, side: (0, 0)),
            ],
            out_specs=[
                pl.BlockSpec((step, columns), lambda i, side: (i, 0)),
                pl.BlockSpec((2, step), lambda i, side: (0, i)),
            ],
        ),
        out_shape=[
            jax.ShapeDtypeStruct((2 * rows, columns), f32),
            jax.ShapeDtypeStruct((2, 2 * rows), f32),
        ],
        compiler_params=params(1),
        cost_estimate=lasting(12),
    )(side, local, remote, weight)


def turn(value, cosine, sine):
    return value * cosine + pltpu.roll(value, value.shape[1] // 2, 1) * sine


def turn_back(value, cosine, sine):
    return value * cosine + pltpu.roll(value * sine, value.shape[1] // 2, 1)


def prepare_body(raw, inverse, gain, cosine, sine, query, key, val):
    width = query.shape[1]
    size = cosine.shape[1]
    for which, out in ((0, query), (1, key)):
        scale = upright(inverse[which : which + 1, :], size)
        for at in range(0, width, size):
            unit = raw[:, which * width + at : which * width + at + size] * scale
            out[:, at : at + size] = turn(
                unit * gain[which : which + 1, at : at + size], cosine[...], sine[...]
            ).astype(b16)
    val[...] = raw[:, 2 * width :].astype(b16)


def prepare(raw, inverse, gain, cosine, sine):
    rows, width = raw.shape[0], raw.shape[1] // 3
    size = cosine.shape[1]
    step = min(256, rows)
    by_row = lambda columns: pl.BlockSpec((step, columns), lambda i: (i, 0))
    return pl.pallas_call(
        prepare_body,
        grid=(rows // step,),
        in_specs=[
            by_row(3 * width),
            pl.BlockSpec((2, step), lambda i: (0, i)),
            pl.BlockSpec((2, width), lambda i: (0, 0)),
            by_row(size),
            by_row(size),
        ],
        out_specs=[by_row(width)] * 3,
        out_shape=[jax.ShapeDtypeStruct((rows, width), b16)] * 3,
        compiler_params=params(1),
        cost_estimate=lasting(3),
    )(raw, inverse, gain, cosine, sine)


def allowed(start, first_key, first_query, shape):
    keys = first_key + lax.broadcasted_iota(i32, shape, 0)
    queries = first_query + lax.broadcasted_iota(i32, shape, 1)
    return (keys >= start) & (keys <= queries)


def forward_body(span, size, spot, low, query, keys, values, start, out, log_total):
    i = pl.program_id(0)
    rows = query.shape[0]
    scale = 1.0 / math.sqrt(size)
    heads = [slice(at, at + size) for at in range(0, query.shape[1], size)]

    def step(j, carry):
        at = pl.multiple_of(j * span, span)
        here = pl.ds(at, span)
        mask = allowed(start[...], at, i * rows, (span, rows))
        after = []
        for head, (peak, total, summed) in zip(heads, carry):
            scores = dot(keys[here, head], query[:, head], 1, 1) * scale
            scores = jnp.where(mask, scores, masked_score)
            new_peak = jnp.maximum(peak, jnp.max(scores, axis=0, keepdims=True))
            shrink = jnp.exp(peak - new_peak)
            exponent = jnp.exp(scores - new_peak)
            total = total * shrink + jnp.sum(exponent, axis=0, keepdims=True)
            summed = summed * shrink + dot(values[here, head], exponent.astype(b16), 0, 0)
            after.append((new_peak, total, summed))
        return tuple(after)

    begin = (
        jnp.full((1, rows), masked_score, f32),
        jnp.zeros((1, rows), f32),
        jnp.zeros((size, rows), f32),
    )
    last = ((i + 1) * rows + span - 1) // span
    carry = lax.fori_loop(low[i], last, step, (begin,) * len(heads))
    for at, (head, (peak, total, summed)) in enumerate(zip(heads, carry)):
        out[:, head] = jnp.transpose(summed / total).astype(b16)
        log_total[at : at + 1, :] = peak + jnp.log(total)


def flash_forward(query, keys, values, start, spot, block, size):
    rows, width = query.shape
    heads = width // size
    blocks = rows // block
    span = min(512, rows)
    low = start.reshape(blocks, block)[:, 0] // span
    full = pl.BlockSpec((rows, width), lambda i, spot, low: (0, 0))
    return pl.pallas_call(
        functools.partial(forward_body, span, size),
        grid_spec=pltpu.PrefetchScalarGridSpec(
            num_scalar_prefetch=2,
            grid=(blocks,),
            in_specs=[
                pl.BlockSpec((block, width), lambda i, spot, low: (i, 0)),
                full,
                full,
                pl.BlockSpec((1, block), lambda i, spot, low: (0, i)),
            ],
            out_specs=[
                pl.BlockSpec((block, width), lambda i, spot, low: (spot[i], 0)),
                pl.BlockSpec((heads, block), lambda i, spot, low: (0, i)),
            ],
        ),
        out_shape=[
            jax.ShapeDtypeStruct((rows, width), b16),
            jax.ShapeDtypeStruct((heads, rows), f32),
        ],
        compiler_params=params(1),
        cost_estimate=lasting(18),
    )(spot, low, query, keys, values, start[None])


def backward_body(
    span,
    size,
    spot,
    low,
    query,
    keys,
    values,
    start,
    log_total,
    grad,
    out,
    d_query,
    d_keys,
    d_values,
):
    i = pl.program_id(0)
    rows = query.shape[0]
    scale = 1.0 / math.sqrt(size)
    heads = [slice(at, at + size) for at in range(0, query.shape[1], size)]

    @pl.when(i == 0)
    def _():
        d_keys[...] = jnp.zeros_like(d_keys)
        d_values[...] = jnp.zeros_like(d_values)

    deltas = [row_sums(grad[:, head].astype(f32) * out[:, head].astype(f32)) for head in heads]

    def step(j, carry):
        at = pl.multiple_of(j * span, span)
        here = pl.ds(at, span)
        mask = allowed(start[...], at, i * rows, (span, rows))
        after = []
        for which, (head, summed) in enumerate(zip(heads, carry)):
            scores = dot(keys[here, head], query[:, head], 1, 1) * scale
            soft = jnp.where(mask, jnp.exp(scores - log_total[which : which + 1, :]), 0.0)
            d_soft = dot(values[here, head], grad[:, head], 1, 1)
            d_scores = (soft * (d_soft - deltas[which]) * scale).astype(b16)
            d_values[here, head] += dot(soft.astype(b16), grad[:, head], 1, 0)
            d_keys[here, head] += dot(d_scores, query[:, head], 1, 0)
            after.append(summed + dot(keys[here, head], d_scores, 0, 0))
        return tuple(after)

    last = ((i + 1) * rows + span - 1) // span
    carry = lax.fori_loop(
        low[i], last, step, (jnp.zeros((size, rows), f32),) * len(heads)
    )
    for head, summed in zip(heads, carry):
        d_query[:, head] = jnp.transpose(summed)


def flash_backward(query, keys, values, start, log_total, grad, out, spot, block, size):
    rows, width = query.shape
    heads = width // size
    blocks = rows // block
    span = min(512, rows)
    low = start.reshape(blocks, block)[:, 0] // span
    natural = pl.BlockSpec((block, width), lambda i, spot, low: (i, 0))
    moved = pl.BlockSpec((block, width), lambda i, spot, low: (spot[i], 0))
    full = pl.BlockSpec((rows, width), lambda i, spot, low: (0, 0))
    return pl.pallas_call(
        functools.partial(backward_body, span, size),
        grid_spec=pltpu.PrefetchScalarGridSpec(
            num_scalar_prefetch=2,
            grid=(blocks,),
            in_specs=[
                natural,
                full,
                full,
                pl.BlockSpec((1, block), lambda i, spot, low: (0, i)),
                pl.BlockSpec((heads, block), lambda i, spot, low: (0, i)),
                moved,
                moved,
            ],
            out_specs=[natural, full, full],
        ),
        out_shape=[jax.ShapeDtypeStruct((rows, width), f32)] * 3,
        compiler_params=params(1),
        cost_estimate=lasting(22),
    )(spot, low, query, keys, values, start[None], log_total, grad, out)


def turned_sums_body(raw, inverse, gain, cosine, sine, d_query, d_key, sums, gains):
    width = d_query.shape[1]
    size = cosine.shape[1]

    @pl.when(pl.program_id(0) == 0)
    def _():
        gains[...] = jnp.zeros_like(gains)

    for which, grad in ((0, d_query), (1, d_key)):
        row = jnp.zeros((raw.shape[0], size), f32)
        scale = upright(inverse[which : which + 1, :], size)
        for at in range(0, width, size):
            unit = raw[:, which * width + at : which * width + at + size] * scale
            product = turn_back(grad[:, at : at + size], cosine[...], sine[...]) * unit
            gains[which : which + 1, at : at + size] += jnp.sum(product, axis=0, keepdims=True)
            row += product * gain[which : which + 1, at : at + size]
        sums[which : which + 1, :] = row_sums(row)


def turned_sums(raw, inverse, gain, cosine, sine, d_query, d_key):
    rows, width = d_query.shape
    size = cosine.shape[1]
    step = min(256, rows)
    by_row = lambda columns: pl.BlockSpec((step, columns), lambda i: (i, 0))
    return pl.pallas_call(
        turned_sums_body,
        grid=(rows // step,),
        in_specs=[
            by_row(3 * width),
            pl.BlockSpec((2, step), lambda i: (0, i)),
            pl.BlockSpec((2, width), lambda i: (0, 0)),
            by_row(size),
            by_row(size),
            by_row(width),
            by_row(width),
        ],
        out_specs=[
            pl.BlockSpec((2, step), lambda i: (0, i)),
            pl.BlockSpec((2, width), lambda i: (0, 0)),
        ],
        out_shape=[
            jax.ShapeDtypeStruct((2, rows), f32),
            jax.ShapeDtypeStruct((2, width), f32),
        ],
        compiler_params=params(1),
        cost_estimate=lasting(4),
    )(raw, inverse, gain, cosine, sine, d_query, d_key)


def raw_grads_body(
    spot, raw, inverse, gain, cosine, sine, d_query, d_key, d_val, means, out, moved
):
    width = d_query.shape[1]
    size = cosine.shape[1]
    for which, grad in ((0, d_query), (1, d_key)):
        scale = upright(inverse[which : which + 1, :], size)
        mean = upright(means[which : which + 1, :], size)
        for at in range(0, width, size):
            place = slice(which * width + at, which * width + at + size)
            unit = raw[:, place] * scale
            scaled = (
                turn_back(grad[:, at : at + size], cosine[...], sine[...])
                * gain[which : which + 1, at : at + size]
            )
            out[:, place] = (scale * (scaled - unit * mean)).astype(b16)
    out[:, 2 * width :] = d_val[...].astype(b16)
    moved[...] = out[...]


def raw_grads(raw, inverse, gain, cosine, sine, d_query, d_key, d_val, means, spot, block):
    rows, width = d_query.shape
    size = cosine.shape[1]
    by_row = lambda columns: pl.BlockSpec((block, columns), lambda i, spot: (i, 0))
    in_line = pl.BlockSpec((2, block), lambda i, spot: (0, i))
    return pl.pallas_call(
        raw_grads_body,
        grid_spec=pltpu.PrefetchScalarGridSpec(
            num_scalar_prefetch=1,
            grid=(rows // block,),
            in_specs=[
                by_row(3 * width),
                in_line,
                pl.BlockSpec((2, width), lambda i, spot: (0, 0)),
                by_row(size),
                by_row(size),
                by_row(width),
                by_row(width),
                by_row(width),
                in_line,
            ],
            out_specs=[
                by_row(3 * width),
                pl.BlockSpec((block, 3 * width), lambda i, spot: (spot[i], 0)),
            ],
        ),
        out_shape=[jax.ShapeDtypeStruct((rows, 3 * width), b16)] * 2,
        compiler_params=params(1),
        cost_estimate=lasting(5),
    )(spot, raw, inverse, gain, cosine, sine, d_query, d_key, d_val, means)


def ffn_forward_body(count, *refs):
    blocks, (w_gate, w_up, full, gate, up, act) = refs[:count], refs[count:]

    @pl.when(pl.program_id(0) == 0)
    def _():
        if count == 5:
            half = blocks[3].shape[0]
            parts = [block.at[:half] for block in blocks[:3]] + [blocks[3]]
            parts += [block.at[half:] for block in blocks[:3]] + [blocks[4]]
        else:
            parts = blocks
        at = 0
        for block in parts:
            full[at : at + block.shape[0], :] = block[...]
            at += block.shape[0]

    gate_pre = dot(full[...], w_gate[...], 1, 0)
    up_pre = dot(full[...], w_up[...], 1, 0)
    gate[...] = gate_pre.astype(b16)
    up[...] = up_pre.astype(b16)
    act[...] = (gate_pre * jax.nn.sigmoid(gate_pre) * up_pre).astype(b16)


def ffn_forward(blocks, w_both):
    rows = sum(block.shape[0] for block in blocks)
    width, columns = w_both.shape
    step = min(256, columns // 2)
    count = columns // 2 // step
    out = pl.BlockSpec((rows, step), lambda j: (0, j))
    hidden = jax.ShapeDtypeStruct((rows, columns // 2), b16)
    return pl.pallas_call(
        functools.partial(ffn_forward_body, len(blocks)),
        grid=(count,),
        in_specs=[pl.BlockSpec(block.shape, lambda j: (0, 0)) for block in blocks]
        + [
            pl.BlockSpec((width, step), lambda j: (0, j)),
            pl.BlockSpec((width, step), lambda j: (0, j + count)),
        ],
        out_specs=[pl.BlockSpec((rows, width), lambda j: (0, 0)), out, out, out],
        out_shape=[jax.ShapeDtypeStruct((rows, width), b16), hidden, hidden, hidden],
        compiler_params=params(1),
        cost_estimate=lasting(10),
    )(*blocks, w_both, w_both)


def branch_back_body(
    both, from_x, from_y, cot, unit, inverse, gain, grad_res, d_branch, grad_gain
):
    @pl.when(pl.program_id(0) == 0)
    def _():
        grad_gain[...] = jnp.zeros_like(grad_gain)

    total = both[...].astype(f32) + from_x[...].astype(f32) + from_y[...].astype(f32)
    total += cot[...].astype(f32)
    grad_res[...] = total
    grad_gain[...] += jnp.sum(total * unit[...], axis=0, keepdims=True)
    scaled = total * gain[...]
    mean = jnp.mean(scaled * unit[...], axis=1, keepdims=True)
    d_branch[...] = (inverse[...] * (scaled - unit[...] * mean)).astype(b16)


def branch_back(both, from_x, from_y, cot, unit, inverse, gain):
    rows, width = unit.shape
    half = rows // 2
    by_row = pl.BlockSpec((half, width), lambda i: (i, 0))
    line = pl.BlockSpec((1, width), lambda i: (0, 0))
    return pl.pallas_call(
        branch_back_body,
        grid=(2,),
        in_specs=[
            pl.BlockSpec((half, width), lambda i: (4 * i, 0)),
            by_row,
            by_row,
            by_row,
            by_row,
            pl.BlockSpec((half, 1), lambda i: (i, 0)),
            line,
        ],
        out_specs=[by_row, by_row, line],
        out_shape=[
            jax.ShapeDtypeStruct((rows, width), f32),
            jax.ShapeDtypeStruct((rows, width), b16),
            jax.ShapeDtypeStruct((1, width), f32),
        ],
        compiler_params=params(1, 60),
        cost_estimate=lasting(4),
    )(both, from_x, from_y, cot, unit, inverse, gain)


def joined_dot_body(*refs):
    blocks, (weight, full, out) = refs[:-3], refs[-3:]
    at = 0
    for block in blocks:
        rows = pl.ds(at, block.shape[0])
        full[rows, :] = block[...]
        out[rows, :] = dot(block[...], weight[...], 1, 0).astype(b16)
        at += block.shape[0]


def joined_dot(blocks, weight):
    rows = sum(block.shape[0] for block in blocks)
    width, columns = weight.shape
    whole = lambda shape: pl.BlockSpec(shape, lambda i: (0, 0))
    return pl.pallas_call(
        joined_dot_body,
        grid=(1,),
        in_specs=[whole(block.shape) for block in blocks] + [whole(weight.shape)],
        out_specs=[whole((rows, width)), whole((rows, columns))],
        out_shape=[
            jax.ShapeDtypeStruct((rows, width), b16),
            jax.ShapeDtypeStruct((rows, columns), b16),
        ],
        compiler_params=params(1),
        cost_estimate=lasting(4),
    )(*blocks, weight)


def ffn_backward_body(grad, w_down, gate, up, d_gate, d_up):
    d_act = dot(grad[...], w_down[...], 1, 0)
    gate_pre, up_pre = gate[...].astype(f32), up[...].astype(f32)
    sigmoid = jax.nn.sigmoid(gate_pre)
    d_gate[...] = (d_act * up_pre * sigmoid * (1.0 + gate_pre * (1.0 - sigmoid))).astype(b16)
    d_up[...] = (d_act * gate_pre * sigmoid).astype(b16)


def ffn_backward(grad, w_down, gate, up):
    rows, width = grad.shape
    columns = w_down.shape[1]
    step = min(256, columns)
    out = pl.BlockSpec((rows, step), lambda j: (0, j))
    return pl.pallas_call(
        ffn_backward_body,
        grid=(columns // step,),
        in_specs=[
            pl.BlockSpec((rows, width), lambda j: (0, 0)),
            pl.BlockSpec((width, step), lambda j: (0, j)),
            out,
            out,
        ],
        out_specs=[out, out],
        out_shape=[jax.ShapeDtypeStruct((rows, columns), b16)] * 2,
        compiler_params=params(1),
        cost_estimate=lasting(6),
    )(grad, w_down, gate, up)


def ffn_residual_body(d_gate, d_up, w_gate, w_up, *rest):
    value = dot(d_gate[...], w_gate[...], 1, 1) + dot(d_up[...], w_up[...], 1, 1)
    if len(rest) == 2:
        value += rest[0][...].astype(f32)
    rest[-1][...] = value.astype(b16)


def ffn_residual(d_gate, d_up, w_both, *received):
    rows, columns = d_gate.shape
    width = w_both.shape[0]
    step = min(256, width)
    full = pl.BlockSpec((rows, columns), lambda j: (0, 0))
    out = pl.BlockSpec((rows, step), lambda j: (0, j))
    return pl.pallas_call(
        ffn_residual_body,
        grid=(width // step,),
        in_specs=[
            full,
            full,
            pl.BlockSpec((step, columns), lambda j: (j, 0)),
            pl.BlockSpec((step, columns), lambda j: (j, 1)),
        ]
        + [out] * len(received),
        out_specs=out,
        out_shape=jax.ShapeDtypeStruct((rows, width), b16),
        compiler_params=params(1),
        cost_estimate=lasting(9),
    )(d_gate, d_up, w_both, w_both, *received)


def columns_body(side, query, key, val, out_weight, out):
    width = query.shape[1]
    for at, piece in enumerate((query, key, val)):
        out[:, at * width : (at + 1) * width] = piece[...].astype(b16)
    out[:, 3 * width :] = jnp.transpose(out_weight[...]).astype(b16)


def attention_columns(side, query, key, val, out_weight):
    piece, width = query.shape[0], query.shape[1] // 2
    upper = pl.BlockSpec((piece, width), lambda i, side: (0, side[0]))
    return pl.pallas_call(
        columns_body,
        grid_spec=pltpu.PrefetchScalarGridSpec(
            num_scalar_prefetch=1,
            grid=(1,),
            in_specs=[
                upper,
                upper,
                upper,
                pl.BlockSpec((width, piece), lambda i, side: (side[0], 0)),
            ],
            out_specs=pl.BlockSpec((piece, 4 * width), lambda i, side: (0, 0)),
        ),
        out_shape=jax.ShapeDtypeStruct((piece, 4 * width), b16),
        compiler_params=params(1, 60),
        cost_estimate=lasting(2),
    )(side, query, key, val, out_weight)


def flip_body(value, out):
    out[...] = jnp.transpose(value[...])


def flip(value):
    rows, columns = value.shape
    step = min(256, columns)
    return pl.pallas_call(
        flip_body,
        grid=(columns // step,),
        in_specs=[pl.BlockSpec((rows, step), lambda i: (0, i))],
        out_specs=pl.BlockSpec((step, rows), lambda i: (i, 0)),
        out_shape=jax.ShapeDtypeStruct((columns, rows), value.dtype),
        compiler_params=params(1),
    )(value)


def adam_step(weight, first_moment, second_moment, gradient):
    new_first = beta_one * first_moment + (1.0 - beta_one) * gradient
    new_second = beta_two * second_moment + (1.0 - beta_two) * gradient * gradient
    first_hat = new_first / (1.0 - beta_one**step_count)
    second_hat = new_second / (1.0 - beta_two**step_count)
    updated = weight - learn_rate * (
        first_hat / (jnp.sqrt(second_hat) + adam_eps) + decay_rate * weight
    )
    return (updated, new_first, new_second)


def assemble_body(count, flags, *refs):
    out = refs[-1]
    spot = pl.program_id(0)
    theirs = ((spot // count) != flags[0]).astype(i32)
    place = theirs * count + ((spot % count) ^ flags[1])
    for at, block in enumerate(refs[:-1]):

        @pl.when(place == at)
        def _(block=block):
            out[0] = block[...].astype(f32)


def assemble(mine, theirs):
    count = len(mine)
    block, width = mine[0].shape
    shift = lax.axis_index(TX) if count == 2 else jnp.zeros((), i32)
    return pl.pallas_call(
        functools.partial(assemble_body, count),
        grid_spec=pltpu.PrefetchScalarGridSpec(
            num_scalar_prefetch=1,
            grid=(2 * count,),
            in_specs=[pl.BlockSpec((block, width), lambda i, flags: (0, 0))] * (2 * count),
            out_specs=pl.BlockSpec((1, block, width), lambda i, flags: (0, i, 0)),
        ),
        out_shape=jax.ShapeDtypeStruct((1, 2 * count * block, width), f32),
        compiler_params=params(1),
        cost_estimate=lasting(5),
    )(jnp.stack([lax.axis_index(TC), shift]), *mine, *theirs)


def over_chips(value):
    count = lax.axis_size(TX)
    if count == 2:
        return [value, swap(value, TX)]
    return jnp.split(lax.all_gather(value, TX, axis=0, tiled=True), count)


def over_core(blocks):
    return [swap(block, TC) for block in blocks]


def adam_body(turned, flag, weight, first, second, own, other, grad, updated, mean, square):
    value = jnp.where(pl.program_id(0) == flag[0], own[...].astype(f32), other[...].astype(f32))
    if turned:
        value = jnp.transpose(value)
    grad[...] = value
    updated[...], mean[...], square[...] = adam_step(
        weight[...], first[...], second[...], value
    )


def adam(weight, first, second, own, other, flag, turned=False, column=0):
    rows, columns = weight.shape
    if turned:
        half = rows // 2
        step = min(256, half)
        count = half // step
        mine = pl.BlockSpec((step, columns), lambda j, i, flag: (j * count + i, 0))
        halves = pl.BlockSpec((columns, step), lambda j, i, flag: (0, column * count + i))
        both = pl.BlockSpec(
            (None, columns, step), lambda j, i, flag: (flag[0], 0, column * count + i)
        )
    else:
        half = columns // 2
        step = min(128, rows)
        count = rows // step
        mine = pl.BlockSpec((step, half), lambda j, i, flag: (i, j))
        halves = pl.BlockSpec((step, half), lambda j, i, flag: (i, column))
        both = pl.BlockSpec((None, step, half), lambda j, i, flag: (flag[0], i, column))
    return pl.pallas_call(
        functools.partial(adam_body, turned),
        grid_spec=pltpu.PrefetchScalarGridSpec(
            num_scalar_prefetch=1,
            grid=(2, count),
            in_specs=[mine] * 3 + [both, halves],
            out_specs=[mine] * 4,
        ),
        out_shape=[jax.ShapeDtypeStruct(weight.shape, f32)] * 4,
        compiler_params=params(2),
        cost_estimate=lasting(weight.size * 8e-6),
    )(flag, weight, first, second, own, other)


def attention_adam_body(flag, *refs):
    states, (own, other), outs = refs[:12], refs[12:14], refs[14:]
    mine = pl.program_id(0) == flag[0]
    width = states[0].shape[1]
    for which in range(4):
        columns = slice(which * width, (which + 1) * width)
        value = jnp.where(mine, own[:, columns].astype(f32), other[:, columns].astype(f32))
        if which == 3:
            value = jnp.transpose(value)
        outs[4 * which][...] = value
        stepped = adam_step(*[ref[...] for ref in states[3 * which : 3 * which + 3]], value)
        for at in range(3):
            outs[4 * which + 1 + at][...] = stepped[at]


def attention_adam(states, own, other, flag):
    piece, width = states[0][0].shape[0], states[0][0].shape[1] // 2
    across_columns = pl.BlockSpec((piece, width), lambda j, flag: (0, j))
    across_rows = pl.BlockSpec((width, piece), lambda j, flag: (j, 0))
    specs = [across_columns] * 3 + [across_rows]
    shapes = [jax.ShapeDtypeStruct(state[0].shape, f32) for state in states]
    out = pl.pallas_call(
        attention_adam_body,
        grid_spec=pltpu.PrefetchScalarGridSpec(
            num_scalar_prefetch=1,
            grid=(2,),
            in_specs=[spec for spec in specs for _ in range(3)]
            + [
                pl.BlockSpec((None, piece, 4 * width), lambda j, flag: (flag[0], 0, 0)),
                pl.BlockSpec((piece, 4 * width), lambda j, flag: (0, 0)),
            ],
            out_specs=[spec for spec in specs for _ in range(4)],
        ),
        out_shape=[shape for shape in shapes for _ in range(4)],
        compiler_params=params(1, 40),
        cost_estimate=lasting(6),
    )(flag, *[array for state in states for array in state], own, other)
    return [out[at : at + 4] for at in range(0, 16, 4)]


def row_mean(a, b):
    return jnp.mean(a * b, axis=1, keepdims=True)


def shards(tokens, cotangent, segment_ids, *state):
    masters, first_moments, second_moments = state[:11], state[11:22], state[22:33]
    inputs = tokens[0]
    docs_here = segment_ids[0]
    rows, width = inputs.shape
    ring = lax.axis_size(SHARD)
    teams = lax.axis_size(TENSOR)
    y = lax.axis_index(CX)
    piece = masters[0].shape[0]
    heads_here = masters[7].shape[0]
    head_piece = masters[7].shape[1]
    size = head_piece * ring * 2
    wide = heads_here * size // 2
    hidden = masters[4].shape[1] // 2
    block = rows // teams
    length = 2 * rows
    my_block = lax.axis_index(TC) * lax.axis_size(TX) + lax.axis_index(TX)

    def my_rows(value):
        return lax.dynamic_slice_in_dim(value, my_block * block, block, 0)

    docs_all = gather_axis(docs_here, CX)
    gains = jnp.concatenate([gain.astype(b16).reshape(-1) for gain in masters[7:]])[None]
    gains = gather_axis(gather_axis(gather_axis(gains, CX), SL), SH).astype(f32)
    first = list(masters[:7])

    def columns_of(weight, index, count):
        return lax.dynamic_slice_in_dim(weight, index * count, count, 1).astype(b16)

    def over_ctx(weights, count):
        mine, theirs = [
            jnp.concatenate([columns_of(w, index, count) for w in weights], axis=1)
            for index in (y, 1 - y)
        ]
        return mine, swap(theirs, CX)

    def over_shard(value):
        return lax.all_gather(value, SHARD, axis=0, tiled=True)

    attn_own = over_shard(attention_columns(y[None], *first[:4]))
    theirs = swap(attention_columns(1 - y[None], *first[:4]), CX)
    theirs, local_rows, gains, docs_all = tie(theirs, my_rows(inputs), gains, docs_all)
    theirs, attn_own = tie(theirs, attn_own)
    attn_other = over_shard(theirs)

    remote, gate_w, up_w, down_w = tie(swap(local_rows, CX), *first[4:])
    remote = gather_axis(remote, TX)
    gate_w = pair(*over_ctx([gate_w], hidden), CX)
    remote, gate_w = tie(remote, gate_w)
    remote = gather_axis(remote, TC)
    up_w = pair(*over_ctx([up_w], hidden), CX)
    attn_other, remote, w_both = tie(
        attn_other, remote, jnp.concatenate([gate_w, up_w], axis=1)
    )
    w_both = over_shard(w_both)
    w_attn = pair(
        *[value.reshape(ring, 1, piece, 4 * wide) for value in (attn_own, attn_other)], CX, 1
    ).reshape(width, 4 * wide)
    w_qkv, w_out = w_attn[:, : 3 * wide], w_attn[:, 3 * wide :]
    down_w = pair(*over_ctx([flip(down_w.astype(b16))], hidden), CX)

    count = heads_here * head_piece
    head_gain = jnp.stack(
        [
            part(
                jnp.transpose(
                    gains[:, which * count : (which + 1) * count].reshape(
                        ring * 2, heads_here, head_piece
                    ),
                    (1, 0, 2),
                ).reshape(2, wide),
                y,
                0,
            )
            for which in range(2)
        ]
    )
    attn_gain = gains[:, 2 * count : 2 * count + piece].reshape(1, width)
    ffn_gain = gains[:, 2 * count + piece :].reshape(1, width)

    doc_range = jnp.arange(DOCS, dtype=i32)
    counts = jnp.sum((docs_all[:, None] == doc_range[None, :]).astype(i32), axis=0)
    starts = jnp.cumsum(counts) - counts
    own_start = jnp.sum(
        jnp.where(docs_all[:, None] == doc_range[None, :], starts[None, :], 0), axis=1
    )
    positions = jnp.arange(length, dtype=i32) - own_start
    frequencies = rope_base ** (-(jnp.arange(size // 2, dtype=f32) * 2.0) / size)
    angles = positions.astype(f32)[:, None] * frequencies[None, :]
    cosine, sine = jnp.cos(angles), jnp.sin(angles)
    cosine = jnp.concatenate([cosine, cosine], axis=1)
    sine = jnp.concatenate([-sine, sine], axis=1)

    raw, squares = project(y[None], inputs, remote, w_attn)
    inverse = lax.rsqrt(plane_sum(squares) / width + norm_eps)
    query, key, val = prepare(raw, inverse, head_gain, cosine, sine)
    query, down_w = tie(query, down_w)
    spot = block_places(CX)
    attended, log_total = flash_forward(query, key, val, own_start, spot, block, size)
    group = length // 2
    branch = collect(
        across(dot(attended[:group], w_out, 1, 1), dot(attended[group:], w_out, 1, 1)), CX
    )
    branch_inv = lax.rsqrt(row_mean(branch, branch) + norm_eps)
    branch_unit = branch * branch_inv
    residual = my_rows(inputs).astype(f32) + branch_unit * attn_gain
    res, w_both, down_w = tie(residual.astype(b16), w_both, down_w)
    w_down = over_shard(down_w)
    res = spread(res, CX)

    res, gate_pre, up_pre, activated = zip(*[ffn_forward(blocks, w_both) for blocks in res])
    *activated, w_down = tie(*activated, w_down)
    parts = 2 if lax.axis_size(TX) == 2 else 1
    grad_out = my_rows(cotangent[0]).astype(f32)
    d_ffn, block_rows, grad_ffn_gain = [], [], 0.0
    for mine, theirs, rows_in, cot in zip(
        *[jnp.split(value, parts) for value in (*activated, residual, grad_out)]
    ):
        ffn_out = collect(across(dot(mine, w_down, 1, 1), dot(theirs, w_down, 1, 1)), CX)
        ffn_inv = lax.rsqrt(row_mean(ffn_out, ffn_out) + norm_eps)
        ffn_unit = ffn_out * ffn_inv
        scaled_out = cot * ffn_gain
        d_ffn.append(
            (ffn_inv * (scaled_out - ffn_unit * row_mean(scaled_out, ffn_unit))).astype(b16)
        )
        grad_ffn_gain = grad_ffn_gain + jnp.sum(cot * ffn_unit, axis=0)
        block_rows.append((rows_in + ffn_unit * ffn_gain).astype(b16))
    d_ffn = joined_halves(spread(jnp.concatenate(d_ffn, 0), CX))
    block_rows = jnp.concatenate(block_rows, 0)

    def both(left, right):
        return (dot(left[0], right[0], 0, 0) + dot(left[1], right[1], 0, 0)).astype(b16)

    def to_shard(partial):
        return lax.psum_scatter(partial, SHARD, scatter_dimension=0, tiled=True)

    def to_owner(summed):
        summed = summed.reshape(2, piece, -1)
        return summed, swap(part(summed, 1 - y, 0), CX)

    *d_ffn, block_rows = tie(*d_ffn, block_rows)
    block_rows = over_chips(block_rows)
    grad_down = both(d_ffn, activated)
    grad_down, *d_ffn = tie(grad_down, *d_ffn)
    grad_down = to_shard(grad_down)
    d_gate, d_up = zip(
        *[ffn_backward(d, w_down, g, u) for d, g, u in zip(d_ffn, gate_pre, up_pre)]
    )
    *block_rows, d_gate0, d_gate1, d_up0, d_up1 = tie(*block_rows, *d_gate, *d_up)
    d_gate, d_up = [d_gate0, d_gate1], [d_up0, d_up1]
    theirs, *turned = tie(ffn_residual(d_gate[1], d_up[1], w_both), *d_gate)
    d_gate = turned
    grad_gate = dot(res[0], d_gate[0], 0, 0).astype(b16)
    theirs, grad_gate = tie(swap(theirs, TC), grad_gate)
    both_ffn = ffn_residual(d_gate[0], d_up[0], w_both, theirs)
    both_ffn, *turned = tie(both_ffn, *d_gate, *d_up)
    d_gate, d_up = turned[:2], turned[2:]
    grad_gate = (grad_gate.astype(f32) + dot(res[1], d_gate[1], 0, 0)).astype(b16)
    grad_gate = to_shard(grad_gate)
    if parts == 2:
        *collected, d_up0, d_up1 = collect_halves(both_ffn, CX, *d_up)
        d_up = [d_up0, d_up1]
        grad_res, d_branch, grad_attn_gain = branch_back(
            *collected, my_rows(cotangent[0]), branch_unit, branch_inv, attn_gain
        )
        grad_attn_gain = grad_attn_gain[0]
    else:
        grad_res = grad_out + collect(both_ffn, CX)
        scaled_res = grad_res * attn_gain
        d_branch = (
            branch_inv * (scaled_res - branch_unit * row_mean(scaled_res, branch_unit))
        ).astype(b16)
        grad_attn_gain = jnp.sum(grad_res * branch_unit, axis=0)
    block_theirs = over_core(block_rows)
    grad_upward = both(res, d_up)
    d_branch, grad_upward, grad_down = tie(d_branch, grad_upward, grad_down)
    down_halves = to_owner(grad_down)
    grad_upward = to_shard(grad_upward)
    triple = lambda i: (masters[i], first_moments[i], second_moments[i])

    d_branch, d_att = zip(*[joined_dot(blocks, w_out) for blocks in spread(d_branch, CX)])
    *d_branch, grad_gate = tie(*d_branch, grad_gate)
    gate_halves = to_owner(grad_gate)
    d_att = jnp.concatenate(d_att, 0)
    d_query, d_key, d_val = flash_backward(
        query, key, val, own_start, log_total, d_att, attended, spot, block, size
    )
    d_query, *turned = tie(d_query, *d_branch, *down_halves, *gate_halves)
    d_branch, down_halves, gate_halves = turned[:2], turned[2:4], turned[4:]
    grad_out_w = both(d_branch, [attended[:group], attended[group:]])
    d_query, grad_out_w = tie(d_query, grad_out_w)
    sums, grad_heads = turned_sums(raw, inverse, head_gain, cosine, sine, d_query, d_key)
    plane_sums = plane_sum(
        jnp.concatenate([sums, grad_attn_gain[None], grad_ffn_gain[None]])
    )
    means = plane_sums[:2] / width
    small = jnp.concatenate([plane_sums[2:].reshape(1, -1), grad_heads.reshape(1, -1)], 1)
    small = sum_axis(sum_axis(small, SL), SH)
    d_qkv, moved = raw_grads(
        raw, inverse, head_gain, cosine, sine, d_query, d_key, d_val, means, spot, block
    )

    sides = d_qkv.reshape(2, rows, 3 * wide)
    grad_qkv = both((inputs, remote), (part(sides, y, 0), part(sides, 1 - y, 0)))
    grad_attn, grad_upward = tie(
        jnp.concatenate([grad_qkv, grad_out_w], axis=1), grad_upward
    )
    grad_attn = to_shard(grad_attn)
    both_attn = across(dot(moved[:group], w_qkv, 1, 1), dot(moved[group:], w_qkv, 1, 1))
    back_attn = collect(both_attn, CX)
    down_step = adam(*triple(6), *down_halves, y[None], turned=True)
    block_share = assemble(block_rows, block_theirs)
    back_attn, small, block_share, grad_upward, *turned = tie(
        back_attn, small, block_share, grad_upward, *down_step, *gate_halves
    )
    down_step, gate_halves = turned[:4], turned[4:]
    gate_step = adam(*triple(4), *gate_halves, y[None])
    up_step = adam(*triple(5), *to_owner(grad_upward), y[None])
    input_rows = over_chips((grad_res + back_attn).astype(b16))
    index = lax.axis_index(SHARD) * 2 + y
    wide_sums = lax.dynamic_slice_in_dim(
        small[0, : 2 * width].reshape(2, width), index * piece, piece, 1
    )
    head_sums = small[0, 2 * width :].reshape(2, 1, heads_here // 2, size)
    head_sums = pair(head_sums, swap(head_sums, CX), CX, 1).reshape(2, heads_here, size)
    head_sums = lax.dynamic_slice_in_dim(head_sums, index * head_piece, head_piece, 2)

    gain_steps = []
    for i, grad in enumerate((head_sums[0], head_sums[1], wide_sums[0], wide_sums[1])):
        gain_steps += (grad,) + adam_step(*triple(7 + i), grad)
    _, *turned = tie(grad_attn[:1, :1], *gain_steps, *up_step, *gate_step, *input_rows)
    gain_steps, up_step, gate_step = turned[:16], turned[16:20], turned[20:24]
    input_rows = turned[24:]
    attn_halves = to_owner(grad_attn)
    input_share = assemble(input_rows, over_core(input_rows))
    stepped = attention_adam([triple(i) for i in range(4)], *attn_halves, y[None])
    stepped += [gate_step, up_step, down_step]
    stepped += [gain_steps[at : at + 4] for at in range(0, 16, 4)]
    return tuple(
        [block_share, input_share]
        + [result[which] for which in range(4) for result in stepped]
    )


def solution(mesh):
    ring, ctx, teams = (mesh.shape[name] for name in mesh.axis_names)
    fine = Mesh(
        mesh.devices.reshape(ring // 2, 2, ctx, teams // 2, 2), (SH, SL, CX, TX, TC)
    )
    owners = (SH, SL, CX)
    column = P(owners, TENSOR)
    row = P(TENSOR, owners)
    vector = P(owners)
    act = P(SHARD, CX, None)
    weights = (column, column, column, row, column, column, row, row, row, vector, vector)
    return jax.shard_map(
        shards,
        mesh=fine,
        in_specs=(act, act, P(SHARD, CX)) + weights * 3,
        out_specs=(act, act) + weights * 4,
        check_vma=False,
    )
```
